128 devices in a mesh: ctx: 16 (over x, y_lo, core), depth: 8 (over y_hi, z).
Axes of the slice: x: 4, y: 4 (y_hi: 2, y_lo: 2; y = y_hi * 2 + y_lo), z: 4, core: 2. Of those that a mesh axis runs over, the one named last changes fastest.
Arguments:
- q_heads: bfloat16 [8192, 2048], P('ctx', 'depth'), may hold values from -200 to 200
- k_heads: bfloat16 [8192, 2048], P('ctx', 'depth'), may hold values from -200 to 200
- v_heads: bfloat16 [8192, 2048], P('ctx', 'depth'), may hold values from -6 to 6
- block_of: int32 [32], replicated, may hold values from 0 to 31, each once
- resid: bfloat16 [8192, 4096], P(('ctx', 'depth')), may hold values from -6 to 6
- w_out_t: bfloat16 [2048, 4096], P('depth'), may hold values from -0.125 to 0.125
- norm_gain: float32 [4096], replicated, may hold values from 0.5 to 1.5
- w_in: bfloat16 [4096, 1024], P('depth'), may hold values from -0.09375 to 0.09375
- embed: bfloat16 [2048, 1024], replicated, may hold values from -6 to 6
- w_qkv: bfloat16 [1024, 3072], replicated, may hold values from -0.1875 to 0.1875
- w_o: bfloat16 [1024, 1024], replicated, may hold values from -0.1875 to 0.1875
- w_head: bfloat16 [1024, 2048], replicated, may hold values from -0.5 to 0.5
- codes: int32 [8192, 8], P(('ctx', 'depth')), may hold values from 0 to 2047
Outputs:
- d_attn: bfloat16 [8192, 2048], P('ctx', 'depth')
- d_wqkv: float32 [1024, 3072], P(('ctx', 'depth'))
The draws below stay inside these ranges and needn't reach their ends.
All inputs are finite; a program needn't handle non-finite values.
Results may differ from the reference program's by a relative error of at most 0.034.
Values may be sent and summed in bfloat16 or wider, within the bound.
A program may use at most 192 MiB of HBM per device.

```python
import math
import jax
import jax.numpy as jnp
from jax import lax

D = 4096
HT = 16
HS = 128
DD = 1024
DHS = 64
K = 8
V = 2048
TDEV = 512
L = 8192
HALF = 256
N_CTX = 16


def shared_keys(key):
    return jax.random.normal(key, (L, HT * HS), jnp.float32)


def draw_q_heads(key, part):
    key = jax.random.fold_in(key, 11)
    own = jax.random.normal(key, (L, HT * HS), jnp.float32)
    return own.astype(jnp.bfloat16)


def draw_k_heads(key, part):
    base = shared_keys(key)
    return base.astype(jnp.bfloat16)


def place_ends(result, key, least, top_value):
    shape = result.shape
    index_at = [jax.random.randint(jax.random.fold_in(key, axis), (), 0, shape[axis]) for axis in range(len(shape))]
    result = result.at[tuple(index_at)].set(least)
    longest = shape.index(max(shape))
    index_at[longest] = (index_at[longest] + 1) % shape[longest]
    return result.at[tuple(index_at)].set(top_value)


def block_levels(stream_key, shape, pieces, low, largest):
    def one(axis_at, blocks):
        steps = jax.random.uniform(jax.random.fold_in(jax.random.fold_in(stream_key, 6), axis_at), (blocks,), jnp.float32, low / len(pieces), largest / len(pieces))
        return jnp.repeat(jnp.exp(steps), shape[axis_at] // blocks).reshape((-1,) + (1,) * (len(shape) - axis_at - 1))

    loudness = one(*pieces[0])
    for cut in pieces[1:]:
        loudness = loudness * one(*cut)
    return loudness


def noise(stream_key, shape, scale, most, split=(), kind=jnp.bfloat16):
    factor_of = block_levels(stream_key, shape, split, -0.22, 0.18) if split else 1.0
    values = jax.random.normal(stream_key, shape, jnp.float32) * scale * factor_of
    return jnp.minimum(jnp.maximum(values, -most), most).astype(kind)


def setup_inputs(seed: int = 0) -> dict:
    arg_keys = jax.random.split(jax.random.key(seed), 14)
    return {
        "q_heads": draw_q_heads(jax.random.fold_in(arg_keys[13], 71), 0),
        "k_heads": draw_k_heads(jax.random.fold_in(arg_keys[13], 71), 0),
        "v_heads": noise(arg_keys[2], (L, HT * HS), 1.0, 6.0, ((0, 16), (1, 8))),
        "block_of": jax.random.permutation(arg_keys[3], 2 * N_CTX).astype(jnp.int32),
        "resid": noise(arg_keys[4], (L, D), 1.0, 6.0, ((0, 128),)),
        "w_out_t": noise(arg_keys[5], (HT * HS, D), (HT * HS) ** -0.5, 0.125, ((0, 8),)),
        "norm_gain": jnp.clip(1.0 + 0.1 * jax.random.normal(arg_keys[6], (D,), jnp.float32), 0.5, 1.5),
        "w_in": noise(arg_keys[7], (D, DD), D ** -0.5, 0.09375, ((0, 8),)),
        "embed": noise(arg_keys[8], (V, DD), 1.0, 6.0),
        "w_qkv": noise(arg_keys[9], (DD, 3 * DD), DD ** -0.5, 0.1875),
        "w_o": noise(arg_keys[10], (DD, DD), DD ** -0.5, 0.1875),
        "w_head": noise(arg_keys[11], (DD, V), (DD // 9) ** -0.5, 0.5),
        "codes": place_ends(jax.random.randint(arg_keys[12], (L, K), 0, V), jax.random.fold_in(arg_keys[12], 1), 0, V - 1).astype(jnp.int32),
    }


eps = 1e-05

def positions_of(index, block_of, half):
    which = index // half
    slots = jnp.arange(block_of.shape[0], dtype=jnp.int32)
    picked = lax.optimization_barrier(jnp.sum(jnp.where(which[:, None] == slots[None, :], block_of[None, :], 0), axis=1))
    return (picked * half + index % half).astype(jnp.int32)

def rms_rows(values):
    return values * lax.rsqrt(lax.optimization_barrier(jnp.mean(values * values, axis=-1, keepdims=True)) + eps)

def depth_front(units, codes, embed):
    frames, steps = codes.shape
    width = embed.shape[1]
    earlier = jnp.take(embed, codes[:, :steps - 1], axis=0).astype(jnp.float32)
    lead = jnp.zeros((frames, 1, width), jnp.float32)
    stream = units.astype(jnp.float32)[:, None, :] + jnp.concatenate([lead, earlier], axis=1)
    normed = rms_rows(stream).astype(jnp.bfloat16).reshape(frames * steps, width)
    return (normed, stream)

def depth_back(packed, stream, codes, w_o, w_head, head_size):
    frames, steps, width = stream.shape
    heads = width // head_size
    parts = packed.reshape(frames, steps, 3, heads, head_size).astype(jnp.float32)
    scores = jnp.einsum('fqhd,fkhd->fhqk', parts[:, :, 0], parts[:, :, 1]) * (1.0 / math.sqrt(head_size))
    causal = jnp.arange(steps)[:, None] >= jnp.arange(steps)[None, :]
    weights = jnp.where(causal, jnp.exp(scores), 0.0)
    weights = weights / lax.optimization_barrier(jnp.sum(weights, axis=-1, keepdims=True))
    mixed = jnp.einsum('fhqk,fkhd->fqhd', weights, parts[:, :, 2]).astype(jnp.bfloat16).reshape(frames * steps, width)
    after = stream.reshape(frames * steps, width) + jnp.dot(mixed, w_o, preferred_element_type=jnp.float32)
    normed = rms_rows(after).astype(jnp.bfloat16)
    logits = jnp.dot(normed, w_head, preferred_element_type=jnp.float32)
    total = jnp.log(lax.optimization_barrier(jnp.sum(jnp.exp(logits), axis=-1)))
    vocab = jnp.arange(w_head.shape[1], dtype=jnp.int32)
    picked = lax.optimization_barrier(jnp.sum(jnp.where(codes.reshape(-1)[:, None] == vocab[None, :], logits, 0.0), axis=-1))
    return jnp.sum(total - picked)

def depth_block(units, codes, embed, w_qkv, w_o, w_head, head_size):
    (normed, stream), pull_front = jax.vjp(lambda u: depth_front(u, codes, embed), units)
    packed = jnp.dot(normed, w_qkv, preferred_element_type=jnp.float32).astype(jnp.bfloat16)
    loss, pull = jax.vjp(lambda a, b: depth_back(a, b, codes, w_o, w_head, head_size), packed, stream)
    d_packed, d_stream = pull(jnp.ones_like(loss))
    d_normed = jnp.einsum('tc,wc->tw', d_packed, w_qkv, preferred_element_type=jnp.float32).astype(jnp.bfloat16)
    d_units, = pull_front((d_normed, d_stream))
    d_weight = jnp.einsum('tw,tc->wc', normed, d_packed, preferred_element_type=jnp.float32)
    return (d_units, d_weight)

def reference(q_heads, k_heads, v_heads, block_of, resid, w_out_t, norm_gain, w_in, embed, w_qkv, w_o, w_head, codes):
    positions = positions_of(jnp.arange(L, dtype=jnp.int32), block_of, HALF)
    keys = k_heads.astype(jnp.float32).reshape(L, HT, HS)
    values = v_heads.astype(jnp.float32).reshape(L, HT, HS)
    scale = 1.0 / math.sqrt(HS)

    def attend(start):
        rows = lax.dynamic_slice_in_dim(q_heads, start, TDEV, 0).astype(jnp.float32).reshape(TDEV, HT, HS)
        pos_q = lax.dynamic_slice_in_dim(positions, start, TDEV, 0)
        visible = pos_q[:, None] >= positions[None, :]
        scores = jnp.einsum('qhd,khd->qhk', rows, keys) * scale
        scores = jnp.where(visible[:, None, :], scores, -jnp.inf)
        top = lax.optimization_barrier(jnp.max(scores, axis=-1, keepdims=True))
        weights = jnp.where(visible[:, None, :], jnp.exp(scores - top), 0.0)
        total = lax.optimization_barrier(jnp.sum(weights, axis=-1))
        rounded = lax.optimization_barrier(weights.astype(jnp.bfloat16)).astype(jnp.float32)
        mixed = jnp.einsum('qhk,khd->qhd', rounded, values)
        return (mixed / total[:, :, None]).astype(jnp.bfloat16).reshape(TDEV, HT * HS)
    starts = (jnp.arange(N_CTX, dtype=jnp.int32) * TDEV).astype(jnp.int32)
    attn = lax.map(attend, starts).reshape(L, HT * HS)
    hidden = resid.astype(jnp.float32) + jnp.dot(attn, w_out_t, preferred_element_type=jnp.float32)
    rscale = lax.rsqrt(lax.optimization_barrier(jnp.mean(hidden * hidden, axis=-1, keepdims=True)) + eps)
    normed = (hidden * rscale * norm_gain).astype(jnp.bfloat16)
    units = jnp.dot(normed, w_in, preferred_element_type=jnp.float32).astype(jnp.bfloat16)
    unit_blocks = units.reshape(L // TDEV, TDEV, DD)
    code_blocks = codes.reshape(L // TDEV, TDEV, K)

    def step(carry, pair):
        d_units, d_weight = depth_block(pair[0], pair[1], embed, w_qkv, w_o, w_head, DHS)
        return (carry + d_weight, d_units)
    d_wqkv, d_blocks = lax.scan(step, jnp.zeros((DD, 3 * DD), jnp.float32), (unit_blocks, code_blocks))
    d_units = d_blocks.reshape(L, DD)
    d_normed = jnp.einsum('fk,dk->fd', d_units, w_in, preferred_element_type=jnp.float32).astype(jnp.bfloat16)
    grad_gain = d_normed.astype(jnp.float32) * norm_gain
    dot_rows = lax.optimization_barrier(jnp.sum(grad_gain * hidden, axis=-1, keepdims=True))
    d_hidden = (rscale * grad_gain - hidden * rscale * rscale * rscale * dot_rows / D).astype(jnp.bfloat16)
    d_attn = jnp.einsum('rd,cd->rc', d_hidden, w_out_t, preferred_element_type=jnp.float32).astype(jnp.bfloat16)
    return (d_attn, d_wqkv)
```

```python
import math

import jax
import jax.numpy as jnp
from jax import lax
from jax.experimental import pallas as pl
from jax.experimental.pallas import tpu as pltpu
from jax.sharding import PartitionSpec as P

D = 4096
HS = 128
DHS = 64


eps = 1e-05
MESH = pl.DeviceIdType.MESH


def positions_of(index, block_of, half):
    which = index // half
    slots = jnp.arange(block_of.shape[0], dtype=jnp.int32)
    picked = jnp.sum(jnp.where(which[:, None] == slots[None, :], block_of[None, :], 0), axis=1)
    return picked * half + index % half


def rms_rows(values):
    return values * lax.rsqrt(jnp.mean(values * values, axis=-1, keepdims=True) + eps)


def depth_front(units, codes, embed):
    frames, steps = codes.shape
    width = embed.shape[1]
    earlier = jnp.take(embed, codes[:, : steps - 1], axis=0).astype(jnp.float32)
    lead = jnp.zeros((frames, 1, width), jnp.float32)
    stream = units.astype(jnp.float32)[:, None, :] + jnp.concatenate([lead, earlier], axis=1)
    normed = rms_rows(stream).astype(jnp.bfloat16).reshape(frames * steps, width)
    return (normed, stream)


def depth_back(packed, stream, codes, w_o, w_head, head_size):
    frames, steps, width = stream.shape
    heads = width // head_size
    parts = packed.reshape(frames, steps, 3, heads, head_size).astype(jnp.float32)
    scores = jnp.einsum("fqhd,fkhd->fhqk", parts[:, :, 0], parts[:, :, 1]) * (
        1.0 / math.sqrt(head_size)
    )
    causal = jnp.arange(steps)[:, None] >= jnp.arange(steps)[None, :]
    weights = jnp.where(causal, jnp.exp(scores), 0.0)
    weights = weights / jnp.sum(weights, axis=-1, keepdims=True)
    mixed = (
        jnp.einsum("fhqk,fkhd->fqhd", weights, parts[:, :, 2])
        .astype(jnp.bfloat16)
        .reshape(frames * steps, width)
    )
    after = stream.reshape(frames * steps, width) + jnp.dot(
        mixed, w_o, preferred_element_type=jnp.float32
    )
    normed = rms_rows(after).astype(jnp.bfloat16)
    logits = jnp.dot(normed, w_head, preferred_element_type=jnp.float32)
    total = jnp.log(jnp.sum(jnp.exp(logits), axis=-1))
    vocab = jnp.arange(w_head.shape[1], dtype=jnp.int32)
    picked = jnp.sum(jnp.where(codes.reshape(-1)[:, None] == vocab[None, :], logits, 0.0), axis=-1)
    return jnp.sum(total - picked)


def depth_block(units, codes, embed, w_qkv, w_o, w_head, head_size):
    normed, stream = depth_front(units, codes, embed)
    packed = jnp.dot(normed, w_qkv, preferred_element_type=jnp.float32).astype(jnp.bfloat16)
    loss, pull = jax.vjp(
        lambda a, b: depth_back(a, b, codes, w_o, w_head, head_size), packed, stream
    )
    d_packed, d_stream = pull(jnp.ones_like(loss))
    return normed, d_packed, stream.reshape(normed.shape), d_stream.reshape(normed.shape)


def place():
    ctx = lax.axis_index("ctx")
    depth = lax.axis_index("depth")
    x = ctx // 4
    y = (depth // 4) * 2 + (ctx // 2) % 2
    return x, y, ctx % 2, depth % 4


def device_at(x, y, core, z):
    return (x * 4 + (y % 2) * 2 + core, (y // 2) * 4 + z)


def step_of(p, by):
    return (p + by + 4) % 4


def greet(devices):
    barrier = pltpu.get_barrier_semaphore()
    for device in devices:
        pl.semaphore_signal(barrier, inc=1, device_id=device, device_id_type=MESH)
    pl.semaphore_wait(barrier, len(devices))


def rows_dot(a, b):
    return lax.dot_general(a, b, (((1,), (1,)), ((), ())), preferred_element_type=jnp.float32)


def columns_dot(a, b):
    return lax.dot_general(a, b, (((0,), (0,)), ((), ())), preferred_element_type=jnp.float32)


CB = 768
ORDER = (0, 2, 1, 3)


def tail_kernel(
    ynorm_in,
    packed_in,
    stream_in,
    dstream_in,
    hidden_in,
    gain_in,
    wqkv_in,
    win_in,
    wout_in,
    d_attn_ref,
    d_wqkv_ref,
    ynorm,
    d_packed,
    stream,
    d_stream,
    hidden,
    gain,
    wqkv,
    win,
    wout,
    dy,
    d_units,
    d_normed,
    d_hidden,
    d_other,
    g_parts,
    core_sum,
    first_in,
    first_out,
    second_in,
    third_out,
    third_in,
    load_sem,
    send_sem,
    recv_sem,
):
    x, y, core, z = place()
    other_core = device_at(x, y, 1 - core, z)

    def x_at(by):
        return device_at(step_of(x, by), y, core, z)

    def y_at(by):
        return device_at(x, step_of(y, by), core, z)

    def z_at(by):
        return device_at(x, y, core, step_of(z, by))

    loads = []
    pairs = (
        (ynorm_in, ynorm),
        (packed_in, d_packed),
        (wqkv_in, wqkv),
        (stream_in, stream),
        (dstream_in, d_stream),
        (win_in, win),
        (hidden_in, hidden),
        (gain_in, gain),
        (wout_in, wout),
    )
    for i, (source, target) in enumerate(pairs):
        load = pltpu.make_async_copy(source, target, load_sem.at[i])
        load.start()
        loads.append(load)
    greet([other_core] + [at(by) for at in (x_at, y_at, z_at) for by in (1, 2, 3)])

    count = [0]

    def send(source, target, device):
        i = count[0]
        count[0] += 1
        copy = pltpu.make_async_remote_copy(
            src_ref=source,
            dst_ref=target,
            send_sem=send_sem.at[i],
            recv_sem=recv_sem.at[i],
            device_id=device,
            device_id_type=MESH,
        )
        copy.start()
        return copy

    loads[0].wait()
    loads[1].wait()

    core_sends = {}
    far = {}
    near = {}

    def axis_of(cb):
        return (x, x_at) if cb < 2 else (y, y_at)

    def sign_of(cb):
        return 1 if cb % 2 == 0 else -1

    def chunk(cb, q):
        return core_sum.at[cb, q] if cb < 2 else core_sum.at[cb, :, q]

    def first_phase(cb):
        core_sends[cb].wait_recv()
        core_sum[cb] = (
            core_sum[cb].astype(jnp.float32) + g_parts[core, cb].astype(jnp.float32)
        ).astype(jnp.bfloat16)
        p, at = axis_of(cb)
        s = sign_of(cb)
        far[cb] = send(chunk(cb, step_of(p, 2)), first_in.at[cb, 0], at(s))
        near[cb] = send(chunk(cb, step_of(p, -s)), first_in.at[cb, 1], at(-s))

    for i, cb in enumerate(ORDER):

        def block(xi, carry, cb=cb):
            left = ynorm[:, pl.ds(pl.multiple_of(xi * 256, 256), 256)]
            product = columns_dot(left, d_packed[:, cb * CB : (cb + 1) * CB])
            product = product.astype(jnp.bfloat16)
            for ylo in range(2):
                for c in range(2):
                    for yhi in range(2):
                        at = ylo * 128 + c * 64 + yhi * 32
                        g_parts[c, cb, xi, yhi * 2 + ylo] = product[at : at + 32]
            return carry

        lax.fori_loop(0, 4, block, 0)
        core_sends[cb] = send(g_parts.at[1 - core, cb], core_sum.at[cb], other_core)
        if i > 0:
            first_phase(ORDER[i - 1])
    loads[2].wait()

    def dy_block(n, carry):
        columns = pl.ds(pl.multiple_of(n * 256, 256), 256)
        dy[:, columns] = rows_dot(d_packed[...], wqkv[columns, :]).astype(jnp.bfloat16)
        return carry

    lax.fori_loop(0, 4, dy_block, 0)
    first_phase(ORDER[3])
    loads[3].wait()
    loads[4].wait()

    def units_block(n, carry):
        rows = pl.ds(pl.multiple_of(n * 64, 64), 64)
        s = stream[rows, :]
        d = dy[rows, :].astype(jnp.float32)
        r = lax.rsqrt(jnp.mean(s * s, axis=-1, keepdims=True) + eps)
        dot = jnp.sum(d * s, axis=-1, keepdims=True)
        ds = d_stream[rows, :] + r * d - s * (r * r * r * dot / 1024)
        d_units[pl.ds(pl.multiple_of(n * 8, 8), 8), :] = jnp.sum(ds.reshape(8, 8, 1024), axis=1)
        return carry

    lax.fori_loop(0, 8, units_block, 0)
    loads[5].wait()

    def normed_block(n, carry):
        columns = pl.ds(pl.multiple_of(n * 512, 512), 512)
        d_normed[:, columns] = rows_dot(d_units[...].astype(jnp.bfloat16), win[columns, :]).astype(
            jnp.bfloat16
        )
        return carry

    lax.fori_loop(0, 8, normed_block, 0)
    loads[6].wait()
    loads[7].wait()
    for n in range(2):
        rows = pl.ds(n * 32, 32)
        h = hidden[rows, :]
        rscale = lax.rsqrt(jnp.mean(h * h, axis=-1, keepdims=True) + eps)
        grad_gain = d_normed[rows, :].astype(jnp.float32) * gain[...]
        dot_rows = jnp.sum(grad_gain * h, axis=-1, keepdims=True)
        d_hidden[z, rows, :] = (
            rscale * grad_gain - h * (rscale * rscale * rscale * dot_rows / D)
        ).astype(jnp.bfloat16)

    to_right = send(d_hidden.at[z], d_hidden.at[z], z_at(1))
    to_left = send(d_hidden.at[z], d_hidden.at[z], z_at(-1))

    second = {}
    last = {}
    for cb in ORDER:
        p, at = axis_of(cb)
        s = sign_of(cb)
        far[cb].wait_recv()
        mid = chunk(cb, step_of(p, s))
        mid[...] = (mid[...].astype(jnp.float32) + first_in[cb, 0].astype(jnp.float32)).astype(
            jnp.bfloat16
        )
        last[cb] = send(mid, first_in.at[cb, 2], at(s))

    loads[8].wait()

    for cb in ORDER:
        p, at = axis_of(cb)
        near[cb].wait_recv()
        last[cb].wait_recv()
        first_out[cb] = (
            chunk(cb, p)[...].astype(jnp.float32)
            + first_in[cb, 1].astype(jnp.float32)
            + first_in[cb, 2].astype(jnp.float32)
        ).astype(jnp.bfloat16)
        q, at = (y, y_at) if cb < 2 else (x, x_at)
        second[cb] = [
            send(first_out.at[cb, step_of(q, by)], second_in.at[cb, by - 1], at(by))
            for by in (1, 2, 3)
        ]

    to_right.wait_recv()
    on_right = send(
        d_hidden.at[step_of(z, -1), pl.ds(0, 32)], d_hidden.at[step_of(z, -1), pl.ds(0, 32)], z_at(1)
    )
    to_left.wait_recv()
    on_left = send(
        d_hidden.at[step_of(z, 1), pl.ds(32, 32)], d_hidden.at[step_of(z, 1), pl.ds(32, 32)], z_at(-1)
    )

    for pair in range(2):
        sums = []
        for cb in (2 * pair, 2 * pair + 1):
            q = y if cb < 2 else x
            total = first_out[cb, q].astype(jnp.float32)
            for by in (1, 2, 3):
                second[cb][by - 1].wait_recv()
                total += second_in[cb, by - 1].astype(jnp.float32)
            sums.append(total)
        for zq in range(4):
            third_out[zq, pair] = jnp.concatenate(
                [one[zq * 8 : zq * 8 + 8] for one in sums], axis=0
            ).astype(jnp.bfloat16)
    third = [
        send(third_out.at[step_of(z, by)], third_in.at[by - 1], z_at(by)) for by in (1, 2, 3)
    ]

    on_right.wait_recv()
    on_left.wait_recv()
    yhi = y // 2
    full = d_hidden[...].reshape(256, D)
    d_other[0] = rows_dot(full, wout[1 - yhi]).astype(jnp.bfloat16)
    to_other = send(d_other.at[0], d_other.at[1], y_at(2))
    d_attn_ref[pl.ds(pl.multiple_of(yhi * 256, 256), 256), :] = rows_dot(full, wout[yhi]).astype(
        jnp.bfloat16
    )

    for pair in range(2):
        total = third_out[z, pair].astype(jnp.float32)
        for by in (1, 2, 3):
            if pair == 0:
                third[by - 1].wait_recv()
            total += third_in[by - 1, pair].astype(jnp.float32)
        d_wqkv_ref[:, pair * 2 * CB : (pair * 2 + 1) * CB] = total[:8]
        d_wqkv_ref[:, (pair * 2 + 1) * CB : (pair * 2 + 2) * CB] = total[8:]

    to_other.wait_recv()
    d_attn_ref[pl.ds(pl.multiple_of((1 - yhi) * 256, 256), 256), :] = d_other[1]
    copies = list(core_sends.values()) + list(far.values()) + list(near.values())
    copies += list(last.values()) + [one for group in second.values() for one in group]
    copies += third + [to_right, to_left, on_right, on_left, to_other]
    for copy in copies:
        copy.wait_send()


def tail(ynorm, d_packed, stream, d_stream, hidden, gain, w_qkv, full_in, out_pair):
    bf16, f32 = jnp.bfloat16, jnp.float32
    operands = (ynorm, d_packed, stream, d_stream, hidden, gain, w_qkv, full_in, out_pair)
    return pl.pallas_call(
        tail_kernel,
        out_shape=(
            jax.ShapeDtypeStruct((512, 256), bf16),
            jax.ShapeDtypeStruct((8, 3072), f32),
        ),
        in_specs=[pl.BlockSpec(memory_space=pl.ANY)] * 9,
        out_specs=(pl.BlockSpec(memory_space=pltpu.VMEM),) * 2,
        scratch_shapes=[pltpu.VMEM(one.shape, one.dtype) for one in operands]
        + [
            pltpu.VMEM((512, 1024), bf16),
            pltpu.VMEM((64, 1024), f32),
            pltpu.VMEM((64, D), bf16),
            pltpu.VMEM((4, 64, D), bf16),
            pltpu.VMEM((2, 256, 256), bf16),
            pltpu.VMEM((2, 4, 4, 4, 32, CB), bf16),
            pltpu.VMEM((4, 4, 4, 32, CB), bf16),
            pltpu.VMEM((4, 3, 4, 32, CB), bf16),
            pltpu.VMEM((4, 4, 32, CB), bf16),
            pltpu.VMEM((4, 3, 32, CB), bf16),
            pltpu.VMEM((4, 2, 16, CB), bf16),
            pltpu.VMEM((3, 2, 16, CB), bf16),
            pltpu.SemaphoreType.DMA((9,)),
            pltpu.SemaphoreType.DMA((40,)),
            pltpu.SemaphoreType.DMA((40,)),
        ],
        compiler_params=pltpu.CompilerParams(
            collective_id=1, has_side_effects=True, vmem_limit_bytes=60 * 1024 * 1024
        ),
        cost_estimate=pl.CostEstimate(
            flops=9_000_000_000, bytes_accessed=30_000_000, transcendentals=0
        ),
    )(*operands)


def body(
    q_heads,
    k_heads,
    v_heads,
    block_of,
    resid,
    w_out_t,
    norm_gain,
    w_in,
    embed,
    w_qkv,
    w_o,
    w_head,
    codes,
):
    rows, width = q_heads.shape
    heads = width // HS
    half = rows // 2
    owners = lax.axis_size("depth")
    owned = rows // owners
    mine = lax.axis_index("depth")
    index = lax.axis_index("ctx") * rows + jnp.arange(rows, dtype=jnp.int32)
    pos_q = positions_of(index, block_of, half)
    queries = q_heads.reshape(rows, heads, HS)
    scale = 1.0 / math.sqrt(HS)
    start_state = (
        jnp.full((rows, heads), -1e30, jnp.float32),
        jnp.zeros((rows, heads), jnp.float32),
        jnp.zeros((rows, heads, HS), jnp.float32),
    )
    keys = lax.all_gather(k_heads, "ctx", axis=0, tiled=True)
    values = lax.all_gather(v_heads, "ctx", axis=0, tiled=True)
    count = keys.shape[0]
    pos_k = positions_of(jnp.arange(count, dtype=jnp.int32), block_of, half)
    visible = pos_q[:, None] >= pos_k[None, :]

    def compute(state):
        top, total, acc = state
        scores = (
            jnp.einsum(
                "qhd,khd->qhk",
                queries,
                keys.reshape(count, heads, HS),
                preferred_element_type=jnp.float32,
            )
            * scale
        )
        scores = jnp.where(visible[:, None, :], scores, -1e30)
        new_top = jnp.maximum(top, jnp.max(scores, axis=-1))
        weights = jnp.where(visible[:, None, :], jnp.exp(scores - new_top[:, :, None]), 0.0)
        total = jnp.sum(weights, axis=-1)
        acc = jnp.einsum(
            "qhk,khd->qhd",
            weights.astype(jnp.bfloat16),
            values.reshape(count, heads, HS),
            preferred_element_type=jnp.float32,
        )
        return (new_top, total, acc)

    top, total, acc = lax.cond(jnp.any(visible), compute, lambda state: state, start_state)
    attn = (acc / total[:, :, None]).astype(jnp.bfloat16).reshape(rows, width)
    partial_value = jnp.dot(attn, w_out_t, preferred_element_type=jnp.float32)
    offset = mine * owned
    own_rows = lax.dynamic_slice_in_dim(partial_value, offset, owned, 0) + resid.astype(jnp.float32)
    partial_value = lax.dynamic_update_slice_in_dim(partial_value, own_rows, offset, 0)
    hidden = lax.psum_scatter(
        partial_value.astype(jnp.bfloat16), "depth", scatter_dimension=0, tiled=True
    ).astype(jnp.float32)
    full_in = lax.all_gather(w_in, "depth", axis=0, tiled=True)
    rscale = lax.rsqrt(jnp.mean(hidden * hidden, axis=-1, keepdims=True) + eps)
    normed = (hidden * rscale * norm_gain).astype(jnp.bfloat16)
    units = jnp.dot(normed, full_in, preferred_element_type=jnp.float32).astype(jnp.bfloat16)
    ynorm, d_packed, stream, d_stream = depth_block(units, codes, embed, w_qkv, w_o, w_head, DHS)
    w_other = lax.ppermute(w_out_t, "depth", [(d, (d + 4) % 8) for d in range(8)])
    upper = mine // 4
    out_pair = jnp.where(
        upper == 0, jnp.stack([w_out_t, w_other]), jnp.stack([w_other, w_out_t])
    )
    d_attn, d_wqkv = tail(
        ynorm, d_packed, stream, d_stream, hidden, norm_gain.reshape(1, D), w_qkv, full_in, out_pair
    )
    return (d_attn, d_wqkv)


def solution(mesh):
    in_specs = (
        P("ctx", "depth"),
        P("ctx", "depth"),
        P("ctx", "depth"),
        P(),
        P(("ctx", "depth"), None),
        P("depth", None),
        P(),
        P("depth", None),
        P(),
        P(),
        P(),
        P(),
        P(("ctx", "depth"), None),
    )
    out_specs = (P("ctx", "depth"), P(("ctx", "depth"), None))
    return jax.shard_map(body, mesh=mesh, in_specs=in_specs, out_specs=out_specs, check_vma=False)
```

```python
import math

import jax
import jax.numpy as jnp
from jax import lax
from jax.experimental import pallas as pl
from jax.experimental.pallas import tpu as pltpu
from jax.sharding import PartitionSpec as P

D = 4096
HS = 128
DHS = 64


eps = 1e-05
MESH = pl.DeviceIdType.MESH


def place():
    ctx = lax.axis_index("ctx")
    depth = lax.axis_index("depth")
    x = ctx // 4
    y = (depth // 4) * 2 + (ctx // 2) % 2
    return x, y, ctx % 2, depth % 4


def device_at(x, y, core, z):
    return (x * 4 + (y % 2) * 2 + core, (y // 2) * 4 + z)


def step_of(p, by):
    return (p + by + 4) % 4


def greet(devices):
    barrier = pltpu.get_barrier_semaphore()
    for device in devices:
        pl.semaphore_signal(barrier, inc=1, device_id=device, device_id_type=MESH)
    pl.semaphore_wait(barrier, len(devices))


def rows_dot(a, b):
    return lax.dot_general(a, b, (((1,), (1,)), ((), ())), preferred_element_type=jnp.float32)


def columns_dot(a, b):
    return lax.dot_general(a, b, (((0,), (0,)), ((), ())), preferred_element_type=jnp.float32)


def front_kernel(
    block_of,
    q_in,
    k_in,
    v_in,
    resid_in,
    gain_ref,
    win_in,
    wout_in,
    embed_in,
    earlier_code,
    units_ref,
    earlier_ref,
    hidden_ref,
    win_out,
    wout_out,
    kv,
    queries,
    top,
    total,
    mixed,
    attn,
    heads_in,
    win,
    wout,
    embed,
    resid,
    partial,
    partial_in,
    normed,
    load_sem,
    send_sem,
    recv_sem,
):
    x, y, core, z = place()
    yhi = y // 2
    ylo = y % 2
    side = y + 1 - 2 * ylo
    cross = 3 - y
    own = yhi * 4 + z
    crossed = (1 - yhi) * 4 + z
    other_core = device_at(x, y, 1 - core, z)

    def x_at(by):
        return device_at(step_of(x, by), y, core, z)

    def z_at(by):
        return device_at(x, y, core, step_of(z, by))

    loads = []

    def load(source, target):
        i = len(loads)
        copy = pltpu.make_async_copy(source, target, load_sem.at[i])
        copy.start()
        loads.append(copy)
        return copy

    sends = []

    def send(source, target, device):
        i = len(sends)
        copy = pltpu.make_async_remote_copy(
            src_ref=source,
            dst_ref=target,
            send_sem=send_sem.at[i],
            recv_sem=recv_sem.at[i],
            device_id=device,
            device_id_type=MESH,
        )
        copy.start()
        sends.append(copy)
        return copy

    def half(which):
        return pl.ds(pl.multiple_of(which * 512, 512), 512)

    def lanes(which):
        return pl.ds(pl.multiple_of(which * 128, 128), 128)

    load_k = load(k_in.at[:, lanes(core)], kv.at[0, x, ylo, half(core)])
    load_v = load(v_in.at[:, lanes(core)], kv.at[1, x, ylo, half(core)])
    load_q = load(q_in.at[:, lanes(core)], queries.at[half(core)])
    greet(
        [
            other_core,
            x_at(1),
            x_at(-1),
            z_at(1),
            z_at(-1),
            device_at(x, side, core, z),
            device_at(x, cross, core, z),
            device_at(x, step_of(y, 2), core, z),
            device_at(x, step_of(y, 2), 1 - core, z),
        ]
    )
    swap_k = send(k_in.at[:, lanes(1 - core)], kv.at[0, x, ylo, half(core)], other_core)
    swap_v = send(v_in.at[:, lanes(1 - core)], kv.at[1, x, ylo, half(core)], other_core)
    swap_q = send(q_in.at[:, lanes(1 - core)], queries.at[half(core)], other_core)

    shard = win_in.at[pl.ds(pl.multiple_of(core * 256, 256), 256)]
    win_cross = send(shard, win.at[own, core], device_at(x, cross, core, z))
    win_right = send(shard, win.at[own, core], z_at(1))
    win_left = send(shard, win.at[own, core], z_at(-1))
    load_win = [
        load(win_in.at[pl.ds(i * 256, 256)], win.at[own, i]) for i in range(2)
    ]
    load_embed = load(embed_in, embed)
    load_wout = load(wout_in, wout.at[yhi])
    load_resid = load(resid_in, resid)

    load_k.wait()
    load_v.wait()
    swap_k.wait_recv()
    swap_v.wait_recv()
    kv_side = send(kv.at[:, x, ylo], kv.at[:, x, ylo], device_at(x, side, core, z))
    kv_right = send(kv.at[:, x, ylo], kv.at[:, x, ylo], x_at(1))
    kv_left = send(kv.at[:, x, ylo], kv.at[:, x, ylo], x_at(-1))

    top[...] = jnp.full_like(top, -1e29)
    total[...] = jnp.zeros_like(total)
    mixed[...] = jnp.zeros_like(mixed)
    factor = math.log2(math.e) / math.sqrt(HS)

    def attend(xi, yi):
        base = xi * 8 + yi * 4
        lane = lax.broadcasted_iota(jnp.int32, (1, 1024), 1)
        block = jnp.where(
            lane < 512,
            jnp.where(lane < 256, block_of[base], block_of[base + 1]),
            jnp.where(lane < 768, block_of[base + 2], block_of[base + 3]),
        )
        key_pos = lane % 256 + block * 256

        def rows_of(n, carry):
            rows = pl.ds(pl.multiple_of(n * 256, 256), 256)
            pos = lax.broadcasted_iota(jnp.int32, (256, 1), 0) + block_of[x * 8 + ylo * 4 + n] * 256
            scores = rows_dot(queries[rows, :], kv[0, xi, yi])
            scores = jnp.where(pos >= key_pos, scores, -1e30)
            before = top[rows, :]
            now = jnp.maximum(before, jnp.max(scores, axis=-1, keepdims=True))
            weights = jnp.exp2((scores - now[:, :1]) * factor)
            fade = jnp.exp2((before - now) * factor)
            top[rows, :] = now
            total[rows, :] = total[rows, :] * fade + jnp.sum(weights, axis=-1, keepdims=True)
            mixed[rows, :] = mixed[rows, :] * fade + jnp.dot(
                weights.astype(jnp.bfloat16), kv[1, xi, yi], preferred_element_type=jnp.float32
            )
            return carry

        lax.fori_loop(0, 4, rows_of, 0)

    load_q.wait()
    swap_q.wait_recv()
    attend(x, ylo)

    load_embed.wait()

    def look_up(n, carry):
        rows = pl.ds(pl.multiple_of(n * 128, 128), 128)
        entry = lax.broadcasted_iota(jnp.int32, (128, 2048), 1)
        hot = (entry == earlier_code[rows, :]).astype(jnp.bfloat16)
        earlier_ref[rows, :] = jnp.dot(
            hot, embed[...], preferred_element_type=jnp.float32
        ).astype(jnp.bfloat16)
        return carry

    lax.fori_loop(0, 4, look_up, 0)

    def pass_on(ref, left_arrived, right_arrived, at, before, after, first, second):
        left_arrived.wait_recv()
        on_right = send(ref(before, first), ref(before, first), at(1))
        right_arrived.wait_recv()
        on_left = send(ref(after, second), ref(after, second), at(-1))
        return on_right, on_left

    def kv_of(yi):
        return lambda xi, part: kv.at[:, xi, yi, part]

    def win_of(up):
        return lambda zi, part: win.at[up * 4 + zi, core, part]

    kv_side.wait_recv()
    side_lo = 1 - ylo
    side_right = send(kv.at[:, x, side_lo], kv.at[:, x, side_lo], x_at(1))
    side_left = send(kv.at[:, x, side_lo], kv.at[:, x, side_lo], x_at(-1))
    win_cross.wait_recv()
    cross_right = send(win.at[crossed, core], win.at[crossed, core], z_at(1))
    cross_left = send(win.at[crossed, core], win.at[crossed, core], z_at(-1))
    wout_half = pl.ds(pl.multiple_of(core * 128, 128), 128)
    wout_cross = send(
        wout_in.at[wout_half], wout.at[yhi, wout_half], device_at(x, cross, core, z)
    )
    to_core = [send(win.at[crossed, core], win.at[crossed, core], other_core)]
    attend(x, side_lo)

    before_x, after_x = step_of(x, -1), step_of(x, 1)
    before_z, after_z = step_of(z, -1), step_of(z, 1)
    win_on = pass_on(
        win_of(yhi), win_right, win_left, z_at, before_z, after_z, pl.ds(0, 128), pl.ds(128, 128)
    )
    kv_on = pass_on(
        kv_of(ylo), kv_right, kv_left, x_at, before_x, after_x, pl.ds(0, 512), pl.ds(512, 512)
    )
    for zi in (before_z, after_z):
        to_core.append(send(win.at[yhi * 4 + zi, core], win.at[yhi * 4 + zi, core], other_core))
    attend(before_x, ylo)
    attend(after_x, ylo)
    side_on = pass_on(
        kv_of(side_lo), side_right, side_left, x_at, before_x, after_x, pl.ds(0, 512), pl.ds(512, 512)
    )
    cross_on = pass_on(
        win_of(1 - yhi), cross_right, cross_left, z_at, before_z, after_z, pl.ds(0, 128), pl.ds(128, 128)
    )
    for zi in (before_z, after_z):
        at = (1 - yhi) * 4 + zi
        to_core.append(send(win.at[at, core], win.at[at, core], other_core))
    attend(before_x, side_lo)
    attend(after_x, side_lo)
    wout_cross.wait_recv()
    wout_core = send(wout.at[1 - yhi, wout_half], wout.at[1 - yhi, wout_half], other_core)
    for one in kv_on:
        one.wait_recv()
    attend(step_of(x, 2), ylo)
    for one in win_on:
        one.wait_recv()
    at = yhi * 4 + step_of(z, 2)
    to_core.append(send(win.at[at, core], win.at[at, core], other_core))
    for one in side_on:
        one.wait_recv()
    attend(step_of(x, 2), side_lo)

    for n in range(4):
        rows = pl.ds(n * 256, 256)
        attn[n // 2, n % 2] = (mixed[rows, :] / total[rows, :]).astype(jnp.bfloat16)
    swaps = [
        send(attn.at[1 - core, yhi], heads_in.at[yhi, core], other_core),
        send(
            attn.at[core, 1 - yhi],
            heads_in.at[yhi, core],
            device_at(x, step_of(y, 2), core, z),
        ),
        send(
            attn.at[1 - core, 1 - yhi],
            heads_in.at[yhi, core],
            device_at(x, step_of(y, 2), 1 - core, z),
        ),
    ]
    heads_in[yhi, core] = attn[core, yhi]
    for one in cross_on:
        one.wait_recv()
    at = (1 - yhi) * 4 + step_of(z, 2)
    to_core.append(send(win.at[at, core], win.at[at, core], other_core))
    load_wout.wait()
    wout_core.wait_recv()
    store_wout = load(wout, wout_out)
    for one in swaps:
        one.wait_recv()

    far = {}
    near = {}
    last = {}
    for cb in range(4):
        s = 1 if cb % 2 == 0 else -1
        columns = pl.ds(cb * 1024, 1024)
        sums = jnp.zeros((256, 1024), jnp.float32)
        for up in range(2):
            left = jnp.concatenate([heads_in[up, 0], heads_in[up, 1]], axis=1)
            sums += jnp.dot(left, wout[up, :, columns], preferred_element_type=jnp.float32)
        partial[cb] = sums.astype(jnp.bfloat16).reshape(4, 64, 1024)
        far[cb] = send(partial.at[cb, step_of(z, 2)], partial_in.at[cb, 0], z_at(s))
        near[cb] = send(partial.at[cb, step_of(z, -s)], partial_in.at[cb, 1], z_at(-s))
    for cb in range(4):
        s = 1 if cb % 2 == 0 else -1
        far[cb].wait_recv()
        mid = step_of(z, s)
        partial[cb, mid] = (
            partial[cb, mid].astype(jnp.float32) + partial_in[cb, 0].astype(jnp.float32)
        ).astype(jnp.bfloat16)
        last[cb] = send(partial.at[cb, mid], partial_in.at[cb, 2], z_at(s))
    load_resid.wait()
    squares = jnp.zeros((64, 1), jnp.float32)
    for cb in range(4):
        columns = pl.ds(cb * 1024, 1024)
        near[cb].wait_recv()
        last[cb].wait_recv()
        h = partial[cb, z].astype(jnp.float32) + resid[:, columns].astype(jnp.float32)
        h = h + partial_in[cb, 1].astype(jnp.float32) + partial_in[cb, 2].astype(jnp.float32)
        hidden_ref[:, columns] = h
        squares += jnp.sum(h * h, axis=-1, keepdims=True)
    rscale = lax.rsqrt(squares / D + eps)
    for cb in range(4):
        columns = pl.ds(cb * 1024, 1024)
        normed[:, columns] = (hidden_ref[:, columns] * rscale * gain_ref[:, columns]).astype(
            jnp.bfloat16
        )
    for one in load_win:
        one.wait()
    for one in to_core:
        one.wait_recv()
    store_win = load(win, win_out)

    def enter(n, carry):
        columns = pl.ds(pl.multiple_of(n * 256, 256), 256)
        units_ref[:, columns] = jnp.dot(
            normed[...],
            win[:, :, :, columns].reshape(D, 256),
            preferred_element_type=jnp.float32,
        ).astype(jnp.bfloat16)
        return carry

    lax.fori_loop(0, 4, enter, 0)
    store_wout.wait()
    store_win.wait()
    for one in sends:
        one.wait_send()


def front(block_of, q, k, v, resid, gain, w_in, w_out, embed, earlier_code):
    bf16, f32 = jnp.bfloat16, jnp.float32
    shapes = (
        ((64, 1024), bf16),
        ((512, 1024), bf16),
        ((64, D), f32),
        ((8, 2, 256, 1024), bf16),
        ((2, 256, D), bf16),
    )
    vmem = pl.BlockSpec(memory_space=pltpu.VMEM)
    anywhere = pl.BlockSpec(memory_space=pl.ANY)
    return pl.pallas_call(
        front_kernel,
        out_shape=tuple(jax.ShapeDtypeStruct(*one) for one in shapes),
        in_specs=[pl.BlockSpec(memory_space=pltpu.SMEM)]
        + [anywhere] * 4
        + [vmem]
        + [anywhere] * 3
        + [vmem],
        out_specs=(vmem, vmem, vmem, anywhere, anywhere),
        scratch_shapes=[
            pltpu.VMEM((2, 4, 2, 1024, HS), bf16),
            pltpu.VMEM((1024, HS), bf16),
            pltpu.VMEM((1024, HS), f32),
            pltpu.VMEM((1024, HS), f32),
            pltpu.VMEM((1024, HS), f32),
            pltpu.VMEM((2, 2, 256, HS), bf16),
            pltpu.VMEM((2, 2, 256, HS), bf16),
            pltpu.VMEM((8, 2, 256, 1024), bf16),
            pltpu.VMEM((2, 256, D), bf16),
            pltpu.VMEM((2048, 1024), bf16),
            pltpu.VMEM((64, D), bf16),
            pltpu.VMEM((4, 4, 64, 1024), bf16),
            pltpu.VMEM((4, 3, 64, 1024), bf16),
            pltpu.VMEM((64, D), bf16),
            pltpu.SemaphoreType.DMA((12,)),
            pltpu.SemaphoreType.DMA((48,)),
            pltpu.SemaphoreType.DMA((48,)),
        ],
        compiler_params=pltpu.CompilerParams(
            collective_id=2, has_side_effects=True, vmem_limit_bytes=60 * 1024 * 1024
        ),
        cost_estimate=pl.CostEstimate(
            flops=9_000_000_000, bytes_accessed=40_000_000, transcendentals=8_000_000
        ),
    )(block_of, q, k, v, resid, gain, w_in, w_out, embed, earlier_code)


STEPS = 8
GROUP = 128


def lower_lanes():
    return lax.broadcasted_iota(jnp.int32, (1, 128), 1) < DHS


def split_heads(value, low):
    zero = jnp.zeros_like(value)
    return jnp.concatenate([jnp.where(low, value, zero), jnp.where(low, zero, value)], axis=0)


def join_heads(value, low):
    return jnp.where(low, value[:GROUP], value[GROUP:])


def per_head(op, value):
    return jnp.concatenate(
        [
            jnp.broadcast_to(op(half, axis=-1, keepdims=True), half.shape)
            for half in (value[:, :GROUP], value[:, GROUP:])
        ],
        axis=1,
    )


def depth_kernel(
    units_ref,
    earlier_ref,
    code_ref,
    wqkv_in,
    wo_in,
    whead_in,
    ynorm,
    d_packed,
    stream,
    d_stream,
    wqkv,
    wo,
    whead,
    packed,
    weights,
    mixed,
    after,
    ynorm2,
    grown,
    d_logits,
    dy2,
    load_sem,
):
    loads = []
    for i, (source, target) in enumerate(((wqkv_in, wqkv), (wo_in, wo), (whead_in, whead))):
        load = pltpu.make_async_copy(source, target, load_sem.at[i])
        load.start()
        loads.append(load)
    frame_of = lax.broadcasted_iota(jnp.int32, (GROUP, 16), 0) // STEPS
    spread = (frame_of == lax.broadcasted_iota(jnp.int32, (GROUP, 16), 1)).astype(jnp.bfloat16)

    def front(n, carry):
        rows = pl.ds(pl.multiple_of(n * GROUP, GROUP), GROUP)
        units = units_ref[pl.ds(pl.multiple_of(n * 16, 16), 16), :]
        s = jnp.dot(spread, units, preferred_element_type=jnp.float32)
        s = s + earlier_ref[rows, :].astype(jnp.float32)
        r = lax.rsqrt(jnp.mean(s * s, axis=-1, keepdims=True) + eps)
        stream[rows, :] = s
        ynorm[rows, :] = (s * r).astype(jnp.bfloat16)
        return carry

    lax.fori_loop(0, 4, front, 0)
    loads[0].wait()

    def project(n, carry):
        columns = pl.ds(pl.multiple_of(n * 512, 512), 512)
        packed[:, columns] = jnp.dot(
            ynorm[...], wqkv[:, columns], preferred_element_type=jnp.float32
        ).astype(jnp.bfloat16)
        return carry

    lax.fori_loop(0, 6, project, 0)

    low = lower_lanes()
    row = lax.broadcasted_iota(jnp.int32, (GROUP, 2 * GROUP), 0)
    column = lax.broadcasted_iota(jnp.int32, (GROUP, 2 * GROUP), 1) % GROUP
    seen = jnp.logical_and(row // STEPS == column // STEPS, column <= row)

    def mix(n, carry):
        rows = pl.ds(pl.multiple_of(n * GROUP, GROUP), GROUP)
        for pair in range(8):
            at = pair * 128
            q = packed[rows, at : at + 128]
            k = split_heads(packed[rows, 1024 + at : 1024 + at + 128], low)
            v = split_heads(packed[rows, 2048 + at : 2048 + at + 128], low)
            scores = rows_dot(q, k) * (1.0 / math.sqrt(DHS))
            grown_scores = jnp.exp(jnp.where(seen, scores, -1e30))
            a = (grown_scores / per_head(jnp.sum, grown_scores)).astype(jnp.bfloat16)
            weights[pair, rows, :] = a
            mixed[rows, at : at + 128] = jnp.dot(
                a, v, preferred_element_type=jnp.float32
            ).astype(jnp.bfloat16)
        return carry

    lax.fori_loop(0, 4, mix, 0)
    loads[1].wait()

    def add_mixed(n, carry):
        columns = pl.ds(pl.multiple_of(n * 256, 256), 256)
        after[:, columns] = stream[:, columns] + jnp.dot(
            mixed[...], wo[:, columns], preferred_element_type=jnp.float32
        )
        return carry

    lax.fori_loop(0, 4, add_mixed, 0)

    def norm2(n, carry):
        rows = pl.ds(pl.multiple_of(n * 64, 64), 64)
        s = after[rows, :]
        r = lax.rsqrt(jnp.mean(s * s, axis=-1, keepdims=True) + eps)
        ynorm2[rows, :] = (s * r).astype(jnp.bfloat16)
        return carry

    lax.fori_loop(0, 8, norm2, 0)
    loads[2].wait()

    def grow(n, total):
        columns = pl.ds(pl.multiple_of(n * 256, 256), 256)
        e = jnp.exp(
            jnp.dot(ynorm2[...], whead[:, columns], preferred_element_type=jnp.float32)
        )
        grown[:, columns] = e
        return total + jnp.sum(e, axis=-1, keepdims=True)

    total = lax.fori_loop(0, 8, grow, jnp.zeros((512, 1), jnp.float32))
    inverse = 1.0 / total
    code = code_ref[...]

    def from_loss(n, carry):
        columns = pl.ds(pl.multiple_of(n * 256, 256), 256)
        entry = lax.broadcasted_iota(jnp.int32, (512, 256), 1) + n * 256
        d_logits[:, columns] = (
            grown[:, columns] * inverse - (entry == code).astype(jnp.float32)
        ).astype(jnp.bfloat16)
        return carry

    lax.fori_loop(0, 8, from_loss, 0)

    def to_ynorm2(n, carry):
        columns = pl.ds(pl.multiple_of(n * 256, 256), 256)
        dy2[:, columns] = rows_dot(d_logits[...], whead[columns, :]).astype(jnp.bfloat16)
        return carry

    lax.fori_loop(0, 4, to_ynorm2, 0)

    def to_after(n, carry):
        rows = pl.ds(pl.multiple_of(n * 64, 64), 64)
        s = after[rows, :]
        d = dy2[rows, :].astype(jnp.float32)
        r = lax.rsqrt(jnp.mean(s * s, axis=-1, keepdims=True) + eps)
        dot = jnp.sum(d * s, axis=-1, keepdims=True)
        da = r * d - s * (r * r * r * dot / 1024)
        d_stream[rows, :] = da
        dy2[rows, :] = da.astype(jnp.bfloat16)
        return carry

    lax.fori_loop(0, 8, to_after, 0)

    def to_mixed(n, carry):
        columns = pl.ds(pl.multiple_of(n * 256, 256), 256)
        mixed[:, columns] = rows_dot(dy2[...], wo[columns, :]).astype(jnp.bfloat16)
        return carry

    lax.fori_loop(0, 4, to_mixed, 0)

    def unmix(n, carry):
        rows = pl.ds(pl.multiple_of(n * GROUP, GROUP), GROUP)
        for pair in range(8):
            at = pair * 128
            q = packed[rows, at : at + 128]
            k = split_heads(packed[rows, 1024 + at : 1024 + at + 128], low)
            v = split_heads(packed[rows, 2048 + at : 2048 + at + 128], low)
            d_mixed = mixed[rows, at : at + 128]
            a = weights[pair, rows, :]
            wide = a.astype(jnp.float32)
            part = wide * rows_dot(d_mixed, v)
            ds = (part - wide * per_head(jnp.sum, part)) * (1.0 / math.sqrt(DHS))
            ds = ds.astype(jnp.bfloat16)
            d_packed[rows, at : at + 128] = jnp.dot(
                ds, k, preferred_element_type=jnp.float32
            ).astype(jnp.bfloat16)
            d_packed[rows, 1024 + at : 1024 + at + 128] = join_heads(
                columns_dot(ds, q), low
            ).astype(jnp.bfloat16)
            d_packed[rows, 2048 + at : 2048 + at + 128] = join_heads(
                columns_dot(a, d_mixed), low
            ).astype(jnp.bfloat16)
        return carry

    lax.fori_loop(0, 4, unmix, 0)


def depth_step(units, earlier, code, w_qkv, w_o, w_head):
    bf16, f32 = jnp.bfloat16, jnp.float32
    shapes = (
        ((512, 1024), bf16),
        ((512, 3072), bf16),
        ((512, 1024), f32),
        ((512, 1024), f32),
    )
    return pl.pallas_call(
        depth_kernel,
        out_shape=tuple(jax.ShapeDtypeStruct(*one) for one in shapes),
        in_specs=[pl.BlockSpec(memory_space=pltpu.VMEM)] * 3
        + [pl.BlockSpec(memory_space=pl.ANY)] * 3,
        out_specs=(pl.BlockSpec(memory_space=pltpu.VMEM),) * 4,
        scratch_shapes=[
            pltpu.VMEM((1024, 3072), bf16),
            pltpu.VMEM((1024, 1024), bf16),
            pltpu.VMEM((1024, 2048), bf16),
            pltpu.VMEM((512, 3072), bf16),
            pltpu.VMEM((8, 512, 256), bf16),
            pltpu.VMEM((512, 1024), bf16),
            pltpu.VMEM((512, 1024), f32),
            pltpu.VMEM((512, 1024), bf16),
            pltpu.VMEM((512, 2048), f32),
            pltpu.VMEM((512, 2048), bf16),
            pltpu.VMEM((512, 1024), bf16),
            pltpu.SemaphoreType.DMA((3,)),
        ],
        compiler_params=pltpu.CompilerParams(vmem_limit_bytes=60 * 1024 * 1024),
        cost_estimate=pl.CostEstimate(
            flops=13_000_000_000, bytes_accessed=30_000_000, transcendentals=2_000_000
        ),
    )(units, earlier, code, w_qkv, w_o, w_head)


CB = 768
ORDER = (0, 2, 1, 3)


def tail_kernel(
    ynorm_in,
    packed_in,
    stream_in,
    dstream_in,
    hidden_in,
    gain_in,
    wqkv_in,
    win_in,
    wout_in,
    d_attn_ref,
    d_wqkv_ref,
    ynorm,
    d_packed,
    stream,
    d_stream,
    hidden,
    gain,
    wqkv,
    win,
    wout,
    dy,
    d_units,
    d_normed,
    d_hidden,
    d_other,
    g_parts,
    core_sum,
    first_in,
    first_out,
    second_in,
    third_out,
    third_in,
    load_sem,
    send_sem,
    recv_sem,
):
    x, y, core, z = place()
    other_core = device_at(x, y, 1 - core, z)

    def x_at(by):
        return device_at(step_of(x, by), y, core, z)

    def y_at(by):
        return device_at(x, step_of(y, by), core, z)

    def z_at(by):
        return device_at(x, y, core, step_of(z, by))

    loads = []
    pairs = (
        (ynorm_in, ynorm),
        (packed_in, d_packed),
        (wqkv_in, wqkv),
        (stream_in, stream),
        (dstream_in, d_stream),
        (win_in, win),
        (hidden_in, hidden),
        (gain_in, gain),
        (wout_in, wout),
    )
    for i, (source, target) in enumerate(pairs):
        load = pltpu.make_async_copy(source, target, load_sem.at[i])
        load.start()
        loads.append(load)
    greet([other_core] + [at(by) for at in (x_at, y_at, z_at) for by in (1, 2, 3)])

    count = [0]

    def send(source, target, device):
        i = count[0]
        count[0] += 1
        copy = pltpu.make_async_remote_copy(
            src_ref=source,
            dst_ref=target,
            send_sem=send_sem.at[i],
            recv_sem=recv_sem.at[i],
            device_id=device,
            device_id_type=MESH,
        )
        copy.start()
        return copy

    loads[0].wait()
    loads[1].wait()

    core_sends = {}
    far = {}
    near = {}

    def axis_of(cb):
        return (x, x_at) if cb < 2 else (y, y_at)

    def sign_of(cb):
        return 1 if cb % 2 == 0 else -1

    def chunk(cb, q):
        return core_sum.at[cb, q] if cb < 2 else core_sum.at[cb, :, q]

    def first_phase(cb):
        core_sends[cb].wait_recv()
        core_sum[cb] = (
            core_sum[cb].astype(jnp.float32) + g_parts[core, cb].astype(jnp.float32)
        ).astype(jnp.bfloat16)
        p, at = axis_of(cb)
        s = sign_of(cb)
        far[cb] = send(chunk(cb, step_of(p, 2)), first_in.at[cb, 0], at(s))
        near[cb] = send(chunk(cb, step_of(p, -s)), first_in.at[cb, 1], at(-s))

    for i, cb in enumerate(ORDER):

        def block(xi, carry, cb=cb):
            left = ynorm[:, pl.ds(pl.multiple_of(xi * 256, 256), 256)]
            product = columns_dot(left, d_packed[:, cb * CB : (cb + 1) * CB])
            product = product.astype(jnp.bfloat16)
            for ylo in range(2):
                for c in range(2):
                    for yhi in range(2):
                        at = ylo * 128 + c * 64 + yhi * 32
                        g_parts[c, cb, xi, yhi * 2 + ylo] = product[at : at + 32]
            return carry

        lax.fori_loop(0, 4, block, 0)
        core_sends[cb] = send(g_parts.at[1 - core, cb], core_sum.at[cb], other_core)
        if i > 0:
            first_phase(ORDER[i - 1])
    loads[2].wait()

    def dy_block(n, carry):
        columns = pl.ds(pl.multiple_of(n * 256, 256), 256)
        dy[:, columns] = rows_dot(d_packed[...], wqkv[columns, :]).astype(jnp.bfloat16)
        return carry

    lax.fori_loop(0, 4, dy_block, 0)
    first_phase(ORDER[3])
    loads[3].wait()
    loads[4].wait()

    def units_block(n, carry):
        rows = pl.ds(pl.multiple_of(n * 64, 64), 64)
        s = stream[rows, :]
        d = dy[rows, :].astype(jnp.float32)
        r = lax.rsqrt(jnp.mean(s * s, axis=-1, keepdims=True) + eps)
        dot = jnp.sum(d * s, axis=-1, keepdims=True)
        ds = d_stream[rows, :] + r * d - s * (r * r * r * dot / 1024)
        d_units[pl.ds(pl.multiple_of(n * 8, 8), 8), :] = jnp.sum(ds.reshape(8, 8, 1024), axis=1)
        return carry

    lax.fori_loop(0, 8, units_block, 0)
    loads[5].wait()

    def normed_block(n, carry):
        columns = pl.ds(pl.multiple_of(n * 512, 512), 512)
        d_normed[:, columns] = rows_dot(d_units[...].astype(jnp.bfloat16), win[columns, :]).astype(
            jnp.bfloat16
        )
        return carry

    lax.fori_loop(0, 8, normed_block, 0)
    loads[6].wait()
    loads[7].wait()
    for n in range(2):
        rows = pl.ds(n * 32, 32)
        h = hidden[rows, :]
        rscale = lax.rsqrt(jnp.mean(h * h, axis=-1, keepdims=True) + eps)
        grad_gain = d_normed[rows, :].astype(jnp.float32) * gain[...]
        dot_rows = jnp.sum(grad_gain * h, axis=-1, keepdims=True)
        d_hidden[z, rows, :] = (
            rscale * grad_gain - h * (rscale * rscale * rscale * dot_rows / D)
        ).astype(jnp.bfloat16)

    to_right = send(d_hidden.at[z], d_hidden.at[z], z_at(1))
    to_left = send(d_hidden.at[z], d_hidden.at[z], z_at(-1))

    second = {}
    last = {}
    for cb in ORDER:
        p, at = axis_of(cb)
        s = sign_of(cb)
        far[cb].wait_recv()
        mid = chunk(cb, step_of(p, s))
        mid[...] = (mid[...].astype(jnp.float32) + first_in[cb, 0].astype(jnp.float32)).astype(
            jnp.bfloat16
        )
        last[cb] = send(mid, first_in.at[cb, 2], at(s))

    loads[8].wait()

    for cb in ORDER:
        p, at = axis_of(cb)
        near[cb].wait_recv()
        last[cb].wait_recv()
        first_out[cb] = (
            chunk(cb, p)[...].astype(jnp.float32)
            + first_in[cb, 1].astype(jnp.float32)
            + first_in[cb, 2].astype(jnp.float32)
        ).astype(jnp.bfloat16)
        q, at = (y, y_at) if cb < 2 else (x, x_at)
        second[cb] = [
            send(first_out.at[cb, step_of(q, by)], second_in.at[cb, by - 1], at(by))
            for by in (1, 2, 3)
        ]

    to_right.wait_recv()
    on_right = send(
        d_hidden.at[step_of(z, -1), pl.ds(0, 32)], d_hidden.at[step_of(z, -1), pl.ds(0, 32)], z_at(1)
    )
    to_left.wait_recv()
    on_left = send(
        d_hidden.at[step_of(z, 1), pl.ds(32, 32)], d_hidden.at[step_of(z, 1), pl.ds(32, 32)], z_at(-1)
    )

    for pair in range(2):
        sums = []
        for cb in (2 * pair, 2 * pair + 1):
            q = y if cb < 2 else x
            total = first_out[cb, q].astype(jnp.float32)
            for by in (1, 2, 3):
                second[cb][by - 1].wait_recv()
                total += second_in[cb, by - 1].astype(jnp.float32)
            sums.append(total)
        for zq in range(4):
            third_out[zq, pair] = jnp.concatenate(
                [one[zq * 8 : zq * 8 + 8] for one in sums], axis=0
            ).astype(jnp.bfloat16)
    third = [
        send(third_out.at[step_of(z, by)], third_in.at[by - 1], z_at(by)) for by in (1, 2, 3)
    ]

    on_right.wait_recv()
    on_left.wait_recv()
    yhi = y // 2
    full = d_hidden[...].reshape(256, D)
    d_other[0] = rows_dot(full, wout[1 - yhi]).astype(jnp.bfloat16)
    to_other = send(d_other.at[0], d_other.at[1], y_at(2))
    d_attn_ref[pl.ds(pl.multiple_of(yhi * 256, 256), 256), :] = rows_dot(full, wout[yhi]).astype(
        jnp.bfloat16
    )

    for pair in range(2):
        total = third_out[z, pair].astype(jnp.float32)
        for by in (1, 2, 3):
            if pair == 0:
                third[by - 1].wait_recv()
            total += third_in[by - 1, pair].astype(jnp.float32)
        d_wqkv_ref[:, pair * 2 * CB : (pair * 2 + 1) * CB] = total[:8]
        d_wqkv_ref[:, (pair * 2 + 1) * CB : (pair * 2 + 2) * CB] = total[8:]

    to_other.wait_recv()
    d_attn_ref[pl.ds(pl.multiple_of((1 - yhi) * 256, 256), 256), :] = d_other[1]
    copies = list(core_sends.values()) + list(far.values()) + list(near.values())
    copies += list(last.values()) + [one for group in second.values() for one in group]
    copies += third + [to_right, to_left, on_right, on_left, to_other]
    for copy in copies:
        copy.wait_send()


def tail(ynorm, d_packed, stream, d_stream, hidden, gain, w_qkv, full_in, out_pair):
    bf16, f32 = jnp.bfloat16, jnp.float32
    operands = (ynorm, d_packed, stream, d_stream, hidden, gain, w_qkv, full_in, out_pair)
    return pl.pallas_call(
        tail_kernel,
        out_shape=(
            jax.ShapeDtypeStruct((512, 256), bf16),
            jax.ShapeDtypeStruct((8, 3072), f32),
        ),
        in_specs=[pl.BlockSpec(memory_space=pl.ANY)] * 9,
        out_specs=(pl.BlockSpec(memory_space=pltpu.VMEM),) * 2,
        scratch_shapes=[pltpu.VMEM(one.shape, one.dtype) for one in operands]
        + [
            pltpu.VMEM((512, 1024), bf16),
            pltpu.VMEM((64, 1024), f32),
            pltpu.VMEM((64, D), bf16),
            pltpu.VMEM((4, 64, D), bf16),
            pltpu.VMEM((2, 256, 256), bf16),
            pltpu.VMEM((2, 4, 4, 4, 32, CB), bf16),
            pltpu.VMEM((4, 4, 4, 32, CB), bf16),
            pltpu.VMEM((4, 3, 4, 32, CB), bf16),
            pltpu.VMEM((4, 4, 32, CB), bf16),
            pltpu.VMEM((4, 3, 32, CB), bf16),
            pltpu.VMEM((4, 2, 16, CB), bf16),
            pltpu.VMEM((3, 2, 16, CB), bf16),
            pltpu.SemaphoreType.DMA((9,)),
            pltpu.SemaphoreType.DMA((40,)),
            pltpu.SemaphoreType.DMA((40,)),
        ],
        compiler_params=pltpu.CompilerParams(
            collective_id=1, has_side_effects=True, vmem_limit_bytes=60 * 1024 * 1024
        ),
        cost_estimate=pl.CostEstimate(
            flops=9_000_000_000, bytes_accessed=30_000_000, transcendentals=0
        ),
    )(*operands)


def body(
    q_heads,
    k_heads,
    v_heads,
    block_of,
    resid,
    w_out_t,
    norm_gain,
    w_in,
    embed,
    w_qkv,
    w_o,
    w_head,
    codes,
):
    gain = norm_gain.reshape(1, D)
    first = jnp.full((codes.shape[0], 1), -1, codes.dtype)
    earlier_code = jnp.concatenate([first, codes[:, :-1]], axis=1).reshape(-1, 1)
    units, earlier, hidden, win, wout = front(
        block_of, q_heads, k_heads, v_heads, resid, gain, w_in, w_out_t, embed, earlier_code
    )
    ynorm, d_packed, stream, d_stream = depth_step(
        units, earlier, codes.reshape(-1, 1), w_qkv, w_o, w_head
    )
    return tail(
        ynorm, d_packed, stream, d_stream, hidden, gain, w_qkv, win.reshape(D, -1), wout
    )


def solution(mesh):
    in_specs = (
        P("ctx", "depth"),
        P("ctx", "depth"),
        P("ctx", "depth"),
        P(),
        P(("ctx", "depth"), None),
        P("depth", None),
        P(),
        P("depth", None),
        P(),
        P(),
        P(),
        P(),
        P(("ctx", "depth"), None),
    )
    out_specs = (P("ctx", "depth"), P(("ctx", "depth"), None))
    return jax.shard_map(body, mesh=mesh, in_specs=in_specs, out_specs=out_specs, check_vma=False)
```

```python
import math

import jax
import jax.numpy as jnp
from jax import lax
from jax.experimental import pallas as pl
from jax.experimental.pallas import tpu as pltpu
from jax.sharding import PartitionSpec as P

D = 4096
HS = 128
DHS = 64


eps = 1e-05
MESH = pl.DeviceIdType.MESH


def place():
    ctx = lax.axis_index("ctx")
    depth = lax.axis_index("depth")
    x = ctx // 4
    y = (depth // 4) * 2 + (ctx // 2) % 2
    return x, y, ctx % 2, depth % 4


def device_at(x, y, core, z):
    return (x * 4 + (y % 2) * 2 + core, (y // 2) * 4 + z)


def step_of(p, by):
    return (p + by + 4) % 4


def greet(devices):
    barrier = pltpu.get_barrier_semaphore()
    for device in devices:
        pl.semaphore_signal(barrier, inc=1, device_id=device, device_id_type=MESH)
    pl.semaphore_wait(barrier, len(devices))


def rows_dot(a, b):
    return lax.dot_general(a, b, (((1,), (1,)), ((), ())), preferred_element_type=jnp.float32)


def front_kernel(
    block_of,
    q_in,
    k_in,
    v_in,
    resid_in,
    gain_ref,
    win_in,
    wout_in,
    embed_in,
    earlier_code,
    units_ref,
    earlier_ref,
    hidden_ref,
    win_out,
    wout_out,
    kv,
    queries,
    top,
    total,
    mixed,
    attn,
    heads_in,
    win,
    wout,
    embed,
    resid,
    partial,
    partial_in,
    hidden,
    normed,
    load_sem,
    send_sem,
    recv_sem,
):
    x, y, core, z = place()
    yhi = y // 2
    ylo = y % 2
    side = y + 1 - 2 * ylo
    cross = 3 - y
    own = yhi * 4 + z
    crossed = (1 - yhi) * 4 + z
    other_core = device_at(x, y, 1 - core, z)

    def x_at(by):
        return device_at(step_of(x, by), y, core, z)

    def z_at(by):
        return device_at(x, y, core, step_of(z, by))

    loads = []

    def load(source, target):
        i = len(loads)
        copy = pltpu.make_async_copy(source, target, load_sem.at[i])
        copy.start()
        loads.append(copy)
        return copy

    sends = []

    def send(source, target, device):
        i = len(sends)
        copy = pltpu.make_async_remote_copy(
            src_ref=source,
            dst_ref=target,
            send_sem=send_sem.at[i],
            recv_sem=recv_sem.at[i],
            device_id=device,
            device_id_type=MESH,
        )
        copy.start()
        sends.append(copy)
        return copy

    def half(which):
        return pl.ds(pl.multiple_of(which * 512, 512), 512)

    def lanes(which):
        return pl.ds(pl.multiple_of(which * 128, 128), 128)

    load_k = load(k_in.at[:, lanes(core)], kv.at[0, x, ylo, half(core)])
    load_v = load(v_in.at[:, lanes(core)], kv.at[1, x, ylo, half(core)])
    load_q = load(q_in.at[:, lanes(core)], queries.at[half(core)])
    greet(
        [
            other_core,
            x_at(1),
            x_at(-1),
            z_at(1),
            z_at(-1),
            device_at(x, side, core, z),
            device_at(x, cross, core, z),
            device_at(x, step_of(y, 2), core, z),
            device_at(x, step_of(y, 2), 1 - core, z),
        ]
    )
    swap_k = send(k_in.at[:, lanes(1 - core)], kv.at[0, x, ylo, half(core)], other_core)
    swap_v = send(v_in.at[:, lanes(1 - core)], kv.at[1, x, ylo, half(core)], other_core)
    swap_q = send(q_in.at[:, lanes(1 - core)], queries.at[half(core)], other_core)

    shard = win_in.at[pl.ds(pl.multiple_of(core * 256, 256), 256)]
    win_cross = send(shard, win.at[own, core], device_at(x, cross, core, z))
    win_right = send(shard, win.at[own, core], z_at(1))
    win_left = send(shard, win.at[own, core], z_at(-1))
    load_win = [
        load(win_in.at[pl.ds(i * 256, 256)], win.at[own, i]) for i in range(2)
    ]
    load_embed = load(embed_in, embed)
    load_wout = load(wout_in, wout.at[yhi])
    load_resid = load(resid_in, resid)

    load_k.wait()
    load_v.wait()
    swap_k.wait_recv()
    swap_v.wait_recv()
    kv_side = send(kv.at[:, x, ylo], kv.at[:, x, ylo], device_at(x, side, core, z))
    kv_right = send(kv.at[:, x, ylo], kv.at[:, x, ylo], x_at(1))
    kv_left = send(kv.at[:, x, ylo], kv.at[:, x, ylo], x_at(-1))

    top[...] = jnp.full_like(top, -1e29)
    total[...] = jnp.zeros_like(total)
    mixed[...] = jnp.zeros_like(mixed)
    factor = math.log2(math.e) / math.sqrt(HS)

    def attend(xi, yi):
        base = xi * 8 + yi * 4
        lane = lax.broadcasted_iota(jnp.int32, (1, 1024), 1)
        block = jnp.where(
            lane < 512,
            jnp.where(lane < 256, block_of[base], block_of[base + 1]),
            jnp.where(lane < 768, block_of[base + 2], block_of[base + 3]),
        )
        key_pos = lane % 256 + block * 256

        def rows_of(n, carry):
            rows = pl.ds(pl.multiple_of(n * 256, 256), 256)
            pos = lax.broadcasted_iota(jnp.int32, (256, 1), 0) + block_of[x * 8 + ylo * 4 + n] * 256
            scores = rows_dot(queries[rows, :], kv[0, xi, yi])
            scores = jnp.where(pos >= key_pos, scores, -1e30)
            before = top[rows, :]
            now = jnp.maximum(before, jnp.max(scores, axis=-1, keepdims=True))
            weights = jnp.exp2((scores - now[:, :1]) * factor)
            fade = jnp.exp2((before - now) * factor)
            top[rows, :] = now
            total[rows, :] = total[rows, :] * fade + jnp.sum(weights, axis=-1, keepdims=True)
            mixed[rows, :] = mixed[rows, :] * fade + jnp.dot(
                weights.astype(jnp.bfloat16), kv[1, xi, yi], preferred_element_type=jnp.float32
            )
            return carry

        lax.fori_loop(0, 4, rows_of, 0)

    load_q.wait()
    swap_q.wait_recv()
    attend(x, ylo)

    load_embed.wait()

    def look_up(n, carry):
        rows = pl.ds(pl.multiple_of(n * 128, 128), 128)
        entry = lax.broadcasted_iota(jnp.int32, (128, 2048), 1)
        hot = (entry == earlier_code[rows, :]).astype(jnp.bfloat16)
        earlier_ref[rows, :] = jnp.dot(
            hot, embed[...], preferred_element_type=jnp.float32
        ).astype(jnp.bfloat16)
        return carry

    lax.fori_loop(0, 4, look_up, 0)

    def pass_on(ref, left_arrived, right_arrived, at, before, after, first, second):
        left_arrived.wait_recv()
        on_right = send(ref(before, first), ref(before, first), at(1))
        right_arrived.wait_recv()
        on_left = send(ref(after, second), ref(after, second), at(-1))
        return on_right, on_left

    def kv_of(yi):
        return lambda xi, part: kv.at[:, xi, yi, part]

    def win_of(up):
        return lambda zi, part: win.at[up * 4 + zi, core, part]

    kv_side.wait_recv()
    side_lo = 1 - ylo
    side_right = send(kv.at[:, x, side_lo], kv.at[:, x, side_lo], x_at(1))
    side_left = send(kv.at[:, x, side_lo], kv.at[:, x, side_lo], x_at(-1))
    win_cross.wait_recv()
    cross_right = send(win.at[crossed, core], win.at[crossed, core], z_at(1))
    cross_left = send(win.at[crossed, core], win.at[crossed, core], z_at(-1))
    wout_half = pl.ds(pl.multiple_of(core * 128, 128), 128)
    wout_cross = send(
        wout_in.at[wout_half], wout.at[yhi, wout_half], device_at(x, cross, core, z)
    )
    to_core = [send(win.at[crossed, core], win.at[crossed, core], other_core)]
    attend(x, side_lo)

    before_x, after_x = step_of(x, -1), step_of(x, 1)
    before_z, after_z = step_of(z, -1), step_of(z, 1)
    win_on = pass_on(
        win_of(yhi), win_right, win_left, z_at, before_z, after_z, pl.ds(0, 128), pl.ds(128, 128)
    )
    kv_on = pass_on(
        kv_of(ylo), kv_right, kv_left, x_at, before_x, after_x, pl.ds(0, 512), pl.ds(512, 512)
    )
    for zi in (before_z, after_z):
        to_core.append(send(win.at[yhi * 4 + zi, core], win.at[yhi * 4 + zi, core], other_core))
    attend(before_x, ylo)
    attend(after_x, ylo)
    side_on = pass_on(
        kv_of(side_lo), side_right, side_left, x_at, before_x, after_x, pl.ds(0, 512), pl.ds(512, 512)
    )
    cross_on = pass_on(
        win_of(1 - yhi), cross_right, cross_left, z_at, before_z, after_z, pl.ds(0, 128), pl.ds(128, 128)
    )
    for zi in (before_z, after_z):
        at = (1 - yhi) * 4 + zi
        to_core.append(send(win.at[at, core], win.at[at, core], other_core))
    attend(before_x, side_lo)
    attend(after_x, side_lo)
    wout_cross.wait_recv()
    wout_core = send(wout.at[1 - yhi, wout_half], wout.at[1 - yhi, wout_half], other_core)
    for one in kv_on:
        one.wait_recv()
    attend(step_of(x, 2), ylo)
    for one in win_on:
        one.wait_recv()
    at = yhi * 4 + step_of(z, 2)
    to_core.append(send(win.at[at, core], win.at[at, core], other_core))
    for one in side_on:
        one.wait_recv()
    attend(step_of(x, 2), side_lo)

    for n in range(4):
        rows = pl.ds(n * 256, 256)
        attn[n // 2, n % 2] = (mixed[rows, :] / total[rows, :]).astype(jnp.bfloat16)
    swaps = [
        send(attn.at[1 - core, yhi], heads_in.at[yhi, core], other_core),
        send(
            attn.at[core, 1 - yhi],
            heads_in.at[yhi, core],
            device_at(x, step_of(y, 2), core, z),
        ),
        send(
            attn.at[1 - core, 1 - yhi],
            heads_in.at[yhi, core],
            device_at(x, step_of(y, 2), 1 - core, z),
        ),
    ]
    heads_in[yhi, core] = attn[core, yhi]
    for one in cross_on:
        one.wait_recv()
    at = (1 - yhi) * 4 + step_of(z, 2)
    to_core.append(send(win.at[at, core], win.at[at, core], other_core))
    load_wout.wait()
    wout_core.wait_recv()
    store_wout = load(wout, wout_out)
    for one in swaps:
        one.wait_recv()

    far = {}
    near = {}
    last = {}
    for cb in range(4):
        s = 1 if cb % 2 == 0 else -1
        columns = pl.ds(cb * 1024, 1024)
        sums = jnp.zeros((256, 1024), jnp.float32)
        for up in range(2):
            left = jnp.concatenate([heads_in[up, 0], heads_in[up, 1]], axis=1)
            sums += jnp.dot(left, wout[up, :, columns], preferred_element_type=jnp.float32)
        partial[cb] = sums.astype(jnp.bfloat16).reshape(4, 64, 1024)
        far[cb] = send(partial.at[cb, step_of(z, 2)], partial_in.at[cb, 0], z_at(s))
        near[cb] = send(partial.at[cb, step_of(z, -s)], partial_in.at[cb, 1], z_at(-s))
    for cb in range(4):
        s = 1 if cb % 2 == 0 else -1
        far[cb].wait_recv()
        mid = step_of(z, s)
        partial[cb, mid] = (
            partial[cb, mid].astype(jnp.float32) + partial_in[cb, 0].astype(jnp.float32)
        ).astype(jnp.bfloat16)
        last[cb] = send(partial.at[cb, mid], partial_in.at[cb, 2], z_at(s))
    load_resid.wait()
    squares = jnp.zeros((64, 1), jnp.float32)
    for cb in range(4):
        columns = pl.ds(cb * 1024, 1024)
        near[cb].wait_recv()
        last[cb].wait_recv()
        h = partial[cb, z].astype(jnp.float32) + resid[:, columns].astype(jnp.float32)
        h = h + partial_in[cb, 1].astype(jnp.float32) + partial_in[cb, 2].astype(jnp.float32)
        hidden[:, columns] = h
        hidden_ref[:, columns] = h.astype(jnp.bfloat16)
        squares += jnp.sum(h * h, axis=-1, keepdims=True)
    rscale = lax.rsqrt(squares / D + eps)
    for cb in range(4):
        columns = pl.ds(cb * 1024, 1024)
        normed[:, columns] = (hidden[:, columns] * rscale * gain_ref[:, columns]).astype(
            jnp.bfloat16
        )
    for one in load_win:
        one.wait()
    for one in to_core:
        one.wait_recv()
    store_win = load(win, win_out)

    def enter(n, carry):
        columns = pl.ds(pl.multiple_of(n * 256, 256), 256)
        units_ref[:, columns] = jnp.dot(
            normed[...],
            win[:, :, :, columns].reshape(D, 256),
            preferred_element_type=jnp.float32,
        ).astype(jnp.bfloat16)
        return carry

    lax.fori_loop(0, 4, enter, 0)
    store_wout.wait()
    store_win.wait()
    for one in sends:
        one.wait_send()


def front(block_of, q, k, v, resid, gain, w_in, w_out, embed, earlier_code):
    bf16, f32 = jnp.bfloat16, jnp.float32
    shapes = (
        ((64, 1024), bf16),
        ((512, 1024), bf16),
        ((64, D), bf16),
        ((8, 2, 256, 1024), bf16),
        ((2, 256, D), bf16),
    )
    vmem = pl.BlockSpec(memory_space=pltpu.VMEM)
    anywhere = pl.BlockSpec(memory_space=pl.ANY)
    return pl.pallas_call(
        front_kernel,
        out_shape=tuple(jax.ShapeDtypeStruct(*one) for one in shapes),
        in_specs=[pl.BlockSpec(memory_space=pltpu.SMEM)]
        + [anywhere] * 4
        + [vmem]
        + [anywhere] * 3
        + [vmem],
        out_specs=(vmem, vmem, vmem, anywhere, anywhere),
        scratch_shapes=[
            pltpu.VMEM((2, 4, 2, 1024, HS), bf16),
            pltpu.VMEM((1024, HS), bf16),
            pltpu.VMEM((1024, HS), f32),
            pltpu.VMEM((1024, HS), f32),
            pltpu.VMEM((1024, HS), f32),
            pltpu.VMEM((2, 2, 256, HS), bf16),
            pltpu.VMEM((2, 2, 256, HS), bf16),
            pltpu.VMEM((8, 2, 256, 1024), bf16),
            pltpu.VMEM((2, 256, D), bf16),
            pltpu.VMEM((2048, 1024), bf16),
            pltpu.VMEM((64, D), bf16),
            pltpu.VMEM((4, 4, 64, 1024), bf16),
            pltpu.VMEM((4, 3, 64, 1024), bf16),
            pltpu.VMEM((64, D), f32),
            pltpu.VMEM((64, D), bf16),
            pltpu.SemaphoreType.DMA((12,)),
            pltpu.SemaphoreType.DMA((48,)),
            pltpu.SemaphoreType.DMA((48,)),
        ],
        compiler_params=pltpu.CompilerParams(
            collective_id=2, has_side_effects=True, vmem_limit_bytes=60 * 1024 * 1024
        ),
        cost_estimate=pl.CostEstimate(
            flops=9_000_000_000, bytes_accessed=40_000_000, transcendentals=8_000_000
        ),
    )(block_of, q, k, v, resid, gain, w_in, w_out, embed, earlier_code)


CB = 768
ORDER = (0, 2, 1, 3)
STEPS = 8
GROUP = 128


def lower_lanes():
    return lax.broadcasted_iota(jnp.int32, (1, 128), 1) < DHS


def split_heads(value, low):
    zero = jnp.zeros_like(value)
    return jnp.concatenate([jnp.where(low, value, zero), jnp.where(low, zero, value)], axis=0)


def join_heads(value, low):
    return jnp.where(low, value[:GROUP], value[GROUP:])


def head_sums(value, axis):
    halves = jnp.split(value, 2, axis=axis)
    return jnp.concatenate(
        [jnp.broadcast_to(jnp.sum(h, axis=axis, keepdims=True), h.shape) for h in halves], axis=axis
    )


def product(a, b):
    return jnp.dot(a, b, preferred_element_type=jnp.float32)


def back_kernel(
    units_ref,
    earlier_ref,
    code_ref,
    gain,
    hidden_in,
    wqkv_in,
    wo_in,
    whead_in,
    win_in,
    wout_in,
    d_attn_ref,
    d_wqkv_ref,
    wqkv,
    wo,
    whead,
    win,
    wide,
    ynorm,
    ynorm_t,
    stream,
    packed,
    weights,
    mixed,
    after,
    ynorm2,
    grown,
    d_units,
    d_normed,
    d_other,
    g_parts,
    core_sum,
    first_in,
    first_out,
    second_in,
    third_out,
    third_in,
    load_sem,
    send_sem,
    recv_sem,
):
    x, y, core, z = place()
    other_core = device_at(x, y, 1 - core, z)

    def x_at(by):
        return device_at(step_of(x, by), y, core, z)

    def y_at(by):
        return device_at(x, step_of(y, by), core, z)

    def z_at(by):
        return device_at(x, y, core, step_of(z, by))

    loads = []

    def load(source, target):
        copy = pltpu.make_async_copy(source, target, load_sem.at[len(loads)])
        copy.start()
        loads.append(copy)
        return copy

    sends = []

    def send(source, target, device):
        i = len(sends)
        copy = pltpu.make_async_remote_copy(
            src_ref=source,
            dst_ref=target,
            send_sem=send_sem.at[i],
            recv_sem=recv_sem.at[i],
            device_id=device,
            device_id_type=MESH,
        )
        copy.start()
        sends.append(copy)
        return copy

    load_wqkv = load(wqkv_in, wqkv)
    load_hidden = load(hidden_in, wide.at[z])
    load_wo = load(wo_in, wo)
    load_whead = load(whead_in, whead)
    load_win = load(win_in, win)

    frame_of = lax.broadcasted_iota(jnp.int32, (GROUP, 16), 0) // STEPS
    spread = (frame_of == lax.broadcasted_iota(jnp.int32, (GROUP, 16), 1)).astype(jnp.bfloat16)

    def enter(n, carry):
        rows = pl.ds(pl.multiple_of(n * GROUP, GROUP), GROUP)
        s = product(spread, units_ref[pl.ds(pl.multiple_of(n * 16, 16), 16), :])
        s = s + earlier_ref[rows, :].astype(jnp.float32)
        r = lax.rsqrt(jnp.mean(s * s, axis=-1, keepdims=True) + eps)
        stream[rows, :] = s
        ynorm[rows, :] = (s * r).astype(jnp.bfloat16)
        return carry

    lax.fori_loop(0, 4, enter, 0)
    greet([other_core] + [at(by) for at in (x_at, y_at, z_at) for by in (1, 2, 3)])
    load_hidden.wait()
    wide_right = send(wide.at[z], wide.at[z], z_at(1))
    wide_left = send(wide.at[z], wide.at[z], z_at(-1))
    load_wqkv.wait()

    def project(n, carry):
        columns = pl.ds(pl.multiple_of(n * 1024, 1024), 1024)
        packed[:, columns] = product(ynorm[...], wqkv[:, columns]).astype(jnp.bfloat16)
        return carry

    lax.fori_loop(0, 3, project, 0)

    low = lower_lanes()
    scale = 1.0 / math.sqrt(DHS)

    def seen(shape, queries):
        at_query = lax.broadcasted_iota(jnp.int32, shape, queries) % GROUP
        at_key = lax.broadcasted_iota(jnp.int32, shape, 1 - queries) % GROUP
        return jnp.logical_and(at_query // STEPS == at_key // STEPS, at_key <= at_query)

    def parts_of(rows, pair):
        at = pair * 128
        q = packed[rows, at : at + 128]
        k = split_heads(packed[rows, 1024 + at : 1024 + at + 128], low)
        v = split_heads(packed[rows, 2048 + at : 2048 + at + 128], low)
        return q, k, v

    def mix(n, carry):
        rows = pl.ds(pl.multiple_of(n * GROUP, GROUP), GROUP)
        allowed = seen((GROUP, 2 * GROUP), 0)
        for first in (0, 4):
            pairs = range(first, first + 4)
            held = [parts_of(rows, pair) for pair in pairs]
            scores = [rows_dot(q, k) for q, k, v in held]
            scores = [jnp.exp(jnp.where(allowed, s * scale, -1e30)) for s in scores]
            scores = [(s / head_sums(s, 1)).astype(jnp.bfloat16) for s in scores]
            outs = [product(a, v) for a, (q, k, v) in zip(scores, held)]
            for pair, a, out in zip(pairs, scores, outs):
                weights[pair, rows, :] = a
                mixed[rows, pair * 128 : pair * 128 + 128] = out.astype(jnp.bfloat16)
        return carry

    lax.fori_loop(0, 4, mix, 0)
    wide_right.wait_recv()
    before, beyond = step_of(z, -1), step_of(z, 1)
    top_rows, end_rows = pl.ds(0, 32), pl.ds(32, 32)
    wide_on_right = send(wide.at[before, top_rows], wide.at[before, top_rows], z_at(1))
    wide_left.wait_recv()
    wide_on_left = send(wide.at[beyond, end_rows], wide.at[beyond, end_rows], z_at(-1))
    load_wo.wait()

    def add_mixed(n, carry):
        columns = pl.ds(pl.multiple_of(n * 512, 512), 512)
        after[:, columns] = stream[:, columns] + product(mixed[...], wo[:, columns])
        return carry

    lax.fori_loop(0, 2, add_mixed, 0)

    def norm2(n, carry):
        rows = pl.ds(pl.multiple_of(n * 64, 64), 64)
        s = after[rows, :]
        r = lax.rsqrt(jnp.mean(s * s, axis=-1, keepdims=True) + eps)
        ynorm2[rows, :] = (s * r).astype(jnp.bfloat16)
        return carry

    lax.fori_loop(0, 8, norm2, 0)
    load_whead.wait()

    def grow(n, total):
        columns = pl.ds(pl.multiple_of(n * 512, 512), 512)
        e = jnp.exp(product(ynorm2[...], whead[:, columns]))
        grown[:, columns] = e.astype(jnp.bfloat16)
        return total + jnp.sum(e, axis=-1, keepdims=True)

    total = lax.fori_loop(0, 4, grow, jnp.zeros((512, 1), jnp.float32))
    inverse = 1.0 / total
    code = code_ref[...]

    def from_loss(n, carry):
        columns = pl.ds(pl.multiple_of(n * 256, 256), 256)
        entry = lax.broadcasted_iota(jnp.int32, (512, 256), 1) + n * 256
        grown[:, columns] = (
            grown[:, columns].astype(jnp.float32) * inverse - (entry == code).astype(jnp.float32)
        ).astype(jnp.bfloat16)
        return carry

    lax.fori_loop(0, 8, from_loss, 0)

    def to_ynorm2(n, carry):
        columns = pl.ds(pl.multiple_of(n * 512, 512), 512)
        ynorm2[:, columns] = rows_dot(grown[...], whead[columns, :]).astype(jnp.bfloat16)
        return carry

    lax.fori_loop(0, 2, to_ynorm2, 0)
    load_wout = [
        load(
            wout_in.at[up, :, pl.ds(part * 2048, 2048)],
            whead.at[pl.ds((up * 2 + part) * 256, 256)],
        )
        for up in range(2)
        for part in range(2)
    ]

    def to_after(n, carry):
        rows = pl.ds(pl.multiple_of(n * 64, 64), 64)
        s = after[rows, :]
        d = ynorm2[rows, :].astype(jnp.float32)
        r = lax.rsqrt(jnp.mean(s * s, axis=-1, keepdims=True) + eps)
        dot = jnp.sum(d * s, axis=-1, keepdims=True)
        da = r * d - s * (r * r * r * dot / 1024)
        after[rows, :] = da
        ynorm2[rows, :] = da.astype(jnp.bfloat16)
        return carry

    lax.fori_loop(0, 8, to_after, 0)

    def to_mixed(n, carry):
        columns = pl.ds(pl.multiple_of(n * 512, 512), 512)
        mixed[:, columns] = rows_dot(ynorm2[...], wo[columns, :]).astype(jnp.bfloat16)
        return carry

    lax.fori_loop(0, 2, to_mixed, 0)

    def unmix(n, carry):
        rows = pl.ds(pl.multiple_of(n * GROUP, GROUP), GROUP)
        allowed = seen((2 * GROUP, GROUP), 1)
        for first in (0, 4):
            pairs = range(first, first + 4)
            held = [parts_of(rows, pair) for pair in pairs]
            outs = [mixed[rows, pair * 128 : pair * 128 + 128] for pair in pairs]
            kept = [weights[pair, rows, :].astype(jnp.float32) for pair in pairs]
            turned = [rows_dot(k, q) for q, k, v in held]
            d_kept = [rows_dot(d, v) for d, (q, k, v) in zip(outs, held)]
            d_turned = [rows_dot(v, d) for d, (q, k, v) in zip(outs, held)]
            turned = [jnp.exp(jnp.where(allowed, s * scale, -1e30)) for s in turned]
            turned = [s / head_sums(s, 0) for s in turned]
            d_kept = [a * d for a, d in zip(kept, d_kept)]
            d_kept = [
                ((d - a * head_sums(d, 1)) * scale).astype(jnp.bfloat16)
                for a, d in zip(kept, d_kept)
            ]
            d_turned = [a * d for a, d in zip(turned, d_turned)]
            d_turned = [
                ((d - a * head_sums(d, 0)) * scale).astype(jnp.bfloat16)
                for a, d in zip(turned, d_turned)
            ]
            d_q = [product(d, k) for d, (q, k, v) in zip(d_kept, held)]
            d_k = [product(d, q) for d, (q, k, v) in zip(d_turned, held)]
            d_v = [product(a.astype(jnp.bfloat16), d) for a, d in zip(turned, outs)]
            for pair, dq, dk, dv in zip(pairs, d_q, d_k, d_v):
                at = pair * 128
                packed[rows, at : at + 128] = dq.astype(jnp.bfloat16)
                packed[rows, 1024 + at : 1024 + at + 128] = join_heads(dk, low).astype(jnp.bfloat16)
                packed[rows, 2048 + at : 2048 + at + 128] = join_heads(dv, low).astype(jnp.bfloat16)
        return carry

    lax.fori_loop(0, 4, unmix, 0)

    for n in range(4):
        ynorm_t[n * 256 : (n + 1) * 256, :] = ynorm[:, n * 256 : (n + 1) * 256].T

    core_sends = {}
    far = {}
    near = {}

    def axis_of(cb):
        return (x, x_at) if cb < 2 else (y, y_at)

    def sign_of(cb):
        return 1 if cb % 2 == 0 else -1

    def chunk(cb, q):
        return core_sum.at[cb, q] if cb < 2 else core_sum.at[cb, :, q]

    def first_phase(cb):
        core_sends[cb].wait_recv()
        core_sum[cb] = (
            core_sum[cb].astype(jnp.float32) + g_parts[core, cb].astype(jnp.float32)
        ).astype(jnp.bfloat16)
        p, at = axis_of(cb)
        s = sign_of(cb)
        far[cb] = send(chunk(cb, step_of(p, 2)), first_in.at[cb, 0], at(s))
        near[cb] = send(chunk(cb, step_of(p, -s)), first_in.at[cb, 1], at(-s))

    for i, cb in enumerate(ORDER):

        def block(xi, carry, cb=cb):
            rows = pl.ds(pl.multiple_of(xi * 256, 256), 256)
            term = product(ynorm_t[rows, :], packed[:, cb * CB : (cb + 1) * CB])
            term = term.astype(jnp.bfloat16)
            for ylo in range(2):
                for c in range(2):
                    for yhi in range(2):
                        at = ylo * 128 + c * 64 + yhi * 32
                        g_parts[c, cb, xi, yhi * 2 + ylo] = term[at : at + 32]
            return carry

        lax.fori_loop(0, 4, block, 0)
        core_sends[cb] = send(g_parts.at[1 - core, cb], core_sum.at[cb], other_core)
        if i > 0:
            first_phase(ORDER[i - 1])

    for n in range(2):
        columns = pl.ds(n * 512, 512)
        mixed[:, columns] = rows_dot(packed[...], wqkv[columns, :]).astype(jnp.bfloat16)
        if n == 0:
            first_phase(ORDER[3])

    def units_block(n, carry):
        rows = pl.ds(pl.multiple_of(n * 128, 128), 128)
        s = stream[rows, :]
        d = mixed[rows, :].astype(jnp.float32)
        r = lax.rsqrt(jnp.mean(s * s, axis=-1, keepdims=True) + eps)
        dot = jnp.sum(d * s, axis=-1, keepdims=True)
        ds = after[rows, :] + r * d - s * (r * r * r * dot / 1024)
        d_units[z, pl.ds(pl.multiple_of(n * 16, 16), 16), :] = jnp.sum(
            ds.reshape(16, 8, 1024), axis=1
        ).astype(jnp.bfloat16)
        return carry

    lax.fori_loop(0, 4, units_block, 0)
    units_right = send(d_units.at[z], d_units.at[z], z_at(1))
    units_left = send(d_units.at[z], d_units.at[z], z_at(-1))

    second = {}
    last = {}
    for cb in ORDER:
        p, at = axis_of(cb)
        s = sign_of(cb)
        far[cb].wait_recv()
        mid = chunk(cb, step_of(p, s))
        mid[...] = (mid[...].astype(jnp.float32) + first_in[cb, 0].astype(jnp.float32)).astype(
            jnp.bfloat16
        )
        last[cb] = send(mid, first_in.at[cb, 2], at(s))

    units_right.wait_recv()
    units_on_right = send(d_units.at[before, top_rows], d_units.at[before, top_rows], z_at(1))
    units_left.wait_recv()
    units_on_left = send(d_units.at[beyond, end_rows], d_units.at[beyond, end_rows], z_at(-1))

    for cb in ORDER:
        p, at = axis_of(cb)
        near[cb].wait_recv()
        last[cb].wait_recv()
        first_out[cb] = (
            chunk(cb, p)[...].astype(jnp.float32)
            + first_in[cb, 1].astype(jnp.float32)
            + first_in[cb, 2].astype(jnp.float32)
        ).astype(jnp.bfloat16)
        q, at = (y, y_at) if cb < 2 else (x, x_at)
        second[cb] = [
            send(first_out.at[cb, step_of(q, by)], second_in.at[cb, by - 1], at(by))
            for by in (1, 2, 3)
        ]

    units_on_right.wait_recv()
    units_on_left.wait_recv()
    load_win.wait()
    every = d_units[...].reshape(256, 1024)

    def normed_block(n, carry):
        columns = pl.ds(pl.multiple_of(n * 512, 512), 512)
        d_normed[:, columns] = rows_dot(every, win[columns, :]).astype(jnp.bfloat16)
        return carry

    lax.fori_loop(0, 8, normed_block, 0)

    for pair in range(2):
        sums = []
        for cb in (2 * pair, 2 * pair + 1):
            q = y if cb < 2 else x
            total = first_out[cb, q].astype(jnp.float32)
            for by in (1, 2, 3):
                second[cb][by - 1].wait_recv()
                total += second_in[cb, by - 1].astype(jnp.float32)
            sums.append(total)
        for zq in range(4):
            third_out[zq, pair] = jnp.concatenate(
                [one[zq * 8 : zq * 8 + 8] for one in sums], axis=0
            ).astype(jnp.bfloat16)
    third = [
        send(third_out.at[step_of(z, by)], third_in.at[by - 1], z_at(by)) for by in (1, 2, 3)
    ]

    wide_on_right.wait_recv()
    wide_on_left.wait_recv()
    wide_sends = (wide_right, wide_left, wide_on_right, wide_on_left)
    for copy in wide_sends:
        copy.wait_send()

    def hidden_block(n, carry):
        rows = pl.ds(pl.multiple_of((n % 2) * 32, 32), 32)
        h = wide[n // 2, rows, :].astype(jnp.float32)
        rscale = lax.rsqrt(jnp.mean(h * h, axis=-1, keepdims=True) + eps)
        grad_gain = (
            d_normed[pl.ds(pl.multiple_of(n * 32, 32), 32), :].astype(jnp.float32) * gain[...]
        )
        dot_rows = jnp.sum(grad_gain * h, axis=-1, keepdims=True)
        wide[n // 2, rows, :] = (
            rscale * grad_gain - h * (rscale * rscale * rscale * dot_rows / D)
        ).astype(jnp.bfloat16)
        return carry

    lax.fori_loop(0, 8, hidden_block, 0)
    for one in load_wout:
        one.wait()
    yhi = y // 2

    def attn_of(up):
        total = jnp.zeros((256, 256), jnp.float32)
        for part in range(2):
            rows = pl.ds(pl.multiple_of((up * 2 + part) * 256, 256), 256)
            total += rows_dot(
                wide[:, :, part * 2048 : (part + 1) * 2048].reshape(256, 2048), whead[rows, :]
            )
        return total.astype(jnp.bfloat16)

    d_other[0] = attn_of(1 - yhi)
    to_other = send(d_other.at[0], d_other.at[1], y_at(2))
    d_attn_ref[pl.ds(pl.multiple_of(yhi * 256, 256), 256), :] = attn_of(yhi)

    for one in third:
        one.wait_recv()
    for pair in range(2):
        total = third_out[z, pair].astype(jnp.float32)
        for by in (1, 2, 3):
            total += third_in[by - 1, pair].astype(jnp.float32)
        d_wqkv_ref[:, pair * 2 * CB : (pair * 2 + 1) * CB] = total[:8]
        d_wqkv_ref[:, (pair * 2 + 1) * CB : (pair * 2 + 2) * CB] = total[8:]

    to_other.wait_recv()
    d_attn_ref[pl.ds(pl.multiple_of((1 - yhi) * 256, 256), 256), :] = d_other[1]
    for copy in sends:
        if not any(copy is one for one in wide_sends):
            copy.wait_send()


def back(units, earlier, code, gain, hidden, w_qkv, w_o, w_head, w_in, w_out):
    bf16, f32 = jnp.bfloat16, jnp.float32
    vmem = pl.BlockSpec(memory_space=pltpu.VMEM)
    anywhere = pl.BlockSpec(memory_space=pl.ANY)
    return pl.pallas_call(
        back_kernel,
        out_shape=(
            jax.ShapeDtypeStruct((512, 256), bf16),
            jax.ShapeDtypeStruct((8, 3072), f32),
        ),
        in_specs=[vmem] * 4 + [anywhere] * 6,
        out_specs=(vmem,) * 2,
        scratch_shapes=[
            pltpu.VMEM((1024, 3072), bf16),
            pltpu.VMEM((1024, 1024), bf16),
            pltpu.VMEM((1024, 2048), bf16),
            pltpu.VMEM((D, 1024), bf16),
            pltpu.VMEM((4, 64, D), bf16),
            pltpu.VMEM((512, 1024), bf16),
            pltpu.VMEM((1024, 512), bf16),
            pltpu.VMEM((512, 1024), f32),
            pltpu.VMEM((512, 3072), bf16),
            pltpu.VMEM((8, 512, 256), bf16),
            pltpu.VMEM((512, 1024), bf16),
            pltpu.VMEM((512, 1024), f32),
            pltpu.VMEM((512, 1024), bf16),
            pltpu.VMEM((512, 2048), bf16),
            pltpu.VMEM((4, 64, 1024), bf16),
            pltpu.VMEM((256, D), bf16),
            pltpu.VMEM((2, 256, 256), bf16),
            pltpu.VMEM((2, 4, 4, 4, 32, CB), bf16),
            pltpu.VMEM((4, 4, 4, 32, CB), bf16),
            pltpu.VMEM((4, 3, 4, 32, CB), bf16),
            pltpu.VMEM((4, 4, 32, CB), bf16),
            pltpu.VMEM((4, 3, 32, CB), bf16),
            pltpu.VMEM((4, 2, 16, CB), bf16),
            pltpu.VMEM((3, 2, 16, CB), bf16),
            pltpu.SemaphoreType.DMA((9,)),
            pltpu.SemaphoreType.DMA((48,)),
            pltpu.SemaphoreType.DMA((48,)),
        ],
        compiler_params=pltpu.CompilerParams(
            collective_id=1, has_side_effects=True, vmem_limit_bytes=62 * 1024 * 1024
        ),
        cost_estimate=pl.CostEstimate(
            flops=22_000_000_000, bytes_accessed=40_000_000, transcendentals=2_000_000
        ),
    )(units, earlier, code, gain, hidden, w_qkv, w_o, w_head, w_in, w_out)


def body(
    q_heads,
    k_heads,
    v_heads,
    block_of,
    resid,
    w_out_t,
    norm_gain,
    w_in,
    embed,
    w_qkv,
    w_o,
    w_head,
    codes,
):
    gain = norm_gain.reshape(1, D)
    first = jnp.full((codes.shape[0], 1), -1, codes.dtype)
    earlier_code = jnp.concatenate([first, codes[:, :-1]], axis=1).reshape(-1, 1)
    units, earlier, hidden, win, wout = front(
        block_of, q_heads, k_heads, v_heads, resid, gain, w_in, w_out_t, embed, earlier_code
    )
    return back(
        units,
        earlier,
        codes.reshape(-1, 1),
        gain,
        hidden,
        w_qkv,
        w_o,
        w_head,
        win.reshape(D, -1),
        wout,
    )


def solution(mesh):
    in_specs = (
        P("ctx", "depth"),
        P("ctx", "depth"),
        P("ctx", "depth"),
        P(),
        P(("ctx", "depth"), None),
        P("depth", None),
        P(),
        P("depth", None),
        P(),
        P(),
        P(),
        P(),
        P(("ctx", "depth"), None),
    )
    out_specs = (P("ctx", "depth"), P(("ctx", "depth"), None))
    return jax.shard_map(body, mesh=mesh, in_specs=in_specs, out_specs=out_specs, check_vma=False)
```

```python
import math

import jax
import jax.numpy as jnp
from jax import lax
from jax.experimental import pallas as pl
from jax.experimental.pallas import tpu as pltpu
from jax.sharding import PartitionSpec as P

D = 4096
HS = 128
DHS = 64


eps = 1e-05
MESH = pl.DeviceIdType.MESH


def place():
    ctx = lax.axis_index("ctx")
    depth = lax.axis_index("depth")
    x = ctx // 4
    y = (depth // 4) * 2 + (ctx // 2) % 2
    return x, y, ctx % 2, depth % 4


def device_at(x, y, core, z):
    return (x * 4 + (y % 2) * 2 + core, (y // 2) * 4 + z)


def step_of(p, by):
    return (p + by + 4) % 4


def greet(devices):
    barrier = pltpu.get_barrier_semaphore()
    for device in devices:
        pl.semaphore_signal(barrier, inc=1, device_id=device, device_id_type=MESH)
    pl.semaphore_wait(barrier, len(devices))


def rows_dot(a, b):
    return lax.dot_general(a, b, (((1,), (1,)), ((), ())), preferred_element_type=jnp.float32)


def code_column(codes_ref, back_by):
    frame = lax.broadcasted_iota(jnp.int32, (512, 64), 0) // 8
    spread = (frame == lax.broadcasted_iota(jnp.int32, (512, 64), 1)).astype(jnp.bfloat16)
    codes = codes_ref[...]
    high = rows_dot(spread, (codes // 128).astype(jnp.float32).astype(jnp.bfloat16))
    low = rows_dot(spread, (codes % 128).astype(jnp.float32).astype(jnp.bfloat16))
    step = lax.broadcasted_iota(jnp.int32, (512, 8), 0) % 8 - back_by
    chosen = step == lax.broadcasted_iota(jnp.int32, (512, 8), 1)
    column = jnp.sum(jnp.where(chosen, high * 128 + low, 0.0), axis=1, keepdims=True)
    return jnp.where(step[:, :1] < 0, -1, column.astype(jnp.int32))


def front_kernel(
    block_of,
    q_in,
    k_in,
    v_in,
    resid_in,
    gain_ref,
    win_in,
    wout_in,
    embed_in,
    codes_ref,
    units_ref,
    earlier_ref,
    hidden_ref,
    win_out,
    wout_out,
    kv,
    other_head,
    queries,
    top,
    total,
    mixed,
    attn,
    heads_in,
    win,
    wout,
    embed,
    resid,
    partial,
    partial_in,
    entered,
    earlier_code,
    load_sem,
    send_sem,
    recv_sem,
):
    x, y, core, z = place()
    yhi = y // 2
    ylo = y % 2
    side = y + 1 - 2 * ylo
    cross = 3 - y
    own = yhi * 4 + z
    crossed = (1 - yhi) * 4 + z
    other_core = device_at(x, y, 1 - core, z)

    def x_at(by):
        return device_at(step_of(x, by), y, core, z)

    def z_at(by):
        return device_at(x, y, core, step_of(z, by))

    loads = []

    def load(source, target):
        i = len(loads)
        copy = pltpu.make_async_copy(source, target, load_sem.at[i])
        copy.start()
        loads.append(copy)
        return copy

    sends = []

    def send(source, target, device):
        i = len(sends)
        copy = pltpu.make_async_remote_copy(
            src_ref=source,
            dst_ref=target,
            send_sem=send_sem.at[i],
            recv_sem=recv_sem.at[i],
            device_id=device,
            device_id_type=MESH,
        )
        copy.start()
        sends.append(copy)
        return copy

    def half(which):
        return pl.ds(pl.multiple_of(which * 512, 512), 512)

    def lanes(which):
        return pl.ds(pl.multiple_of(which * 128, 128), 128)

    load_k = load(k_in.at[:, lanes(core)], kv.at[0, x, ylo, half(core)])
    load_v = load(v_in.at[:, lanes(core)], kv.at[1, x, ylo, half(core)])
    load_q = load(q_in.at[:, lanes(core)], queries.at[half(core)])
    load_other = [
        load(one.at[:, lanes(1 - core)], other_head.at[i]) for i, one in enumerate((k_in, v_in))
    ]
    greet(
        [
            other_core,
            x_at(1),
            x_at(-1),
            device_at(step_of(x, 1), y, 1 - core, z),
            device_at(step_of(x, -1), y, 1 - core, z),
            device_at(x, side, 1 - core, z),
            z_at(1),
            z_at(-1),
            device_at(x, side, core, z),
            device_at(x, cross, core, z),
            device_at(x, step_of(y, 2), core, z),
            device_at(x, step_of(y, 2), 1 - core, z),
        ]
    )
    for one in [load_k, load_v] + load_other:
        one.wait()
    here = kv.at[:, x, ylo, half(core)]
    swap_kv = send(other_head, here, other_core)

    def spread(xi, yi):
        return [
            send(here, here, device_at(xi, yi, core, z)),
            send(other_head, here, device_at(xi, yi, 1 - core, z)),
        ]

    kv_right = spread(step_of(x, 1), y)
    kv_left = spread(step_of(x, -1), y)
    kv_side = spread(x, side)
    swap_q = send(q_in.at[:, lanes(1 - core)], queries.at[half(core)], other_core)

    shard = win_in.at[pl.ds(pl.multiple_of(core * 256, 256), 256)]
    win_cross = send(shard, win.at[own, core], device_at(x, cross, core, z))
    win_right = send(shard, win.at[own, core], z_at(1))
    win_left = send(shard, win.at[own, core], z_at(-1))
    load_win = [
        load(win_in.at[pl.ds(i * 256, 256)], win.at[own, i]) for i in range(2)
    ]
    stores = []
    load_embed = load(embed_in, embed)
    load_wout = load(wout_in, wout.at[yhi])
    load_resid = load(resid_in, resid)

    top[...] = jnp.full_like(top, -1e29)
    total[...] = jnp.zeros_like(total)
    mixed[...] = jnp.zeros_like(mixed)
    factor = math.log2(math.e) / math.sqrt(HS)

    def attend(xi, yi):
        base = xi * 8 + yi * 4
        lane = lax.broadcasted_iota(jnp.int32, (1, 1024), 1)
        block = jnp.where(
            lane < 512,
            jnp.where(lane < 256, block_of[base], block_of[base + 1]),
            jnp.where(lane < 768, block_of[base + 2], block_of[base + 3]),
        )
        key_pos = lane % 256 + block * 256

        values = jnp.concatenate([kv[1, xi, yi], jnp.ones((1024, HS), jnp.bfloat16)], axis=1)

        def rows_of(n, carry):
            parts = [pl.ds(pl.multiple_of(n * 512 + i * 256, 256), 256) for i in range(2)]
            start = lax.broadcasted_iota(jnp.int32, (256, 1), 0)
            pos = [start + block_of[x * 8 + ylo * 4 + 2 * n + i] * 256 for i in range(2)]
            scores = [rows_dot(queries[rows, :], kv[0, xi, yi]) for rows in parts]
            scores = [jnp.where(p >= key_pos, s, -1e30) for p, s in zip(pos, scores)]
            before = [top[rows, :] for rows in parts]
            now = [
                jnp.maximum(b, jnp.max(s, axis=-1, keepdims=True)) for b, s in zip(before, scores)
            ]
            weights = [
                jnp.exp2((s - m[:, :1]) * factor).astype(jnp.bfloat16) for s, m in zip(scores, now)
            ]
            sums = [
                jnp.dot(w, values, preferred_element_type=jnp.float32) for w in weights
            ]
            for rows, b, m, s in zip(parts, before, now, sums):
                fade = jnp.exp2((b - m) * factor)
                top[rows, :] = m
                total[rows, :] = total[rows, :] * fade + s[:, HS:]
                mixed[rows, :] = mixed[rows, :] * fade + s[:, :HS]
            return carry

        lax.fori_loop(0, 2, rows_of, 0)

    load_q.wait()
    swap_q.wait_recv()
    swap_kv.wait_recv()
    attend(x, ylo)

    load_embed.wait()
    earlier_code[...] = code_column(codes_ref, 1)

    def look_up(n, carry):
        rows = pl.ds(pl.multiple_of(n * 128, 128), 128)
        entry = lax.broadcasted_iota(jnp.int32, (128, 2048), 1)
        hot = (entry == earlier_code[rows, :]).astype(jnp.bfloat16)
        earlier_ref[rows, :] = jnp.dot(
            hot, embed[...], preferred_element_type=jnp.float32
        ).astype(jnp.bfloat16)
        return carry

    lax.fori_loop(0, 4, look_up, 0)

    def pass_on(ref, left_arrived, right_arrived, at, before, after, first, second):
        for one in left_arrived:
            one.wait_recv()
        on_right = send(ref(before, first), ref(before, first), at(1))
        for one in right_arrived:
            one.wait_recv()
        on_left = send(ref(after, second), ref(after, second), at(-1))
        return on_right, on_left

    def keep(d, c):
        stores.append(load(win.at[d, c], win_out.at[d, c]))

    def kv_of(yi):
        return lambda xi, part: kv.at[:, xi, yi, part]

    def win_of(up):
        return lambda zi, part: win.at[up * 4 + zi, core, part]

    for one in load_win:
        one.wait()
    keep(own, 0)
    keep(own, 1)
    load_wout.wait()
    stores.append(load(wout.at[yhi], wout_out.at[yhi]))
    for one in kv_side:
        one.wait_recv()
    side_lo = 1 - ylo
    first_half, second_half = pl.ds(0, 512), pl.ds(512, 512)
    side_right = send(kv.at[:, x, side_lo, first_half], kv.at[:, x, side_lo, first_half], x_at(1))
    side_left = send(kv.at[:, x, side_lo, second_half], kv.at[:, x, side_lo, second_half], x_at(-1))
    win_cross.wait_recv()
    keep(crossed, core)
    cross_right = send(win.at[crossed, core], win.at[crossed, core], z_at(1))
    cross_left = send(win.at[crossed, core], win.at[crossed, core], z_at(-1))
    wout_half = pl.ds(pl.multiple_of(core * 128, 128), 128)
    wout_cross = send(
        wout_in.at[wout_half], wout.at[yhi, wout_half], device_at(x, cross, core, z)
    )
    to_core = [send(win.at[crossed, core], win.at[crossed, core], other_core)]
    attend(x, side_lo)

    before_x, after_x = step_of(x, -1), step_of(x, 1)
    before_z, after_z = step_of(z, -1), step_of(z, 1)
    win_on = pass_on(
        win_of(yhi), [win_right], [win_left], z_at, before_z, after_z, pl.ds(0, 128), pl.ds(128, 128)
    )
    kv_on = pass_on(
        kv_of(ylo), kv_right, kv_left, x_at, before_x, after_x, first_half, second_half
    )
    beside = device_at(x, side, core, z)
    kv_across = [
        send(kv.at[:, xi, ylo, part], kv.at[:, xi, ylo, part], beside)
        for xi, part in ((before_x, second_half), (after_x, first_half))
    ]
    for zi in (before_z, after_z):
        to_core.append(send(win.at[yhi * 4 + zi, core], win.at[yhi * 4 + zi, core], other_core))
        keep(yhi * 4 + zi, core)
    attend(before_x, ylo)
    attend(after_x, ylo)
    side_on = pass_on(
        kv_of(side_lo), [side_right], [side_left], x_at, before_x, after_x, first_half, second_half
    )
    cross_on = pass_on(
        win_of(1 - yhi), [cross_right], [cross_left], z_at, before_z, after_z, pl.ds(0, 128), pl.ds(128, 128)
    )
    for zi in (before_z, after_z):
        at = (1 - yhi) * 4 + zi
        to_core.append(send(win.at[at, core], win.at[at, core], other_core))
        keep(at, core)
    for one in kv_across:
        one.wait_recv()
    attend(before_x, side_lo)
    attend(after_x, side_lo)
    wout_cross.wait_recv()
    wout_core = send(wout.at[1 - yhi, wout_half], wout.at[1 - yhi, wout_half], other_core)
    stores.append(load(wout.at[1 - yhi, wout_half], wout_out.at[1 - yhi, wout_half]))
    for one in kv_on:
        one.wait_recv()
    attend(step_of(x, 2), ylo)
    for one in win_on:
        one.wait_recv()
    at = yhi * 4 + step_of(z, 2)
    to_core.append(send(win.at[at, core], win.at[at, core], other_core))
    keep(at, core)
    for one in side_on:
        one.wait_recv()
    attend(step_of(x, 2), side_lo)

    for n in range(4):
        rows = pl.ds(n * 256, 256)
        attn[n // 2, n % 2] = (mixed[rows, :] / total[rows, :]).astype(jnp.bfloat16)
    swaps = [
        send(attn.at[1 - core, yhi], heads_in.at[yhi, core], other_core),
        send(
            attn.at[core, 1 - yhi],
            heads_in.at[yhi, core],
            device_at(x, step_of(y, 2), core, z),
        ),
        send(
            attn.at[1 - core, 1 - yhi],
            heads_in.at[yhi, core],
            device_at(x, step_of(y, 2), 1 - core, z),
        ),
    ]
    heads_in[yhi, core] = attn[core, yhi]
    for one in cross_on:
        one.wait_recv()
    at = (1 - yhi) * 4 + step_of(z, 2)
    to_core.append(send(win.at[at, core], win.at[at, core], other_core))
    keep(at, core)
    wout_core.wait_recv()
    rest = pl.ds(pl.multiple_of((1 - core) * 128, 128), 128)
    stores.append(load(wout.at[1 - yhi, rest], wout_out.at[1 - yhi, rest]))
    for one in swaps:
        one.wait_recv()

    far = {}
    near = {}
    last = {}
    for cb in range(4):
        s = 1 if cb % 2 == 0 else -1
        columns = pl.ds(cb * 1024, 1024)
        sums = jnp.zeros((256, 1024), jnp.float32)
        for up in range(2):
            left = jnp.concatenate([heads_in[up, 0], heads_in[up, 1]], axis=1)
            sums += jnp.dot(left, wout[up, :, columns], preferred_element_type=jnp.float32)
        partial[cb] = sums.astype(jnp.bfloat16).reshape(4, 64, 1024)
        far[cb] = send(partial.at[cb, step_of(z, 2)], partial_in.at[cb, 0], z_at(s))
        near[cb] = send(partial.at[cb, step_of(z, -s)], partial_in.at[cb, 1], z_at(-s))
    arrived = [crossed]
    arrived += [up * 4 + zi for up in (yhi, 1 - yhi) for zi in (before_z, after_z)]
    arrived += [up * 4 + step_of(z, 2) for up in (yhi, 1 - yhi)]
    for one, d in zip(to_core, arrived):
        one.wait_recv()
        keep(d, 1 - core)
    for cb in range(4):
        s = 1 if cb % 2 == 0 else -1
        far[cb].wait_recv()
        mid = step_of(z, s)
        partial[cb, mid] = (
            partial[cb, mid].astype(jnp.float32) + partial_in[cb, 0].astype(jnp.float32)
        ).astype(jnp.bfloat16)
        last[cb] = send(partial.at[cb, mid], partial_in.at[cb, 2], z_at(s))
    load_resid.wait()
    squares = jnp.zeros((64, 1), jnp.float32)
    for cb in range(4):
        columns = pl.ds(cb * 1024, 1024)
        near[cb].wait_recv()
        last[cb].wait_recv()
        h = partial[cb, z].astype(jnp.float32) + resid[:, columns].astype(jnp.float32)
        h = h + partial_in[cb, 1].astype(jnp.float32) + partial_in[cb, 2].astype(jnp.float32)
        hidden_ref[:, columns] = h.astype(jnp.bfloat16)
        squares += jnp.sum(h * h, axis=-1, keepdims=True)
        gained = (h * gain_ref[:, columns]).astype(jnp.bfloat16)
        for n in range(2):
            some = pl.ds(n * 512, 512)
            term = jnp.dot(
                gained,
                win[2 * cb : 2 * cb + 2, :, :, some].reshape(1024, 512),
                preferred_element_type=jnp.float32,
            )
            entered[:, some] = term if cb == 0 else entered[:, some] + term
    rscale = lax.rsqrt(squares / D + eps)
    units_ref[...] = (entered[...] * rscale).astype(jnp.bfloat16)
    for one in stores:
        one.wait()
    for one in sends:
        one.wait_send()


def front(block_of, q, k, v, resid, gain, w_in, w_out, embed, codes):
    bf16, f32 = jnp.bfloat16, jnp.float32
    shapes = (
        ((64, 1024), bf16),
        ((512, 1024), bf16),
        ((64, D), bf16),
        ((8, 2, 256, 1024), bf16),
        ((2, 256, D), bf16),
    )
    vmem = pl.BlockSpec(memory_space=pltpu.VMEM)
    anywhere = pl.BlockSpec(memory_space=pl.ANY)
    return pl.pallas_call(
        front_kernel,
        out_shape=tuple(jax.ShapeDtypeStruct(*one) for one in shapes),
        in_specs=[pl.BlockSpec(memory_space=pltpu.SMEM)]
        + [anywhere] * 4
        + [vmem]
        + [anywhere] * 3
        + [vmem],
        out_specs=(vmem, vmem, vmem, anywhere, anywhere),
        scratch_shapes=[
            pltpu.VMEM((2, 4, 2, 1024, HS), bf16),
            pltpu.VMEM((2, 512, HS), bf16),
            pltpu.VMEM((1024, HS), bf16),
            pltpu.VMEM((1024, HS), f32),
            pltpu.VMEM((1024, HS), f32),
            pltpu.VMEM((1024, HS), f32),
            pltpu.VMEM((2, 2, 256, HS), bf16),
            pltpu.VMEM((2, 2, 256, HS), bf16),
            pltpu.VMEM((8, 2, 256, 1024), bf16),
            pltpu.VMEM((2, 256, D), bf16),
            pltpu.VMEM((2048, 1024), bf16),
            pltpu.VMEM((64, D), bf16),
            pltpu.VMEM((4, 4, 64, 1024), bf16),
            pltpu.VMEM((4, 3, 64, 1024), bf16),
            pltpu.VMEM((64, 1024), f32),
            pltpu.VMEM((512, 1), jnp.int32),
            pltpu.SemaphoreType.DMA((32,)),
            pltpu.SemaphoreType.DMA((56,)),
            pltpu.SemaphoreType.DMA((56,)),
        ],
        compiler_params=pltpu.CompilerParams(
            collective_id=2, has_side_effects=True, vmem_limit_bytes=60 * 1024 * 1024
        ),
        cost_estimate=pl.CostEstimate(
            flops=9_000_000_000, bytes_accessed=40_000_000, transcendentals=8_000_000
        ),
    )(block_of, q, k, v, resid, gain, w_in, w_out, embed, codes)


CB = 768
STEPS = 8
GROUP = 128


def lower_lanes():
    return lax.broadcasted_iota(jnp.int32, (1, 128), 1) < DHS


def split_heads(value, low):
    zero = jnp.zeros_like(value)
    return jnp.concatenate([jnp.where(low, value, zero), jnp.where(low, zero, value)], axis=0)


def join_heads(value, low):
    return jnp.where(low, value[:GROUP], value[GROUP:])


def head_sums(value, axis):
    halves = jnp.split(value, 2, axis=axis)
    return jnp.concatenate(
        [jnp.broadcast_to(jnp.sum(h, axis=axis, keepdims=True), h.shape) for h in halves], axis=axis
    )


def product(a, b):
    return jnp.dot(a, b, preferred_element_type=jnp.float32)


def back_kernel(
    units_ref,
    earlier_ref,
    codes_ref,
    gain,
    hidden_in,
    wqkv_in,
    wo_in,
    whead_in,
    win_in,
    wout_in,
    d_attn_ref,
    d_wqkv_ref,
    wqkv,
    wo,
    whead,
    win,
    wide,
    ynorm,
    ynorm_t,
    stream,
    packed,
    weights,
    mixed,
    after,
    ynorm2,
    grown,
    d_units,
    d_normed,
    d_other,
    g_parts,
    core_sum,
    first_in,
    first_out,
    second_in,
    third_out,
    third_in,
    sums,
    code_at,
    load_sem,
    send_sem,
    recv_sem,
):
    x, y, core, z = place()
    other_core = device_at(x, y, 1 - core, z)

    def x_at(by):
        return device_at(step_of(x, by), y, core, z)

    def y_at(by):
        return device_at(x, step_of(y, by), core, z)

    def z_at(by):
        return device_at(x, y, core, step_of(z, by))

    loads = []

    def load(source, target):
        copy = pltpu.make_async_copy(source, target, load_sem.at[len(loads)])
        copy.start()
        loads.append(copy)
        return copy

    sends = []

    def send(source, target, device):
        i = len(sends)
        copy = pltpu.make_async_remote_copy(
            src_ref=source,
            dst_ref=target,
            send_sem=send_sem.at[i],
            recv_sem=recv_sem.at[i],
            device_id=device,
            device_id_type=MESH,
        )
        copy.start()
        sends.append(copy)
        return copy

    load_hidden = load(hidden_in, wide.at[z])
    load_wqkv = [
        load(
            wqkv_in.at[pl.ds(n * 256, 256), pl.ds(part * 1024, 1024)],
            wqkv.at[pl.ds(n * 256, 256), pl.ds(part * 1024, 1024)],
        )
        for part in range(3)
        for n in range(4)
    ]

    frame_of = lax.broadcasted_iota(jnp.int32, (GROUP, 16), 0) // STEPS
    spread = (frame_of == lax.broadcasted_iota(jnp.int32, (GROUP, 16), 1)).astype(jnp.bfloat16)

    def enter(n, carry):
        rows = pl.ds(pl.multiple_of(n * GROUP, GROUP), GROUP)
        s = product(spread, units_ref[pl.ds(pl.multiple_of(n * 16, 16), 16), :])
        s = s + earlier_ref[rows, :].astype(jnp.float32)
        r = lax.rsqrt(jnp.mean(s * s, axis=-1, keepdims=True) + eps)
        stream[rows, :] = s
        ynorm[rows, :] = (s * r).astype(jnp.bfloat16)
        return carry

    lax.fori_loop(0, 4, enter, 0)
    greet([other_core] + [at(by) for at in (x_at, y_at, z_at) for by in (1, 2, 3)])
    load_hidden.wait()
    wide_right = send(wide.at[z], wide.at[z], z_at(1))
    wide_left = send(wide.at[z], wide.at[z], z_at(-1))
    code_at[...] = code_column(codes_ref, 0)
    for n in range(4):
        ynorm_t[n * 256 : (n + 1) * 256, :] = ynorm[:, n * 256 : (n + 1) * 256].T
    load_wo = load(wo_in, wo)
    load_whead = load(whead_in, whead)
    for n in range(3):
        columns = pl.ds(n * 1024, 1024)
        for one in load_wqkv[n * 4 : n * 4 + 4]:
            one.wait()
        packed[:, columns] = product(ynorm[...], wqkv[:, columns]).astype(jnp.bfloat16)
    load_win = load(win_in, win)

    low = lower_lanes()
    scale = 1.0 / math.sqrt(DHS)

    def seen(shape, queries):
        at_query = lax.broadcasted_iota(jnp.int32, shape, queries) % GROUP
        at_key = lax.broadcasted_iota(jnp.int32, shape, 1 - queries) % GROUP
        return jnp.logical_and(at_query // STEPS == at_key // STEPS, at_key <= at_query)

    def parts_of(rows, pair):
        at = pair * 128
        q = packed[rows, at : at + 128]
        k = split_heads(packed[rows, 1024 + at : 1024 + at + 128], low)
        v = split_heads(packed[rows, 2048 + at : 2048 + at + 128], low)
        return q, k, v

    def mix(n, carry):
        rows = pl.ds(pl.multiple_of(n * GROUP, GROUP), GROUP)
        allowed = seen((GROUP, 2 * GROUP), 0)
        for first in (0, 4):
            pairs = range(first, first + 4)
            held = [parts_of(rows, pair) for pair in pairs]
            scores = [rows_dot(q, k) for q, k, v in held]
            scores = [jnp.exp(jnp.where(allowed, s * scale, -1e30)) for s in scores]
            scores = [(s / head_sums(s, 1)).astype(jnp.bfloat16) for s in scores]
            outs = [product(a, v) for a, (q, k, v) in zip(scores, held)]
            for pair, a, out in zip(pairs, scores, outs):
                weights[pair, rows, :] = a
                mixed[rows, pair * 128 : pair * 128 + 128] = out.astype(jnp.bfloat16)
        return carry

    lax.fori_loop(0, 4, mix, 0)
    load_wo.wait()

    def add_mixed(n, carry):
        columns = pl.ds(pl.multiple_of(n * 512, 512), 512)
        after[:, columns] = stream[:, columns] + product(mixed[...], wo[:, columns])
        return carry

    lax.fori_loop(0, 2, add_mixed, 0)

    def norm2(n, carry):
        rows = pl.ds(pl.multiple_of(n * 64, 64), 64)
        s = after[rows, :]
        r = lax.rsqrt(jnp.mean(s * s, axis=-1, keepdims=True) + eps)
        ynorm2[rows, :] = (s * r).astype(jnp.bfloat16)
        return carry

    lax.fori_loop(0, 8, norm2, 0)
    load_whead.wait()

    def grow(n, carry):
        columns = pl.ds(pl.multiple_of(n * 512, 512), 512)
        e = jnp.exp(product(ynorm2[...], whead[:, columns]))
        grown[:, columns] = e.astype(jnp.bfloat16)
        sums[...] += e[:, :128] + e[:, 128:256] + e[:, 256:384] + e[:, 384:]
        return carry

    sums[...] = jnp.zeros_like(sums)
    lax.fori_loop(0, 4, grow, 0)

    def from_loss(n, carry):
        rows = pl.ds(pl.multiple_of(n * 64, 64), 64)
        inverse = 1.0 / jnp.sum(sums[rows, :], axis=-1, keepdims=True)
        code = code_at[rows, :]
        for part in range(4):
            columns = pl.ds(part * 512, 512)
            entry = lax.broadcasted_iota(jnp.int32, (64, 512), 1) + part * 512
            scaled = grown[rows, columns].astype(jnp.float32) * inverse
            grown[rows, columns] = jnp.where(entry == code, scaled - 1.0, scaled).astype(
                jnp.bfloat16
            )
        return carry

    lax.fori_loop(0, 8, from_loss, 0)
    wide_right.wait_recv()
    before, beyond = step_of(z, -1), step_of(z, 1)
    top_rows, end_rows = pl.ds(0, 32), pl.ds(32, 32)
    wide_on_right = send(wide.at[before, top_rows], wide.at[before, top_rows], z_at(1))
    wide_left.wait_recv()
    wide_on_left = send(wide.at[beyond, end_rows], wide.at[beyond, end_rows], z_at(-1))

    def to_ynorm2(n, carry):
        columns = pl.ds(pl.multiple_of(n * 512, 512), 512)
        ynorm2[:, columns] = rows_dot(grown[...], whead[columns, :]).astype(jnp.bfloat16)
        return carry

    lax.fori_loop(0, 2, to_ynorm2, 0)
    load_wout = [
        load(
            wout_in.at[up, :, pl.ds(part * 2048, 2048)],
            whead.at[pl.ds((up * 2 + part) * 256, 256)],
        )
        for up in range(2)
        for part in range(2)
    ]

    def to_after(n, carry):
        rows = pl.ds(pl.multiple_of(n * 64, 64), 64)
        s = after[rows, :]
        d = ynorm2[rows, :].astype(jnp.float32)
        r = lax.rsqrt(jnp.mean(s * s, axis=-1, keepdims=True) + eps)
        dot = jnp.sum(d * s, axis=-1, keepdims=True)
        da = r * d - s * (r * r * r * dot / 1024)
        after[rows, :] = da
        ynorm2[rows, :] = da.astype(jnp.bfloat16)
        return carry

    lax.fori_loop(0, 8, to_after, 0)

    def to_mixed(n, carry):
        columns = pl.ds(pl.multiple_of(n * 512, 512), 512)
        mixed[:, columns] = rows_dot(ynorm2[...], wo[columns, :]).astype(jnp.bfloat16)
        return carry

    lax.fori_loop(0, 2, to_mixed, 0)

    def unmix(n, carry):
        rows = pl.ds(pl.multiple_of(n * GROUP, GROUP), GROUP)
        allowed = seen((2 * GROUP, GROUP), 1)
        for first in (0, 4):
            pairs = range(first, first + 4)
            held = [parts_of(rows, pair) for pair in pairs]
            outs = [mixed[rows, pair * 128 : pair * 128 + 128] for pair in pairs]
            kept = [weights[pair, rows, :].astype(jnp.float32) for pair in pairs]
            turned = [rows_dot(k, q) for q, k, v in held]
            d_kept = [rows_dot(d, v) for d, (q, k, v) in zip(outs, held)]
            d_turned = [rows_dot(v, d) for d, (q, k, v) in zip(outs, held)]
            turned = [jnp.exp(jnp.where(allowed, s * scale, -1e30)) for s in turned]
            turned = [s / head_sums(s, 0) for s in turned]
            d_kept = [a * d for a, d in zip(kept, d_kept)]
            d_kept = [
                ((d - a * head_sums(d, 1)) * scale).astype(jnp.bfloat16)
                for a, d in zip(kept, d_kept)
            ]
            d_turned = [a * d for a, d in zip(turned, d_turned)]
            d_turned = [
                ((d - a * head_sums(d, 0)) * scale).astype(jnp.bfloat16)
                for a, d in zip(turned, d_turned)
            ]
            d_q = [product(d, k) for d, (q, k, v) in zip(d_kept, held)]
            d_k = [product(d, q) for d, (q, k, v) in zip(d_turned, held)]
            d_v = [product(a.astype(jnp.bfloat16), d) for a, d in zip(turned, outs)]
            for pair, dq, dk, dv in zip(pairs, d_q, d_k, d_v):
                at = pair * 128
                packed[rows, at : at + 128] = dq.astype(jnp.bfloat16)
                packed[rows, 1024 + at : 1024 + at + 128] = join_heads(dk, low).astype(jnp.bfloat16)
                packed[rows, 2048 + at : 2048 + at + 128] = join_heads(dv, low).astype(jnp.bfloat16)
        return carry

    lax.fori_loop(0, 4, unmix, 0)

    core_sends = {}
    far = {}
    near = {}

    def axis_of(cb):
        return (x, x_at) if cb < 2 else (y, y_at)

    def sign_of(cb):
        return 1 if cb % 2 == 0 else -1

    def chunk(cb, q):
        return core_sum.at[cb, q] if cb < 2 else core_sum.at[cb, :, q]

    def first_phase(cb):
        core_sends[cb].wait_recv()
        core_sum[cb] = (
            core_sum[cb].astype(jnp.float32) + g_parts[core, cb].astype(jnp.float32)
        ).astype(jnp.bfloat16)
        p, at = axis_of(cb)
        s = sign_of(cb)
        far[cb] = send(chunk(cb, step_of(p, 2)), first_in.at[cb, 0], at(s))
        near[cb] = send(chunk(cb, step_of(p, -s)), first_in.at[cb, 1], at(-s))

    def multiply(cb):
        def block(xi, carry):
            rows = pl.ds(pl.multiple_of(xi * 256, 256), 256)
            term = product(ynorm_t[rows, :], packed[:, cb * CB : (cb + 1) * CB])
            term = term.astype(jnp.bfloat16)
            for ylo in range(2):
                for c in range(2):
                    for yhi in range(2):
                        at = ylo * 128 + c * 64 + yhi * 32
                        g_parts[c, cb, xi, yhi * 2 + ylo] = term[at : at + 32]
            return carry

        lax.fori_loop(0, 4, block, 0)
        core_sends[cb] = send(g_parts.at[1 - core, cb], core_sum.at[cb], other_core)

    second = {}
    last = {}

    def second_phase(cb):
        p, at = axis_of(cb)
        s = sign_of(cb)
        far[cb].wait_recv()
        mid = chunk(cb, step_of(p, s))
        mid[...] = (mid[...].astype(jnp.float32) + first_in[cb, 0].astype(jnp.float32)).astype(
            jnp.bfloat16
        )
        last[cb] = send(mid, first_in.at[cb, 2], at(s))

    def other_axis(cb):
        p, at = axis_of(cb)
        near[cb].wait_recv()
        last[cb].wait_recv()
        first_out[cb] = (
            chunk(cb, p)[...].astype(jnp.float32)
            + first_in[cb, 1].astype(jnp.float32)
            + first_in[cb, 2].astype(jnp.float32)
        ).astype(jnp.bfloat16)
        q, at = (y, y_at) if cb < 2 else (x, x_at)
        second[cb] = [
            send(first_out.at[cb, step_of(q, by)], second_in.at[cb, by - 1], at(by))
            for by in (1, 2, 3)
        ]

    multiply(0)
    multiply(2)
    first_phase(0)
    multiply(1)
    first_phase(2)
    multiply(3)
    first_phase(1)
    mixed[:, :512] = rows_dot(packed[...], wqkv[:512, :]).astype(jnp.bfloat16)
    first_phase(3)
    mixed[:, 512:] = rows_dot(packed[...], wqkv[512:, :]).astype(jnp.bfloat16)

    def units_block(n, carry):
        rows = pl.ds(pl.multiple_of(n * 128, 128), 128)
        s = stream[rows, :]
        d = mixed[rows, :].astype(jnp.float32)
        r = lax.rsqrt(jnp.mean(s * s, axis=-1, keepdims=True) + eps)
        dot = jnp.sum(d * s, axis=-1, keepdims=True)
        ds = after[rows, :] + r * d - s * (r * r * r * dot / 1024)
        d_units[z, pl.ds(pl.multiple_of(n * 16, 16), 16), :] = jnp.sum(
            ds.reshape(16, 8, 1024), axis=1
        ).astype(jnp.bfloat16)
        return carry

    lax.fori_loop(0, 4, units_block, 0)
    units_right = send(d_units.at[z], d_units.at[z], z_at(1))
    units_left = send(d_units.at[z], d_units.at[z], z_at(-1))
    for cb in (0, 2, 1, 3):
        second_phase(cb)
    units_right.wait_recv()
    units_on_right = send(d_units.at[before, top_rows], d_units.at[before, top_rows], z_at(1))
    units_left.wait_recv()
    units_on_left = send(d_units.at[beyond, end_rows], d_units.at[beyond, end_rows], z_at(-1))
    other_axis(0)
    other_axis(2)
    other_axis(1)
    units_on_right.wait_recv()
    units_on_left.wait_recv()
    load_win.wait()
    every = d_units[...].reshape(256, 1024)

    def normed_block(n, carry):
        columns = pl.ds(pl.multiple_of(n * 512, 512), 512)
        d_normed[:, columns] = rows_dot(every, win[columns, :]).astype(jnp.bfloat16)
        return carry

    lax.fori_loop(0, 4, normed_block, 0)
    other_axis(3)
    lax.fori_loop(4, 8, normed_block, 0)

    wide_on_right.wait_recv()
    wide_on_left.wait_recv()
    wide_sends = (wide_right, wide_left, wide_on_right, wide_on_left)
    for copy in wide_sends:
        copy.wait_send()

    def hidden_block(n, carry):
        rows = pl.ds(pl.multiple_of((n % 2) * 32, 32), 32)
        h = wide[n // 2, rows, :].astype(jnp.float32)
        rscale = lax.rsqrt(jnp.mean(h * h, axis=-1, keepdims=True) + eps)
        grad_gain = (
            d_normed[pl.ds(pl.multiple_of(n * 32, 32), 32), :].astype(jnp.float32) * gain[...]
        )
        dot_rows = jnp.sum(grad_gain * h, axis=-1, keepdims=True)
        wide[n // 2, rows, :] = (
            rscale * grad_gain - h * (rscale * rscale * rscale * dot_rows / D)
        ).astype(jnp.bfloat16)
        return carry

    lax.fori_loop(0, 8, hidden_block, 0)
    for pair in range(2):
        totals = []
        for cb in (2 * pair, 2 * pair + 1):
            q = y if cb < 2 else x
            total = first_out[cb, q].astype(jnp.float32)
            for by in (1, 2, 3):
                second[cb][by - 1].wait_recv()
                total += second_in[cb, by - 1].astype(jnp.float32)
            totals.append(total)
        for zq in range(4):
            third_out[zq, pair] = jnp.concatenate(
                [one[zq * 8 : zq * 8 + 8] for one in totals], axis=0
            ).astype(jnp.bfloat16)
    third = [
        send(third_out.at[step_of(z, by)], third_in.at[by - 1], z_at(by)) for by in (1, 2, 3)
    ]
    for one in load_wout:
        one.wait()
    yhi = y // 2

    def attn_of(up):
        total = jnp.zeros((256, 256), jnp.float32)
        for part in range(2):
            rows = pl.ds(pl.multiple_of((up * 2 + part) * 256, 256), 256)
            total += rows_dot(
                wide[:, :, part * 2048 : (part + 1) * 2048].reshape(256, 2048), whead[rows, :]
            )
        return total.astype(jnp.bfloat16)

    d_other[0] = attn_of(1 - yhi)
    to_other = send(d_other.at[0], d_other.at[1], y_at(2))
    d_attn_ref[pl.ds(pl.multiple_of(yhi * 256, 256), 256), :] = attn_of(yhi)

    to_other.wait_recv()
    d_attn_ref[pl.ds(pl.multiple_of((1 - yhi) * 256, 256), 256), :] = d_other[1]
    for one in third:
        one.wait_recv()
    for pair in range(2):
        total = third_out[z, pair].astype(jnp.float32)
        for by in (1, 2, 3):
            total += third_in[by - 1, pair].astype(jnp.float32)
        d_wqkv_ref[:, pair * 2 * CB : (pair * 2 + 1) * CB] = total[:8]
        d_wqkv_ref[:, (pair * 2 + 1) * CB : (pair * 2 + 2) * CB] = total[8:]

    for copy in sends:
        if not any(copy is one for one in wide_sends):
            copy.wait_send()


def back(units, earlier, codes, gain, hidden, w_qkv, w_o, w_head, w_in, w_out):
    bf16, f32 = jnp.bfloat16, jnp.float32
    vmem = pl.BlockSpec(memory_space=pltpu.VMEM)
    anywhere = pl.BlockSpec(memory_space=pl.ANY)
    return pl.pallas_call(
        back_kernel,
        out_shape=(
            jax.ShapeDtypeStruct((512, 256), bf16),
            jax.ShapeDtypeStruct((8, 3072), f32),
        ),
        in_specs=[vmem] * 4 + [anywhere] * 6,
        out_specs=(vmem,) * 2,
        scratch_shapes=[
            pltpu.VMEM((1024, 3072), bf16),
            pltpu.VMEM((1024, 1024), bf16),
            pltpu.VMEM((1024, 2048), bf16),
            pltpu.VMEM((D, 1024), bf16),
            pltpu.VMEM((4, 64, D), bf16),
            pltpu.VMEM((512, 1024), bf16),
            pltpu.VMEM((1024, 512), bf16),
            pltpu.VMEM((512, 1024), f32),
            pltpu.VMEM((512, 3072), bf16),
            pltpu.VMEM((8, 512, 256), bf16),
            pltpu.VMEM((512, 1024), bf16),
            pltpu.VMEM((512, 1024), f32),
            pltpu.VMEM((512, 1024), bf16),
            pltpu.VMEM((512, 2048), bf16),
            pltpu.VMEM((4, 64, 1024), bf16),
            pltpu.VMEM((256, D), bf16),
            pltpu.VMEM((2, 256, 256), bf16),
            pltpu.VMEM((2, 4, 4, 4, 32, CB), bf16),
            pltpu.VMEM((4, 4, 4, 32, CB), bf16),
            pltpu.VMEM((4, 3, 4, 32, CB), bf16),
            pltpu.VMEM((4, 4, 32, CB), bf16),
            pltpu.VMEM((4, 3, 32, CB), bf16),
            pltpu.VMEM((4, 2, 16, CB), bf16),
            pltpu.VMEM((3, 2, 16, CB), bf16),
            pltpu.VMEM((512, 128), f32),
            pltpu.VMEM((512, 1), jnp.int32),
            pltpu.SemaphoreType.DMA((24,)),
            pltpu.SemaphoreType.DMA((48,)),
            pltpu.SemaphoreType.DMA((48,)),
        ],
        compiler_params=pltpu.CompilerParams(
            collective_id=1, has_side_effects=True, vmem_limit_bytes=62 * 1024 * 1024
        ),
        cost_estimate=pl.CostEstimate(
            flops=22_000_000_000, bytes_accessed=40_000_000, transcendentals=2_000_000
        ),
    )(units, earlier, codes, gain, hidden, w_qkv, w_o, w_head, w_in, w_out)


def finish_kernel(attn_in, wqkv_in, attn_out, wqkv_out):
    attn_out[...] = attn_in[...]
    wqkv_out[...] = wqkv_in[...]


def finish(d_attn, d_wqkv):
    return pl.pallas_call(
        finish_kernel,
        out_shape=tuple(jax.ShapeDtypeStruct(one.shape, one.dtype) for one in (d_attn, d_wqkv)),
        in_specs=[pl.BlockSpec(memory_space=pltpu.VMEM)] * 2,
        out_specs=(pl.BlockSpec(memory_space=pltpu.VMEM),) * 2,
    )(d_attn, d_wqkv)


def body(
    q_heads,
    k_heads,
    v_heads,
    block_of,
    resid,
    w_out_t,
    norm_gain,
    w_in,
    embed,
    w_qkv,
    w_o,
    w_head,
    codes,
):
    gain = norm_gain.reshape(1, D)
    codes = codes.T
    units, earlier, hidden, win, wout = front(
        block_of, q_heads, k_heads, v_heads, resid, gain, w_in, w_out_t, embed, codes
    )
    return finish(*back(
        units,
        earlier,
        codes,
        gain,
        hidden,
        w_qkv,
        w_o,
        w_head,
        win.reshape(D, -1),
        wout,
    ))


def solution(mesh):
    in_specs = (
        P("ctx", "depth"),
        P("ctx", "depth"),
        P("ctx", "depth"),
        P(),
        P(("ctx", "depth"), None),
        P("depth", None),
        P(),
        P("depth", None),
        P(),
        P(),
        P(),
        P(),
        P(("ctx", "depth"), None),
    )
    out_specs = (P("ctx", "depth"), P(("ctx", "depth"), None))
    return jax.shard_map(body, mesh=mesh, in_specs=in_specs, out_specs=out_specs, check_vma=False)
```

```python
import math

import jax
import jax.numpy as jnp
from jax import lax
from jax.experimental import pallas as pl
from jax.experimental.pallas import tpu as pltpu
from jax.sharding import PartitionSpec as P

D = 4096
HS = 128
DHS = 64


eps = 1e-05
MESH = pl.DeviceIdType.MESH


def place():
    ctx = lax.axis_index("ctx")
    depth = lax.axis_index("depth")
    x = ctx // 4
    y = (depth // 4) * 2 + (ctx // 2) % 2
    return x, y, ctx % 2, depth % 4


def device_at(x, y, core, z):
    return (x * 4 + (y % 2) * 2 + core, (y // 2) * 4 + z)


def step_of(p, by):
    return (p + by + 4) % 4


def greet(devices):
    barrier = pltpu.get_barrier_semaphore()
    for device in devices:
        pl.semaphore_signal(barrier, inc=1, device_id=device, device_id_type=MESH)
    pl.semaphore_wait(barrier, len(devices))


def rows_dot(a, b):
    return lax.dot_general(a, b, (((1,), (1,)), ((), ())), preferred_element_type=jnp.float32)


def code_column(codes_ref, back_by):
    frame = lax.broadcasted_iota(jnp.int32, (512, 64), 0) // 8
    spread = (frame == lax.broadcasted_iota(jnp.int32, (512, 64), 1)).astype(jnp.bfloat16)
    codes = codes_ref[...]
    high = rows_dot(spread, (codes // 128).astype(jnp.float32).astype(jnp.bfloat16))
    low = rows_dot(spread, (codes % 128).astype(jnp.float32).astype(jnp.bfloat16))
    step = lax.broadcasted_iota(jnp.int32, (512, 8), 0) % 8 - back_by
    chosen = step == lax.broadcasted_iota(jnp.int32, (512, 8), 1)
    column = jnp.sum(jnp.where(chosen, high * 128 + low, 0.0), axis=1, keepdims=True)
    return jnp.where(step[:, :1] < 0, -1, column.astype(jnp.int32))


def front_kernel(
    block_of,
    q_in,
    k_in,
    v_in,
    resid_in,
    gain_ref,
    win_in,
    wout_in,
    embed_in,
    codes_ref,
    units_ref,
    earlier_ref,
    hidden_ref,
    win_out,
    wout_out,
    kv,
    other_head,
    queries,
    top,
    total,
    mixed,
    attn,
    heads_in,
    win,
    wout,
    embed,
    resid,
    partial,
    partial_in,
    entered,
    earlier_code,
    load_sem,
    send_sem,
    recv_sem,
):
    x, y, core, z = place()
    yhi = y // 2
    ylo = y % 2
    side = y + 1 - 2 * ylo
    cross = 3 - y
    own = yhi * 4 + z
    crossed = (1 - yhi) * 4 + z
    other_core = device_at(x, y, 1 - core, z)

    def x_at(by):
        return device_at(step_of(x, by), y, core, z)

    def z_at(by):
        return device_at(x, y, core, step_of(z, by))

    loads = []

    def load(source, target):
        i = len(loads)
        copy = pltpu.make_async_copy(source, target, load_sem.at[i])
        copy.start()
        loads.append(copy)
        return copy

    sends = []

    def send(source, target, device):
        i = len(sends)
        copy = pltpu.make_async_remote_copy(
            src_ref=source,
            dst_ref=target,
            send_sem=send_sem.at[i],
            recv_sem=recv_sem.at[i],
            device_id=device,
            device_id_type=MESH,
        )
        copy.start()
        sends.append(copy)
        return copy

    def half(which):
        return pl.ds(pl.multiple_of(which * 512, 512), 512)

    def lanes(which):
        return pl.ds(pl.multiple_of(which * 128, 128), 128)

    load_k = load(k_in.at[:, lanes(core)], kv.at[0, x, ylo, half(core)])
    load_v = load(v_in.at[:, lanes(core)], kv.at[1, x, ylo, half(core)])
    load_q = load(q_in.at[:, lanes(core)], queries.at[half(core)])
    load_other = [
        load(one.at[:, lanes(1 - core)], other_head.at[i]) for i, one in enumerate((k_in, v_in))
    ]
    greet(
        [
            other_core,
            x_at(1),
            x_at(-1),
            device_at(step_of(x, 1), y, 1 - core, z),
            device_at(step_of(x, -1), y, 1 - core, z),
            device_at(x, side, 1 - core, z),
            z_at(1),
            z_at(-1),
            device_at(x, side, core, z),
            device_at(x, cross, core, z),
            device_at(x, step_of(y, 2), core, z),
            device_at(x, step_of(y, 2), 1 - core, z),
        ]
    )
    for one in [load_k, load_v] + load_other:
        one.wait()
    here = kv.at[:, x, ylo, half(core)]
    swap_kv = send(other_head, here, other_core)

    def spread(xi, yi):
        return [
            send(here, here, device_at(xi, yi, core, z)),
            send(other_head, here, device_at(xi, yi, 1 - core, z)),
        ]

    kv_right = spread(step_of(x, 1), y)
    kv_left = spread(step_of(x, -1), y)
    kv_side = spread(x, side)
    swap_q = send(q_in.at[:, lanes(1 - core)], queries.at[half(core)], other_core)

    shard = win_in.at[pl.ds(pl.multiple_of(core * 256, 256), 256)]
    win_cross = send(shard, win.at[own, core], device_at(x, cross, core, z))
    win_right = send(shard, win.at[own, core], z_at(1))
    win_left = send(shard, win.at[own, core], z_at(-1))
    load_win = [
        load(win_in.at[pl.ds(i * 256, 256)], win.at[own, i]) for i in range(2)
    ]
    stores = []
    load_embed = load(embed_in, embed)
    load_wout = load(wout_in, wout.at[yhi])
    load_resid = load(resid_in, resid)

    top[...] = jnp.full_like(top, -1e29)
    total[...] = jnp.zeros_like(total)
    mixed[...] = jnp.zeros_like(mixed)
    factor = math.log2(math.e) / math.sqrt(HS)

    def attend(xi, yi):
        base = xi * 8 + yi * 4
        lane = lax.broadcasted_iota(jnp.int32, (1, 1024), 1)
        block = jnp.where(
            lane < 512,
            jnp.where(lane < 256, block_of[base], block_of[base + 1]),
            jnp.where(lane < 768, block_of[base + 2], block_of[base + 3]),
        )
        key_pos = lane % 256 + block * 256

        values = jnp.concatenate([kv[1, xi, yi], jnp.ones((1024, HS), jnp.bfloat16)], axis=1)

        def rows_of(n, carry):
            parts = [pl.ds(pl.multiple_of(n * 512 + i * 256, 256), 256) for i in range(2)]
            start = lax.broadcasted_iota(jnp.int32, (256, 1), 0)
            pos = [start + block_of[x * 8 + ylo * 4 + 2 * n + i] * 256 for i in range(2)]
            scores = [rows_dot(queries[rows, :], kv[0, xi, yi]) for rows in parts]
            scores = [jnp.where(p >= key_pos, s, -1e30) for p, s in zip(pos, scores)]
            before = [top[rows, :] for rows in parts]
            now = [
                jnp.maximum(b, jnp.max(s, axis=-1, keepdims=True)) for b, s in zip(before, scores)
            ]
            weights = [
                jnp.exp2((s - m[:, :1]) * factor).astype(jnp.bfloat16) for s, m in zip(scores, now)
            ]
            sums = [
                jnp.dot(w, values, preferred_element_type=jnp.float32) for w in weights
            ]
            for rows, b, m, s in zip(parts, before, now, sums):
                fade = jnp.exp2((b - m) * factor)
                top[rows, :] = m
                total[rows, :] = total[rows, :] * fade + s[:, HS:]
                mixed[rows, :] = mixed[rows, :] * fade + s[:, :HS]
            return carry

        lax.fori_loop(0, 2, rows_of, 0)

    load_q.wait()
    swap_q.wait_recv()
    swap_kv.wait_recv()
    attend(x, ylo)

    load_embed.wait()
    earlier_code[...] = code_column(codes_ref, 1)

    def look_up(n, carry):
        rows = pl.ds(pl.multiple_of(n * 128, 128), 128)
        entry = lax.broadcasted_iota(jnp.int32, (128, 2048), 1)
        hot = (entry == earlier_code[rows, :]).astype(jnp.bfloat16)
        earlier_ref[rows, :] = jnp.dot(
            hot, embed[...], preferred_element_type=jnp.float32
        ).astype(jnp.bfloat16)
        return carry

    lax.fori_loop(0, 4, look_up, 0)

    def pass_on(ref, left_arrived, right_arrived, at, before, after, first, second):
        for one in left_arrived:
            one.wait_recv()
        on_right = send(ref(before, first), ref(before, first), at(1))
        for one in right_arrived:
            one.wait_recv()
        on_left = send(ref(after, second), ref(after, second), at(-1))
        return on_right, on_left

    def keep(d, c):
        stores.append(load(win.at[d, c], win_out.at[d, c]))

    def kv_of(yi):
        return lambda xi, part: kv.at[:, xi, yi, part]

    def win_of(up):
        return lambda zi, part: win.at[up * 4 + zi, core, part]

    for one in load_win:
        one.wait()
    keep(own, 0)
    keep(own, 1)
    load_wout.wait()
    stores.append(load(wout.at[yhi], wout_out.at[yhi]))
    wout_half = pl.ds(pl.multiple_of(core * 128, 128), 128)
    wout_cross = send(
        wout_in.at[wout_half], wout.at[yhi, wout_half], device_at(x, cross, core, z)
    )
    before_x, after_x, far_x = step_of(x, -1), step_of(x, 1), step_of(x, 2)
    before_z, after_z, far_z = step_of(z, -1), step_of(z, 1), step_of(z, 2)
    first_half, second_half = pl.ds(0, 512), pl.ds(512, 512)
    win_first, win_second = pl.ds(0, 128), pl.ds(128, 128)
    side_lo = 1 - ylo
    to_core = []

    def share(d):
        to_core.append(send(win.at[d, core], win.at[d, core], other_core))
        keep(d, core)

    for one in kv_side:
        one.wait_recv()
    side_right = send(kv.at[:, x, side_lo, first_half], kv.at[:, x, side_lo, first_half], x_at(1))
    side_left = send(kv.at[:, x, side_lo, second_half], kv.at[:, x, side_lo, second_half], x_at(-1))
    kv_on = pass_on(
        kv_of(ylo), kv_right, kv_left, x_at, before_x, after_x, first_half, second_half
    )
    beside = device_at(x, side, core, z)
    kv_across = [
        send(kv.at[:, xi, ylo, part], kv.at[:, xi, ylo, part], beside)
        for xi, part in ((before_x, second_half), (after_x, first_half))
    ]
    win_on = pass_on(
        win_of(yhi), [win_right], [win_left], z_at, before_z, after_z, win_first, win_second
    )
    attend(x, side_lo)
    share(yhi * 4 + before_z)
    share(yhi * 4 + after_z)
    attend(before_x, ylo)
    win_cross.wait_recv()
    cross_right = send(win.at[crossed, core], win.at[crossed, core], z_at(1))
    cross_left = send(win.at[crossed, core], win.at[crossed, core], z_at(-1))
    share(crossed)
    attend(after_x, ylo)
    side_on = pass_on(
        kv_of(side_lo), [side_right], [side_left], x_at, before_x, after_x, first_half, second_half
    )
    for one in kv_on:
        one.wait_recv()
    attend(far_x, ylo)
    for one in win_on:
        one.wait_recv()
    share(yhi * 4 + far_z)
    for one in kv_across:
        one.wait_recv()
    attend(before_x, side_lo)
    attend(after_x, side_lo)
    cross_on = pass_on(
        win_of(1 - yhi), [cross_right], [cross_left], z_at, before_z, after_z, win_first, win_second
    )
    share((1 - yhi) * 4 + before_z)
    share((1 - yhi) * 4 + after_z)
    for one in side_on:
        one.wait_recv()
    attend(far_x, side_lo)

    for n in range(4):
        rows = pl.ds(n * 256, 256)
        attn[n // 2, n % 2] = (mixed[rows, :] / total[rows, :]).astype(jnp.bfloat16)
    swaps = [
        send(attn.at[1 - core, yhi], heads_in.at[yhi, core], other_core),
        send(
            attn.at[core, 1 - yhi],
            heads_in.at[yhi, core],
            device_at(x, step_of(y, 2), core, z),
        ),
        send(
            attn.at[1 - core, 1 - yhi],
            heads_in.at[yhi, core],
            device_at(x, step_of(y, 2), 1 - core, z),
        ),
    ]
    heads_in[yhi, core] = attn[core, yhi]
    wout_cross.wait_recv()
    wout_core = send(wout.at[1 - yhi, wout_half], wout.at[1 - yhi, wout_half], other_core)
    stores.append(load(wout.at[1 - yhi, wout_half], wout_out.at[1 - yhi, wout_half]))
    wout_core.wait_recv()
    rest = pl.ds(pl.multiple_of((1 - core) * 128, 128), 128)
    stores.append(load(wout.at[1 - yhi, rest], wout_out.at[1 - yhi, rest]))
    for one in swaps:
        one.wait_recv()

    far = {}
    near = {}
    last = {}
    for cb in range(4):
        s = 1 if cb % 2 == 0 else -1
        columns = pl.ds(cb * 1024, 1024)
        sums = jnp.zeros((256, 1024), jnp.float32)
        for up in range(2):
            left = jnp.concatenate([heads_in[up, 0], heads_in[up, 1]], axis=1)
            sums += jnp.dot(left, wout[up, :, columns], preferred_element_type=jnp.float32)
        partial[cb] = sums.astype(jnp.bfloat16).reshape(4, 64, 1024)
        far[cb] = send(partial.at[cb, step_of(z, 2)], partial_in.at[cb, 0], z_at(s))
        near[cb] = send(partial.at[cb, step_of(z, -s)], partial_in.at[cb, 1], z_at(-s))
    for one in cross_on:
        one.wait_recv()
    share((1 - yhi) * 4 + far_z)
    arrived = [yhi * 4 + before_z, yhi * 4 + after_z, crossed, yhi * 4 + far_z]
    arrived += [(1 - yhi) * 4 + zi for zi in (before_z, after_z, far_z)]
    for one, d in zip(to_core, arrived):
        one.wait_recv()
        keep(d, 1 - core)
    for cb in range(4):
        s = 1 if cb % 2 == 0 else -1
        far[cb].wait_recv()
        mid = step_of(z, s)
        partial[cb, mid] = (
            partial[cb, mid].astype(jnp.float32) + partial_in[cb, 0].astype(jnp.float32)
        ).astype(jnp.bfloat16)
        last[cb] = send(partial.at[cb, mid], partial_in.at[cb, 2], z_at(s))
    load_resid.wait()
    squares = jnp.zeros((64, 1), jnp.float32)
    for cb in range(4):
        columns = pl.ds(cb * 1024, 1024)
        near[cb].wait_recv()
        last[cb].wait_recv()
        h = partial[cb, z].astype(jnp.float32) + resid[:, columns].astype(jnp.float32)
        h = h + partial_in[cb, 1].astype(jnp.float32) + partial_in[cb, 2].astype(jnp.float32)
        hidden_ref[:, columns] = h.astype(jnp.bfloat16)
        squares += jnp.sum(h * h, axis=-1, keepdims=True)
        gained = (h * gain_ref[:, columns]).astype(jnp.bfloat16)
        for n in range(2):
            some = pl.ds(n * 512, 512)
            term = jnp.dot(
                gained,
                win[2 * cb : 2 * cb + 2, :, :, some].reshape(1024, 512),
                preferred_element_type=jnp.float32,
            )
            entered[:, some] = term if cb == 0 else entered[:, some] + term
    rscale = lax.rsqrt(squares / D + eps)
    units_ref[...] = (entered[...] * rscale).astype(jnp.bfloat16)
    for one in stores:
        one.wait()
    for one in sends:
        one.wait_send()


def front(block_of, q, k, v, resid, gain, w_in, w_out, embed, codes):
    bf16, f32 = jnp.bfloat16, jnp.float32
    shapes = (
        ((64, 1024), bf16),
        ((512, 1024), bf16),
        ((64, D), bf16),
        ((8, 2, 256, 1024), bf16),
        ((2, 256, D), bf16),
    )
    vmem = pl.BlockSpec(memory_space=pltpu.VMEM)
    anywhere = pl.BlockSpec(memory_space=pl.ANY)
    return pl.pallas_call(
        front_kernel,
        out_shape=tuple(jax.ShapeDtypeStruct(*one) for one in shapes),
        in_specs=[pl.BlockSpec(memory_space=pltpu.SMEM)]
        + [anywhere] * 4
        + [vmem]
        + [anywhere] * 3
        + [vmem],
        out_specs=(vmem, vmem, vmem, anywhere, anywhere),
        scratch_shapes=[
            pltpu.VMEM((2, 4, 2, 1024, HS), bf16),
            pltpu.VMEM((2, 512, HS), bf16),
            pltpu.VMEM((1024, HS), bf16),
            pltpu.VMEM((1024, HS), f32),
            pltpu.VMEM((1024, HS), f32),
            pltpu.VMEM((1024, HS), f32),
            pltpu.VMEM((2, 2, 256, HS), bf16),
            pltpu.VMEM((2, 2, 256, HS), bf16),
            pltpu.VMEM((8, 2, 256, 1024), bf16),
            pltpu.VMEM((2, 256, D), bf16),
            pltpu.VMEM((2048, 1024), bf16),
            pltpu.VMEM((64, D), bf16),
            pltpu.VMEM((4, 4, 64, 1024), bf16),
            pltpu.VMEM((4, 3, 64, 1024), bf16),
            pltpu.VMEM((64, 1024), f32),
            pltpu.VMEM((512, 1), jnp.int32),
            pltpu.SemaphoreType.DMA((32,)),
            pltpu.SemaphoreType.DMA((56,)),
            pltpu.SemaphoreType.DMA((56,)),
        ],
        compiler_params=pltpu.CompilerParams(
            collective_id=2, has_side_effects=True, vmem_limit_bytes=60 * 1024 * 1024
        ),
        cost_estimate=pl.CostEstimate(
            flops=9_000_000_000, bytes_accessed=40_000_000, transcendentals=8_000_000
        ),
    )(block_of, q, k, v, resid, gain, w_in, w_out, embed, codes)


CB = 768
STEPS = 8
GROUP = 128


def lower_lanes():
    return lax.broadcasted_iota(jnp.int32, (1, 128), 1) < DHS


def split_heads(value, low):
    zero = jnp.zeros_like(value)
    return jnp.concatenate([jnp.where(low, value, zero), jnp.where(low, zero, value)], axis=0)


def join_heads(value, low):
    return jnp.where(low, value[:GROUP], value[GROUP:])


def head_sums(value, axis):
    halves = jnp.split(value, 2, axis=axis)
    return jnp.concatenate(
        [jnp.broadcast_to(jnp.sum(h, axis=axis, keepdims=True), h.shape) for h in halves], axis=axis
    )


def product(a, b):
    return jnp.dot(a, b, preferred_element_type=jnp.float32)


def back_kernel(
    units_ref,
    earlier_ref,
    codes_ref,
    gain,
    hidden_in,
    wqkv_in,
    wo_in,
    whead_in,
    win_in,
    wout_in,
    d_attn_ref,
    d_wqkv_ref,
    wqkv,
    wo,
    whead,
    win,
    wide,
    ynorm,
    ynorm_t,
    stream,
    packed,
    weights,
    mixed,
    after,
    ynorm2,
    grown,
    d_units,
    d_normed,
    d_other,
    g_parts,
    core_sum,
    first_in,
    first_out,
    second_in,
    third_out,
    third_in,
    sums,
    code_at,
    load_sem,
    send_sem,
    recv_sem,
):
    x, y, core, z = place()
    other_core = device_at(x, y, 1 - core, z)

    def x_at(by):
        return device_at(step_of(x, by), y, core, z)

    def y_at(by):
        return device_at(x, step_of(y, by), core, z)

    def z_at(by):
        return device_at(x, y, core, step_of(z, by))

    loads = []

    def load(source, target):
        copy = pltpu.make_async_copy(source, target, load_sem.at[len(loads)])
        copy.start()
        loads.append(copy)
        return copy

    sends = []

    def send(source, target, device):
        i = len(sends)
        copy = pltpu.make_async_remote_copy(
            src_ref=source,
            dst_ref=target,
            send_sem=send_sem.at[i],
            recv_sem=recv_sem.at[i],
            device_id=device,
            device_id_type=MESH,
        )
        copy.start()
        sends.append(copy)
        return copy

    load_hidden = load(hidden_in, wide.at[z])
    load_wqkv = [
        load(
            wqkv_in.at[pl.ds(n * 256, 256), pl.ds(part * 1024, 1024)],
            wqkv.at[pl.ds(n * 256, 256), pl.ds(part * 1024, 1024)],
        )
        for part in range(3)
        for n in range(4)
    ]

    frame_of = lax.broadcasted_iota(jnp.int32, (GROUP, 16), 0) // STEPS
    spread = (frame_of == lax.broadcasted_iota(jnp.int32, (GROUP, 16), 1)).astype(jnp.bfloat16)

    def enter(n, carry):
        rows = pl.ds(pl.multiple_of(n * GROUP, GROUP), GROUP)
        s = product(spread, units_ref[pl.ds(pl.multiple_of(n * 16, 16), 16), :])
        s = s + earlier_ref[rows, :].astype(jnp.float32)
        r = lax.rsqrt(jnp.mean(s * s, axis=-1, keepdims=True) + eps)
        stream[rows, :] = s
        ynorm[rows, :] = (s * r).astype(jnp.bfloat16)
        return carry

    lax.fori_loop(0, 4, enter, 0)
    greet([other_core] + [at(by) for at in (x_at, y_at, z_at) for by in (1, 2, 3)])
    load_hidden.wait()
    wide_right = send(wide.at[z], wide.at[z], z_at(1))
    wide_left = send(wide.at[z], wide.at[z], z_at(-1))
    code_at[...] = code_column(codes_ref, 0)
    for n in range(4):
        ynorm_t[n * 256 : (n + 1) * 256, :] = ynorm[:, n * 256 : (n + 1) * 256].T
    load_wo = load(wo_in, wo)
    load_whead = load(whead_in, whead)
    for n in range(3):
        columns = pl.ds(n * 1024, 1024)
        for one in load_wqkv[n * 4 : n * 4 + 4]:
            one.wait()
        packed[:, columns] = product(ynorm[...], wqkv[:, columns]).astype(jnp.bfloat16)
    load_win = load(win_in, win)

    low = lower_lanes()
    scale = 1.0 / math.sqrt(DHS)

    def seen(shape, queries):
        at_query = lax.broadcasted_iota(jnp.int32, shape, queries) % GROUP
        at_key = lax.broadcasted_iota(jnp.int32, shape, 1 - queries) % GROUP
        return jnp.logical_and(at_query // STEPS == at_key // STEPS, at_key <= at_query)

    def parts_of(rows, pair):
        at = pair * 128
        q = packed[rows, at : at + 128]
        k = split_heads(packed[rows, 1024 + at : 1024 + at + 128], low)
        v = split_heads(packed[rows, 2048 + at : 2048 + at + 128], low)
        return q, k, v

    def mix(n, carry):
        rows = pl.ds(pl.multiple_of(n * GROUP, GROUP), GROUP)
        allowed = seen((GROUP, 2 * GROUP), 0)
        for first in (0, 4):
            pairs = range(first, first + 4)
            held = [parts_of(rows, pair) for pair in pairs]
            scores = [rows_dot(q, k) for q, k, v in held]
            scores = [jnp.exp(jnp.where(allowed, s * scale, -1e30)) for s in scores]
            scores = [(s / head_sums(s, 1)).astype(jnp.bfloat16) for s in scores]
            outs = [product(a, v) for a, (q, k, v) in zip(scores, held)]
            for pair, a, out in zip(pairs, scores, outs):
                weights[pair, rows, :] = a
                mixed[rows, pair * 128 : pair * 128 + 128] = out.astype(jnp.bfloat16)
        return carry

    lax.fori_loop(0, 4, mix, 0)
    load_wo.wait()

    def add_mixed(n, carry):
        columns = pl.ds(pl.multiple_of(n * 512, 512), 512)
        after[:, columns] = stream[:, columns] + product(mixed[...], wo[:, columns])
        return carry

    lax.fori_loop(0, 2, add_mixed, 0)

    def norm2(n, carry):
        rows = pl.ds(pl.multiple_of(n * 64, 64), 64)
        s = after[rows, :]
        r = lax.rsqrt(jnp.mean(s * s, axis=-1, keepdims=True) + eps)
        ynorm2[rows, :] = (s * r).astype(jnp.bfloat16)
        return carry

    lax.fori_loop(0, 8, norm2, 0)
    load_whead.wait()

    def grow(n, carry):
        columns = pl.ds(pl.multiple_of(n * 512, 512), 512)
        e = jnp.exp(product(ynorm2[...], whead[:, columns]))
        grown[:, columns] = e.astype(jnp.bfloat16)
        sums[...] += e[:, :128] + e[:, 128:256] + e[:, 256:384] + e[:, 384:]
        return carry

    sums[...] = jnp.zeros_like(sums)
    lax.fori_loop(0, 4, grow, 0)

    def from_loss(n, carry):
        rows = pl.ds(pl.multiple_of(n * 64, 64), 64)
        inverse = 1.0 / jnp.sum(sums[rows, :], axis=-1, keepdims=True)
        code = code_at[rows, :]
        for part in range(4):
            columns = pl.ds(part * 512, 512)
            entry = lax.broadcasted_iota(jnp.int32, (64, 512), 1) + part * 512
            scaled = grown[rows, columns].astype(jnp.float32) * inverse
            grown[rows, columns] = jnp.where(entry == code, scaled - 1.0, scaled).astype(
                jnp.bfloat16
            )
        return carry

    lax.fori_loop(0, 8, from_loss, 0)
    wide_right.wait_recv()
    before, beyond = step_of(z, -1), step_of(z, 1)
    top_rows, end_rows = pl.ds(0, 32), pl.ds(32, 32)
    wide_on_right = send(wide.at[before, top_rows], wide.at[before, top_rows], z_at(1))
    wide_left.wait_recv()
    wide_on_left = send(wide.at[beyond, end_rows], wide.at[beyond, end_rows], z_at(-1))

    def to_ynorm2(n, carry):
        columns = pl.ds(pl.multiple_of(n * 512, 512), 512)
        ynorm2[:, columns] = rows_dot(grown[...], whead[columns, :]).astype(jnp.bfloat16)
        return carry

    lax.fori_loop(0, 2, to_ynorm2, 0)
    load_wout = [
        load(
            wout_in.at[up, :, pl.ds(part * 2048, 2048)],
            whead.at[pl.ds((up * 2 + part) * 256, 256)],
        )
        for up in range(2)
        for part in range(2)
    ]

    def to_after(n, carry):
        rows = pl.ds(pl.multiple_of(n * 64, 64), 64)
        s = after[rows, :]
        d = ynorm2[rows, :].astype(jnp.float32)
        r = lax.rsqrt(jnp.mean(s * s, axis=-1, keepdims=True) + eps)
        dot = jnp.sum(d * s, axis=-1, keepdims=True)
        da = r * d - s * (r * r * r * dot / 1024)
        after[rows, :] = da
        ynorm2[rows, :] = da.astype(jnp.bfloat16)
        return carry

    lax.fori_loop(0, 8, to_after, 0)

    def to_mixed(n, carry):
        columns = pl.ds(pl.multiple_of(n * 512, 512), 512)
        mixed[:, columns] = rows_dot(ynorm2[...], wo[columns, :]).astype(jnp.bfloat16)
        return carry

    lax.fori_loop(0, 2, to_mixed, 0)

    def unmix(n, carry):
        rows = pl.ds(pl.multiple_of(n * GROUP, GROUP), GROUP)
        allowed = seen((2 * GROUP, GROUP), 1)
        for first in (0, 4):
            pairs = range(first, first + 4)
            held = [parts_of(rows, pair) for pair in pairs]
            outs = [mixed[rows, pair * 128 : pair * 128 + 128] for pair in pairs]
            kept = [weights[pair, rows, :].astype(jnp.float32) for pair in pairs]
            turned = [rows_dot(k, q) for q, k, v in held]
            d_kept = [rows_dot(d, v) for d, (q, k, v) in zip(outs, held)]
            d_turned = [rows_dot(v, d) for d, (q, k, v) in zip(outs, held)]
            turned = [jnp.exp(jnp.where(allowed, s * scale, -1e30)) for s in turned]
            turned = [s / head_sums(s, 0) for s in turned]
            d_kept = [a * d for a, d in zip(kept, d_kept)]
            d_kept = [
                ((d - a * head_sums(d, 1)) * scale).astype(jnp.bfloat16)
                for a, d in zip(kept, d_kept)
            ]
            d_turned = [a * d for a, d in zip(turned, d_turned)]
            d_turned = [
                ((d - a * head_sums(d, 0)) * scale).astype(jnp.bfloat16)
                for a, d in zip(turned, d_turned)
            ]
            d_q = [product(d, k) for d, (q, k, v) in zip(d_kept, held)]
            d_k = [product(d, q) for d, (q, k, v) in zip(d_turned, held)]
            d_v = [product(a.astype(jnp.bfloat16), d) for a, d in zip(turned, outs)]
            for pair, dq, dk, dv in zip(pairs, d_q, d_k, d_v):
                at = pair * 128
                packed[rows, at : at + 128] = dq.astype(jnp.bfloat16)
                packed[rows, 1024 + at : 1024 + at + 128] = join_heads(dk, low).astype(jnp.bfloat16)
                packed[rows, 2048 + at : 2048 + at + 128] = join_heads(dv, low).astype(jnp.bfloat16)
        return carry

    lax.fori_loop(0, 4, unmix, 0)

    core_sends = {}
    far = {}
    near = {}

    def axis_of(cb):
        return (x, x_at) if cb < 2 else (y, y_at)

    def sign_of(cb):
        return 1 if cb % 2 == 0 else -1

    def chunk(cb, q):
        return core_sum.at[cb, q] if cb < 2 else core_sum.at[cb, :, q]

    def first_phase(cb):
        core_sends[cb].wait_recv()
        core_sum[cb] = (
            core_sum[cb].astype(jnp.float32) + g_parts[core, cb].astype(jnp.float32)
        ).astype(jnp.bfloat16)
        p, at = axis_of(cb)
        s = sign_of(cb)
        far[cb] = send(chunk(cb, step_of(p, 2)), first_in.at[cb, 0], at(s))
        near[cb] = send(chunk(cb, step_of(p, -s)), first_in.at[cb, 1], at(-s))

    def multiply(cb):
        def block(xi, carry):
            rows = pl.ds(pl.multiple_of(xi * 256, 256), 256)
            term = product(ynorm_t[rows, :], packed[:, cb * CB : (cb + 1) * CB])
            term = term.astype(jnp.bfloat16)
            for ylo in range(2):
                for c in range(2):
                    for yhi in range(2):
                        at = ylo * 128 + c * 64 + yhi * 32
                        g_parts[c, cb, xi, yhi * 2 + ylo] = term[at : at + 32]
            return carry

        lax.fori_loop(0, 4, block, 0)
        core_sends[cb] = send(g_parts.at[1 - core, cb], core_sum.at[cb], other_core)

    second = {}
    last = {}

    def second_phase(cb):
        p, at = axis_of(cb)
        s = sign_of(cb)
        far[cb].wait_recv()
        mid = chunk(cb, step_of(p, s))
        mid[...] = (mid[...].astype(jnp.float32) + first_in[cb, 0].astype(jnp.float32)).astype(
            jnp.bfloat16
        )
        last[cb] = send(mid, first_in.at[cb, 2], at(s))

    def other_axis(cb):
        p, at = axis_of(cb)
        near[cb].wait_recv()
        last[cb].wait_recv()
        first_out[cb] = (
            chunk(cb, p)[...].astype(jnp.float32)
            + first_in[cb, 1].astype(jnp.float32)
            + first_in[cb, 2].astype(jnp.float32)
        ).astype(jnp.bfloat16)
        q, at = (y, y_at) if cb < 2 else (x, x_at)
        second[cb] = [
            send(first_out.at[cb, step_of(q, by)], second_in.at[cb, by - 1], at(by))
            for by in (1, 2, 3)
        ]

    multiply(0)
    multiply(2)
    first_phase(0)
    multiply(1)
    first_phase(2)
    multiply(3)
    first_phase(1)
    mixed[:, :512] = rows_dot(packed[...], wqkv[:512, :]).astype(jnp.bfloat16)
    first_phase(3)
    mixed[:, 512:] = rows_dot(packed[...], wqkv[512:, :]).astype(jnp.bfloat16)

    def units_block(n, carry):
        rows = pl.ds(pl.multiple_of(n * 128, 128), 128)
        s = stream[rows, :]
        d = mixed[rows, :].astype(jnp.float32)
        r = lax.rsqrt(jnp.mean(s * s, axis=-1, keepdims=True) + eps)
        dot = jnp.sum(d * s, axis=-1, keepdims=True)
        ds = after[rows, :] + r * d - s * (r * r * r * dot / 1024)
        d_units[z, pl.ds(pl.multiple_of(n * 16, 16), 16), :] = jnp.sum(
            ds.reshape(16, 8, 1024), axis=1
        ).astype(jnp.bfloat16)
        return carry

    lax.fori_loop(0, 4, units_block, 0)
    units_right = send(d_units.at[z], d_units.at[z], z_at(1))
    units_left = send(d_units.at[z], d_units.at[z], z_at(-1))
    for cb in (0, 2, 1, 3):
        second_phase(cb)
    units_right.wait_recv()
    units_on_right = send(d_units.at[before, top_rows], d_units.at[before, top_rows], z_at(1))
    units_left.wait_recv()
    units_on_left = send(d_units.at[beyond, end_rows], d_units.at[beyond, end_rows], z_at(-1))
    other_axis(0)
    other_axis(2)
    other_axis(1)
    units_on_right.wait_recv()
    units_on_left.wait_recv()
    load_win.wait()
    every = d_units[...].reshape(256, 1024)

    def normed_block(n, carry):
        columns = pl.ds(pl.multiple_of(n * 512, 512), 512)
        d_normed[:, columns] = rows_dot(every, win[columns, :]).astype(jnp.bfloat16)
        return carry

    lax.fori_loop(0, 4, normed_block, 0)
    other_axis(3)
    lax.fori_loop(4, 8, normed_block, 0)

    wide_on_right.wait_recv()
    wide_on_left.wait_recv()
    wide_sends = (wide_right, wide_left, wide_on_right, wide_on_left)
    for copy in wide_sends:
        copy.wait_send()

    def hidden_block(n, carry):
        rows = pl.ds(pl.multiple_of((n % 2) * 32, 32), 32)
        h = wide[n // 2, rows, :].astype(jnp.float32)
        rscale = lax.rsqrt(jnp.mean(h * h, axis=-1, keepdims=True) + eps)
        grad_gain = (
            d_normed[pl.ds(pl.multiple_of(n * 32, 32), 32), :].astype(jnp.float32) * gain[...]
        )
        dot_rows = jnp.sum(grad_gain * h, axis=-1, keepdims=True)
        wide[n // 2, rows, :] = (
            rscale * grad_gain - h * (rscale * rscale * rscale * dot_rows / D)
        ).astype(jnp.bfloat16)
        return carry

    lax.fori_loop(0, 8, hidden_block, 0)
    for one in load_wout:
        one.wait()
    yhi = y // 2

    def attn_of(up):
        total = jnp.zeros((256, 256), jnp.float32)
        for part in range(2):
            rows = pl.ds(pl.multiple_of((up * 2 + part) * 256, 256), 256)
            total += rows_dot(
                wide[:, :, part * 2048 : (part + 1) * 2048].reshape(256, 2048), whead[rows, :]
            )
        return total.astype(jnp.bfloat16)

    d_other[0] = attn_of(1 - yhi)
    to_other = send(d_other.at[0], d_other.at[1], y_at(2))
    for pair in range(2):
        totals = []
        for cb in (2 * pair, 2 * pair + 1):
            q = y if cb < 2 else x
            total = first_out[cb, q].astype(jnp.float32)
            for by in (1, 2, 3):
                second[cb][by - 1].wait_recv()
                total += second_in[cb, by - 1].astype(jnp.float32)
            totals.append(total)
        for zq in range(4):
            third_out[zq, pair] = jnp.concatenate(
                [one[zq * 8 : zq * 8 + 8] for one in totals], axis=0
            ).astype(jnp.bfloat16)
    third = [
        send(third_out.at[step_of(z, by)], third_in.at[by - 1], z_at(by)) for by in (1, 2, 3)
    ]
    d_attn_ref[pl.ds(pl.multiple_of(yhi * 256, 256), 256), :] = attn_of(yhi)

    to_other.wait_recv()
    d_attn_ref[pl.ds(pl.multiple_of((1 - yhi) * 256, 256), 256), :] = d_other[1]
    for one in third:
        one.wait_recv()
    for pair in range(2):
        total = third_out[z, pair].astype(jnp.float32)
        for by in (1, 2, 3):
            total += third_in[by - 1, pair].astype(jnp.float32)
        d_wqkv_ref[:, pair * 2 * CB : (pair * 2 + 1) * CB] = total[:8]
        d_wqkv_ref[:, (pair * 2 + 1) * CB : (pair * 2 + 2) * CB] = total[8:]

    for copy in sends:
        if not any(copy is one for one in wide_sends):
            copy.wait_send()


def back(units, earlier, codes, gain, hidden, w_qkv, w_o, w_head, w_in, w_out):
    bf16, f32 = jnp.bfloat16, jnp.float32
    vmem = pl.BlockSpec(memory_space=pltpu.VMEM)
    anywhere = pl.BlockSpec(memory_space=pl.ANY)
    return pl.pallas_call(
        back_kernel,
        out_shape=(
            jax.ShapeDtypeStruct((512, 256), bf16),
            jax.ShapeDtypeStruct((8, 3072), f32),
        ),
        in_specs=[vmem] * 4 + [anywhere] * 6,
        out_specs=(vmem,) * 2,
        scratch_shapes=[
            pltpu.VMEM((1024, 3072), bf16),
            pltpu.VMEM((1024, 1024), bf16),
            pltpu.VMEM((1024, 2048), bf16),
            pltpu.VMEM((D, 1024), bf16),
            pltpu.VMEM((4, 64, D), bf16),
            pltpu.VMEM((512, 1024), bf16),
            pltpu.VMEM((1024, 512), bf16),
            pltpu.VMEM((512, 1024), f32),
            pltpu.VMEM((512, 3072), bf16),
            pltpu.VMEM((8, 512, 256), bf16),
            pltpu.VMEM((512, 1024), bf16),
            pltpu.VMEM((512, 1024), f32),
            pltpu.VMEM((512, 1024), bf16),
            pltpu.VMEM((512, 2048), bf16),
            pltpu.VMEM((4, 64, 1024), bf16),
            pltpu.VMEM((256, D), bf16),
            pltpu.VMEM((2, 256, 256), bf16),
            pltpu.VMEM((2, 4, 4, 4, 32, CB), bf16),
            pltpu.VMEM((4, 4, 4, 32, CB), bf16),
            pltpu.VMEM((4, 3, 4, 32, CB), bf16),
            pltpu.VMEM((4, 4, 32, CB), bf16),
            pltpu.VMEM((4, 3, 32, CB), bf16),
            pltpu.VMEM((4, 2, 16, CB), bf16),
            pltpu.VMEM((3, 2, 16, CB), bf16),
            pltpu.VMEM((512, 128), f32),
            pltpu.VMEM((512, 1), jnp.int32),
            pltpu.SemaphoreType.DMA((24,)),
            pltpu.SemaphoreType.DMA((48,)),
            pltpu.SemaphoreType.DMA((48,)),
        ],
        compiler_params=pltpu.CompilerParams(
            collective_id=1, has_side_effects=True, vmem_limit_bytes=62 * 1024 * 1024
        ),
        cost_estimate=pl.CostEstimate(
            flops=22_000_000_000, bytes_accessed=40_000_000, transcendentals=2_000_000
        ),
    )(units, earlier, codes, gain, hidden, w_qkv, w_o, w_head, w_in, w_out)


def finish_kernel(attn_in, wqkv_in, attn_out, wqkv_out):
    attn_out[...] = attn_in[...]
    wqkv_out[...] = wqkv_in[...]


def finish(d_attn, d_wqkv):
    return pl.pallas_call(
        finish_kernel,
        out_shape=tuple(jax.ShapeDtypeStruct(one.shape, one.dtype) for one in (d_attn, d_wqkv)),
        in_specs=[pl.BlockSpec(memory_space=pltpu.VMEM)] * 2,
        out_specs=(pl.BlockSpec(memory_space=pltpu.VMEM),) * 2,
    )(d_attn, d_wqkv)


def body(
    q_heads,
    k_heads,
    v_heads,
    block_of,
    resid,
    w_out_t,
    norm_gain,
    w_in,
    embed,
    w_qkv,
    w_o,
    w_head,
    codes,
):
    gain = norm_gain.reshape(1, D)
    codes = codes.T
    units, earlier, hidden, win, wout = front(
        block_of, q_heads, k_heads, v_heads, resid, gain, w_in, w_out_t, embed, codes
    )
    return finish(*back(
        units,
        earlier,
        codes,
        gain,
        hidden,
        w_qkv,
        w_o,
        w_head,
        win.reshape(D, -1),
        wout,
    ))


def solution(mesh):
    in_specs = (
        P("ctx", "depth"),
        P("ctx", "depth"),
        P("ctx", "depth"),
        P(),
        P(("ctx", "depth"), None),
        P("depth", None),
        P(),
        P("depth", None),
        P(),
        P(),
        P(),
        P(),
        P(("ctx", "depth"), None),
    )
    out_specs = (P("ctx", "depth"), P(("ctx", "depth"), None))
    return jax.shard_map(body, mesh=mesh, in_specs=in_specs, out_specs=out_specs, check_vma=False)
```

```python
import functools
import math

import jax
import jax.numpy as jnp
from jax import lax
from jax.experimental import pallas as pl
from jax.experimental.pallas import tpu as pltpu
from jax.sharding import PartitionSpec as P

D = 4096
HS = 128
DHS = 64


eps = 1e-05
MESH = pl.DeviceIdType.MESH


def place():
    ctx = lax.axis_index("ctx")
    depth = lax.axis_index("depth")
    x = ctx // 4
    y = (depth // 4) * 2 + (ctx // 2) % 2
    return x, y, ctx % 2, depth % 4


def device_at(x, y, core, z):
    return (x * 4 + (y % 2) * 2 + core, (y // 2) * 4 + z)


def step_of(p, by):
    return (p + by + 4) % 4


def greet(devices):
    barrier = pltpu.get_barrier_semaphore()
    for device in devices:
        pl.semaphore_signal(barrier, inc=1, device_id=device, device_id_type=MESH)
    pl.semaphore_wait(barrier, len(devices))


def rows_dot(a, b):
    return lax.dot_general(a, b, (((1,), (1,)), ((), ())), preferred_element_type=jnp.float32)


def code_column(codes_ref, back_by):
    frame = lax.broadcasted_iota(jnp.int32, (512, 64), 0) // 8
    spread = (frame == lax.broadcasted_iota(jnp.int32, (512, 64), 1)).astype(jnp.bfloat16)
    codes = codes_ref[...]
    high = rows_dot(spread, (codes // 128).astype(jnp.float32).astype(jnp.bfloat16))
    low = rows_dot(spread, (codes % 128).astype(jnp.float32).astype(jnp.bfloat16))
    step = lax.broadcasted_iota(jnp.int32, (512, 8), 0) % 8 - back_by
    chosen = step == lax.broadcasted_iota(jnp.int32, (512, 8), 1)
    column = jnp.sum(jnp.where(chosen, high * 128 + low, 0.0), axis=1, keepdims=True)
    return jnp.where(step[:, :1] < 0, -1, column.astype(jnp.int32))


def front_kernel(
    block_of,
    q_in,
    k_in,
    v_in,
    resid_in,
    gain_ref,
    win_in,
    wout_in,
    embed_in,
    codes_ref,
    units_ref,
    earlier_ref,
    hidden_ref,
    win_out,
    wout_out,
    kv,
    other_head,
    queries,
    top,
    total,
    mixed,
    attn,
    heads_in,
    win,
    wout,
    embed,
    resid,
    partial,
    partial_in,
    entered,
    earlier_code,
    load_sem,
    send_sem,
    recv_sem,
):
    x, y, core, z = place()
    yhi = y // 2
    ylo = y % 2
    side = y + 1 - 2 * ylo
    cross = 3 - y
    own = yhi * 4 + z
    crossed = (1 - yhi) * 4 + z
    other_core = device_at(x, y, 1 - core, z)

    def x_at(by):
        return device_at(step_of(x, by), y, core, z)

    def z_at(by):
        return device_at(x, y, core, step_of(z, by))

    loads = []

    def load(source, target):
        i = len(loads)
        copy = pltpu.make_async_copy(source, target, load_sem.at[i])
        copy.start()
        loads.append(copy)
        return copy

    sends = []

    def send(source, target, device):
        i = len(sends)
        copy = pltpu.make_async_remote_copy(
            src_ref=source,
            dst_ref=target,
            send_sem=send_sem.at[i],
            recv_sem=recv_sem.at[i],
            device_id=device,
            device_id_type=MESH,
        )
        copy.start()
        sends.append(copy)
        return copy

    def half(which):
        return pl.ds(pl.multiple_of(which * 512, 512), 512)

    def lanes(which):
        return pl.ds(pl.multiple_of(which * 128, 128), 128)

    load_k = load(k_in.at[:, lanes(core)], kv.at[0, x, ylo, half(core)])
    load_v = load(v_in.at[:, lanes(core)], kv.at[1, x, ylo, half(core)])
    load_q = load(q_in.at[:, lanes(core)], queries.at[half(core)])
    load_other = [
        load(one.at[:, lanes(1 - core)], other_head.at[i]) for i, one in enumerate((k_in, v_in))
    ]
    greet(
        [
            other_core,
            x_at(1),
            x_at(-1),
            device_at(step_of(x, 1), y, 1 - core, z),
            device_at(step_of(x, -1), y, 1 - core, z),
            device_at(x, side, 1 - core, z),
            z_at(1),
            z_at(-1),
            device_at(x, side, core, z),
            device_at(x, cross, core, z),
            device_at(x, step_of(y, 2), core, z),
            device_at(x, step_of(y, 2), 1 - core, z),
        ]
    )
    for one in [load_k, load_v] + load_other:
        one.wait()
    here = kv.at[:, x, ylo, half(core)]
    swap_kv = send(other_head, here, other_core)

    def spread(xi, yi):
        return [
            send(here, here, device_at(xi, yi, core, z)),
            send(other_head, here, device_at(xi, yi, 1 - core, z)),
        ]

    kv_right = spread(step_of(x, 1), y)
    kv_left = spread(step_of(x, -1), y)
    kv_side = spread(x, side)
    swap_q = send(q_in.at[:, lanes(1 - core)], queries.at[half(core)], other_core)

    shard = win_in.at[pl.ds(pl.multiple_of(core * 256, 256), 256)]
    win_cross = send(shard, win.at[own, core], device_at(x, cross, core, z))
    win_right = send(shard, win.at[own, core], z_at(1))
    win_left = send(shard, win.at[own, core], z_at(-1))
    load_win = [
        load(win_in.at[pl.ds(i * 256, 256)], win.at[own, i]) for i in range(2)
    ]
    load_embed = load(embed_in, embed)
    load_wout = load(wout_in, wout.at[yhi])
    load_resid = load(resid_in, resid)

    top[...] = jnp.full_like(top, -1e29)
    total[...] = jnp.zeros_like(total)
    mixed[...] = jnp.zeros_like(mixed)
    factor = math.log2(math.e) / math.sqrt(HS)

    def attend(xi, yi):
        base = xi * 8 + yi * 4
        lane = lax.broadcasted_iota(jnp.int32, (1, 1024), 1)
        block = jnp.where(
            lane < 512,
            jnp.where(lane < 256, block_of[base], block_of[base + 1]),
            jnp.where(lane < 768, block_of[base + 2], block_of[base + 3]),
        )
        key_pos = lane % 256 + block * 256

        values = jnp.concatenate([kv[1, xi, yi], jnp.ones((1024, HS), jnp.bfloat16)], axis=1)

        def rows_of(n, carry):
            parts = [pl.ds(pl.multiple_of(n * 512 + i * 256, 256), 256) for i in range(2)]
            start = lax.broadcasted_iota(jnp.int32, (256, 1), 0)
            pos = [start + block_of[x * 8 + ylo * 4 + 2 * n + i] * 256 for i in range(2)]
            scores = [rows_dot(queries[rows, :], kv[0, xi, yi]) for rows in parts]
            scores = [jnp.where(p >= key_pos, s, -1e30) for p, s in zip(pos, scores)]
            before = [top[rows, :] for rows in parts]
            now = [
                jnp.maximum(b, jnp.max(s, axis=-1, keepdims=True)) for b, s in zip(before, scores)
            ]
            weights = [
                jnp.exp2((s - m[:, :1]) * factor).astype(jnp.bfloat16) for s, m in zip(scores, now)
            ]
            sums = [
                jnp.dot(w, values, preferred_element_type=jnp.float32) for w in weights
            ]
            for rows, b, m, s in zip(parts, before, now, sums):
                fade = jnp.exp2((b - m) * factor)
                top[rows, :] = m
                total[rows, :] = total[rows, :] * fade + s[:, HS:]
                mixed[rows, :] = mixed[rows, :] * fade + s[:, :HS]
            return carry

        lax.fori_loop(0, 2, rows_of, 0)

    load_q.wait()
    swap_q.wait_recv()
    swap_kv.wait_recv()
    attend(x, ylo)

    load_embed.wait()
    earlier_code[...] = code_column(codes_ref, 1)

    def look_up(n, carry):
        rows = pl.ds(pl.multiple_of(n * 128, 128), 128)
        entry = lax.broadcasted_iota(jnp.int32, (128, 2048), 1)
        hot = (entry == earlier_code[rows, :]).astype(jnp.bfloat16)
        earlier_ref[rows, :] = jnp.dot(
            hot, embed[...], preferred_element_type=jnp.float32
        ).astype(jnp.bfloat16)
        return carry

    lax.fori_loop(0, 4, look_up, 0)
    stores = []

    def pass_on(ref, left_arrived, right_arrived, at, before, after, first, second):
        for one in left_arrived:
            one.wait_recv()
        on_right = send(ref(before, first), ref(before, first), at(1))
        for one in right_arrived:
            one.wait_recv()
        on_left = send(ref(after, second), ref(after, second), at(-1))
        return on_right, on_left

    def keep(d, c):
        stores.append(load(win.at[d, c], win_out.at[d, c]))

    def kv_of(yi):
        return lambda xi, part: kv.at[:, xi, yi, part]

    def win_of(up):
        return lambda zi, part: win.at[up * 4 + zi, core, part]

    for one in load_win:
        one.wait()
    keep(own, 0)
    keep(own, 1)
    load_wout.wait()
    stores.append(load(wout.at[yhi], wout_out.at[yhi]))
    wout_half = pl.ds(pl.multiple_of(core * 128, 128), 128)
    wout_cross = send(
        wout_in.at[wout_half], wout.at[yhi, wout_half], device_at(x, cross, core, z)
    )
    before_x, after_x, far_x = step_of(x, -1), step_of(x, 1), step_of(x, 2)
    before_z, after_z, far_z = step_of(z, -1), step_of(z, 1), step_of(z, 2)
    first_half, second_half = pl.ds(0, 512), pl.ds(512, 512)
    win_first, win_second = pl.ds(0, 128), pl.ds(128, 128)
    side_lo = 1 - ylo
    to_core = []

    def share(d):
        to_core.append(send(win.at[d, core], win.at[d, core], other_core))
        keep(d, core)

    for one in kv_side:
        one.wait_recv()
    side_right = send(kv.at[:, x, side_lo, first_half], kv.at[:, x, side_lo, first_half], x_at(1))
    side_left = send(kv.at[:, x, side_lo, second_half], kv.at[:, x, side_lo, second_half], x_at(-1))
    for one in kv_right + kv_left:
        one.wait_recv()
    beside = device_at(x, side, core, z)
    kv_across = [
        send(kv.at[:, xi, ylo, part], kv.at[:, xi, ylo, part], beside)
        for xi, part in ((before_x, second_half), (after_x, first_half))
    ]
    win_on = pass_on(
        win_of(yhi), [win_right], [win_left], z_at, before_z, after_z, win_first, win_second
    )
    attend(x, side_lo)
    kv_on = pass_on(kv_of(ylo), [], [], x_at, before_x, after_x, first_half, second_half)
    share(yhi * 4 + before_z)
    share(yhi * 4 + after_z)
    attend(before_x, ylo)
    win_cross.wait_recv()
    cross_right = send(win.at[crossed, core], win.at[crossed, core], z_at(1))
    cross_left = send(win.at[crossed, core], win.at[crossed, core], z_at(-1))
    share(crossed)
    attend(after_x, ylo)
    side_on = pass_on(
        kv_of(side_lo), [side_right], [side_left], x_at, before_x, after_x, first_half, second_half
    )
    for one in kv_on:
        one.wait_recv()
    attend(far_x, ylo)
    for one in win_on:
        one.wait_recv()
    share(yhi * 4 + far_z)
    for one in kv_across:
        one.wait_recv()
    attend(before_x, side_lo)
    attend(after_x, side_lo)
    cross_on = pass_on(
        win_of(1 - yhi), [cross_right], [cross_left], z_at, before_z, after_z, win_first, win_second
    )
    share((1 - yhi) * 4 + before_z)
    share((1 - yhi) * 4 + after_z)
    for one in side_on:
        one.wait_recv()
    attend(far_x, side_lo)

    for n in range(4):
        rows = pl.ds(n * 256, 256)
        attn[n // 2, n % 2] = (mixed[rows, :] / total[rows, :]).astype(jnp.bfloat16)
    swaps = [
        send(attn.at[1 - core, yhi], heads_in.at[yhi, core], other_core),
        send(
            attn.at[core, 1 - yhi],
            heads_in.at[yhi, core],
            device_at(x, step_of(y, 2), core, z),
        ),
        send(
            attn.at[1 - core, 1 - yhi],
            heads_in.at[yhi, core],
            device_at(x, step_of(y, 2), 1 - core, z),
        ),
    ]
    heads_in[yhi, core] = attn[core, yhi]
    wout_cross.wait_recv()
    wout_core = send(wout.at[1 - yhi, wout_half], wout.at[1 - yhi, wout_half], other_core)
    stores.append(load(wout.at[1 - yhi, wout_half], wout_out.at[1 - yhi, wout_half]))
    wout_core.wait_recv()
    rest = pl.ds(pl.multiple_of((1 - core) * 128, 128), 128)
    stores.append(load(wout.at[1 - yhi, rest], wout_out.at[1 - yhi, rest]))
    for one in swaps:
        one.wait_recv()

    far = {}
    near = {}
    last = {}
    for cb in range(4):
        s = 1 if cb % 2 == 0 else -1
        columns = pl.ds(cb * 1024, 1024)
        sums = jnp.zeros((256, 1024), jnp.float32)
        for up in range(2):
            left = jnp.concatenate([heads_in[up, 0], heads_in[up, 1]], axis=1)
            sums += jnp.dot(left, wout[up, :, columns], preferred_element_type=jnp.float32)
        partial[cb] = sums.astype(jnp.bfloat16).reshape(4, 64, 1024)
        far[cb] = send(partial.at[cb, step_of(z, 2)], partial_in.at[cb, 0], z_at(s))
        near[cb] = send(partial.at[cb, step_of(z, -s)], partial_in.at[cb, 1], z_at(-s))
    for one in cross_on:
        one.wait_recv()
    share((1 - yhi) * 4 + far_z)
    arrived = [yhi * 4 + before_z, yhi * 4 + after_z, crossed, yhi * 4 + far_z]
    arrived += [(1 - yhi) * 4 + zi for zi in (before_z, after_z, far_z)]
    for one, d in zip(to_core, arrived):
        one.wait_recv()
        keep(d, 1 - core)
    for cb in range(4):
        s = 1 if cb % 2 == 0 else -1
        far[cb].wait_recv()
        mid = step_of(z, s)
        partial[cb, mid] = (
            partial[cb, mid].astype(jnp.float32) + partial_in[cb, 0].astype(jnp.float32)
        ).astype(jnp.bfloat16)
        last[cb] = send(partial.at[cb, mid], partial_in.at[cb, 2], z_at(s))
    load_resid.wait()
    squares = jnp.zeros((64, 1), jnp.float32)
    for cb in range(4):
        columns = pl.ds(cb * 1024, 1024)
        near[cb].wait_recv()
        last[cb].wait_recv()
        h = partial[cb, z].astype(jnp.float32) + resid[:, columns].astype(jnp.float32)
        h = h + partial_in[cb, 1].astype(jnp.float32) + partial_in[cb, 2].astype(jnp.float32)
        hidden_ref[:, columns] = h.astype(jnp.bfloat16)
        squares += jnp.sum(h * h, axis=-1, keepdims=True)
        gained = (h * gain_ref[:, columns]).astype(jnp.bfloat16)
        for n in range(2):
            some = pl.ds(n * 512, 512)
            term = jnp.dot(
                gained,
                win[2 * cb : 2 * cb + 2, :, :, some].reshape(1024, 512),
                preferred_element_type=jnp.float32,
            )
            entered[:, some] = term if cb == 0 else entered[:, some] + term
    rscale = lax.rsqrt(squares / D + eps)
    units_ref[...] = (entered[...] * rscale).astype(jnp.bfloat16)
    for one in stores:
        one.wait()
    for one in sends:
        one.wait_send()


def front(block_of, q, k, v, resid, gain, w_in, w_out, embed, codes):
    bf16, f32 = jnp.bfloat16, jnp.float32
    shapes = (
        ((64, 1024), bf16),
        ((512, 1024), bf16),
        ((64, D), bf16),
        ((8, 2, 256, 1024), bf16),
        ((2, 256, D), bf16),
    )
    vmem = pl.BlockSpec(memory_space=pltpu.VMEM)
    anywhere = pl.BlockSpec(memory_space=pl.ANY)
    return pl.pallas_call(
        front_kernel,
        out_shape=tuple(jax.ShapeDtypeStruct(*one) for one in shapes),
        in_specs=[pl.BlockSpec(memory_space=pltpu.SMEM)]
        + [anywhere] * 4
        + [vmem]
        + [anywhere] * 3
        + [vmem],
        out_specs=(vmem, vmem, vmem, anywhere, anywhere),
        scratch_shapes=[
            pltpu.VMEM((2, 4, 2, 1024, HS), bf16),
            pltpu.VMEM((2, 512, HS), bf16),
            pltpu.VMEM((1024, HS), bf16),
            pltpu.VMEM((1024, HS), f32),
            pltpu.VMEM((1024, HS), f32),
            pltpu.VMEM((1024, HS), f32),
            pltpu.VMEM((2, 2, 256, HS), bf16),
            pltpu.VMEM((2, 2, 256, HS), bf16),
            pltpu.VMEM((8, 2, 256, 1024), bf16),
            pltpu.VMEM((2, 256, D), bf16),
            pltpu.VMEM((2048, 1024), bf16),
            pltpu.VMEM((64, D), bf16),
            pltpu.VMEM((4, 4, 64, 1024), bf16),
            pltpu.VMEM((4, 3, 64, 1024), bf16),
            pltpu.VMEM((64, 1024), f32),
            pltpu.VMEM((512, 1), jnp.int32),
            pltpu.SemaphoreType.DMA((32,)),
            pltpu.SemaphoreType.DMA((56,)),
            pltpu.SemaphoreType.DMA((56,)),
        ],
        compiler_params=pltpu.CompilerParams(
            collective_id=2, has_side_effects=True, vmem_limit_bytes=60 * 1024 * 1024
        ),
        cost_estimate=pl.CostEstimate(
            flops=9_000_000_000, bytes_accessed=40_000_000, transcendentals=8_000_000
        ),
    )(block_of, q, k, v, resid, gain, w_in, w_out, embed, codes)


CB = 768
STEPS = 8
GROUP = 128


def lower_lanes():
    return lax.broadcasted_iota(jnp.int32, (1, 128), 1) < DHS


def split_heads(value, low):
    zero = jnp.zeros_like(value)
    return jnp.concatenate([jnp.where(low, value, zero), jnp.where(low, zero, value)], axis=0)


def join_heads(value, low):
    return jnp.where(low, value[:GROUP], value[GROUP:])


def head_sums(value, axis):
    halves = jnp.split(value, 2, axis=axis)
    return jnp.concatenate(
        [jnp.broadcast_to(jnp.sum(h, axis=axis, keepdims=True), h.shape) for h in halves], axis=axis
    )


def product(a, b):
    return jnp.dot(a, b, preferred_element_type=jnp.float32)


def back_kernel(
    units_ref,
    earlier_ref,
    codes_ref,
    gain,
    hidden_in,
    wqkv_in,
    wo_in,
    whead_in,
    win_in,
    wout_in,
    d_attn_ref,
    d_wqkv_ref,
    wqkv,
    wo,
    whead,
    win,
    wide,
    ynorm,
    ynorm_t,
    stream,
    packed,
    weights,
    mixed,
    after,
    ynorm2,
    grown,
    d_units,
    d_normed,
    d_other,
    turned_other,
    packed_other,
    core_sum,
    first_in,
    first_out,
    second_in,
    third_out,
    third_in,
    sums,
    code_at,
    load_sem,
    send_sem,
    recv_sem,
):
    x, y, core, z = place()
    other_core = device_at(x, y, 1 - core, z)

    def x_at(by):
        return device_at(step_of(x, by), y, core, z)

    def y_at(by):
        return device_at(x, step_of(y, by), core, z)

    def z_at(by):
        return device_at(x, y, core, step_of(z, by))

    loads = []

    def load(source, target):
        copy = pltpu.make_async_copy(source, target, load_sem.at[len(loads)])
        copy.start()
        loads.append(copy)
        return copy

    sends = []

    def send(source, target, device):
        i = len(sends)
        copy = pltpu.make_async_remote_copy(
            src_ref=source,
            dst_ref=target,
            send_sem=send_sem.at[i],
            recv_sem=recv_sem.at[i],
            device_id=device,
            device_id_type=MESH,
        )
        copy.start()
        sends.append(copy)
        return copy

    load_hidden = load(hidden_in, wide.at[z])
    load_wqkv = [
        load(
            wqkv_in.at[pl.ds(n * 256, 256), pl.ds(part * 1024, 1024)],
            wqkv.at[pl.ds(n * 256, 256), pl.ds(part * 1024, 1024)],
        )
        for part in range(3)
        for n in range(4)
    ]

    frame_of = lax.broadcasted_iota(jnp.int32, (GROUP, 16), 0) // STEPS
    spread = (frame_of == lax.broadcasted_iota(jnp.int32, (GROUP, 16), 1)).astype(jnp.bfloat16)

    def enter(n, carry):
        rows = pl.ds(pl.multiple_of(n * GROUP, GROUP), GROUP)
        s = product(spread, units_ref[pl.ds(pl.multiple_of(n * 16, 16), 16), :])
        s = s + earlier_ref[rows, :].astype(jnp.float32)
        r = lax.rsqrt(jnp.mean(s * s, axis=-1, keepdims=True) + eps)
        stream[rows, :] = s
        ynorm[rows, :] = (s * r).astype(jnp.bfloat16)
        return carry

    lax.fori_loop(0, 4, enter, 0)
    greet([other_core] + [at(by) for at in (x_at, y_at, z_at) for by in (1, 2, 3)])
    load_hidden.wait()
    wide_right = send(wide.at[z], wide.at[z], z_at(1))
    wide_left = send(wide.at[z], wide.at[z], z_at(-1))
    code_at[...] = code_column(codes_ref, 0)
    for n in range(4):
        turned = ynorm[:, n * 256 : (n + 1) * 256].T
        for ylo in range(2):
            for c in range(2):
                at = ylo * 128 + c * 64
                ynorm_t[c, n * 2 + ylo] = turned[at : at + 64]
    swap_turned = send(ynorm_t.at[1 - core], turned_other, other_core)
    load_wo = load(wo_in, wo)
    load_whead = load(whead_in, whead)
    for n in range(3):
        columns = pl.ds(n * 1024, 1024)
        for one in load_wqkv[n * 4 : n * 4 + 4]:
            one.wait()
        packed[:, columns] = product(ynorm[...], wqkv[:, columns]).astype(jnp.bfloat16)
    load_win = load(win_in, win)

    low = lower_lanes()
    scale = 1.0 / math.sqrt(DHS)

    def seen(shape, queries):
        at_query = lax.broadcasted_iota(jnp.int32, shape, queries) % GROUP
        at_key = lax.broadcasted_iota(jnp.int32, shape, 1 - queries) % GROUP
        return jnp.logical_and(at_query // STEPS == at_key // STEPS, at_key <= at_query)

    def lanes_of(pair, which=0):
        return pl.ds(pl.multiple_of(which * 1024 + pair * 128, 128), 128)

    def parts_of(rows, pair):
        q, k, v = (packed[rows, lanes_of(pair, which)] for which in range(3))
        return q, split_heads(k, low), split_heads(v, low)

    def mix(n, carry):
        rows = pl.ds(pl.multiple_of((n // 2) * GROUP, GROUP), GROUP)
        allowed = seen((GROUP, 2 * GROUP), 0)
        pairs = [(n % 2) * 4 + i for i in range(4)]
        held = [parts_of(rows, pair) for pair in pairs]
        scores = [rows_dot(q, k) for q, k, v in held]
        scores = [jnp.exp(jnp.where(allowed, s * scale, -1e30)) for s in scores]
        scores = [(s / head_sums(s, 1)).astype(jnp.bfloat16) for s in scores]
        outs = [product(a, v) for a, (q, k, v) in zip(scores, held)]
        for pair, a, out in zip(pairs, scores, outs):
            weights[pair, rows, :] = a
            mixed[rows, lanes_of(pair)] = out.astype(jnp.bfloat16)
        return carry

    lax.fori_loop(0, 8, mix, 0)
    load_wo.wait()

    def add_mixed(n, carry):
        columns = pl.ds(pl.multiple_of(n * 512, 512), 512)
        after[:, columns] = stream[:, columns] + product(mixed[...], wo[:, columns])
        return carry

    lax.fori_loop(0, 2, add_mixed, 0)

    def norm2(n, carry):
        rows = pl.ds(pl.multiple_of(n * 64, 64), 64)
        s = after[rows, :]
        r = lax.rsqrt(jnp.mean(s * s, axis=-1, keepdims=True) + eps)
        ynorm2[rows, :] = (s * r).astype(jnp.bfloat16)
        return carry

    lax.fori_loop(0, 8, norm2, 0)
    load_whead.wait()

    def grow(n, carry):
        columns = pl.ds(pl.multiple_of(n * 512, 512), 512)
        e = jnp.exp(product(ynorm2[...], whead[:, columns]))
        grown[:, columns] = e.astype(jnp.bfloat16)
        sums[...] += e[:, :128] + e[:, 128:256] + e[:, 256:384] + e[:, 384:]
        return carry

    sums[...] = jnp.zeros_like(sums)
    lax.fori_loop(0, 4, grow, 0)

    def from_loss(n, carry):
        rows = pl.ds(pl.multiple_of(n * 64, 64), 64)
        inverse = 1.0 / jnp.sum(sums[rows, :], axis=-1, keepdims=True)
        code = code_at[rows, :]
        for part in range(4):
            columns = pl.ds(part * 512, 512)
            entry = lax.broadcasted_iota(jnp.int32, (64, 512), 1) + part * 512
            scaled = grown[rows, columns].astype(jnp.float32) * inverse
            grown[rows, columns] = jnp.where(entry == code, scaled - 1.0, scaled).astype(
                jnp.bfloat16
            )
        return carry

    lax.fori_loop(0, 8, from_loss, 0)
    wide_right.wait_recv()
    before, beyond = step_of(z, -1), step_of(z, 1)
    top_rows, end_rows = pl.ds(0, 32), pl.ds(32, 32)
    wide_on_right = send(wide.at[before, top_rows], wide.at[before, top_rows], z_at(1))
    wide_left.wait_recv()
    wide_on_left = send(wide.at[beyond, end_rows], wide.at[beyond, end_rows], z_at(-1))

    def to_ynorm2(n, carry):
        columns = pl.ds(pl.multiple_of(n * 512, 512), 512)
        ynorm2[:, columns] = rows_dot(grown[...], whead[columns, :]).astype(jnp.bfloat16)
        return carry

    lax.fori_loop(0, 2, to_ynorm2, 0)
    load_wout = [
        load(
            wout_in.at[up, :, pl.ds(part * 2048, 2048)],
            whead.at[pl.ds((up * 2 + part) * 256, 256)],
        )
        for up in range(2)
        for part in range(2)
    ]

    def to_after(n, carry):
        rows = pl.ds(pl.multiple_of(n * 64, 64), 64)
        s = after[rows, :]
        d = ynorm2[rows, :].astype(jnp.float32)
        r = lax.rsqrt(jnp.mean(s * s, axis=-1, keepdims=True) + eps)
        dot = jnp.sum(d * s, axis=-1, keepdims=True)
        da = r * d - s * (r * r * r * dot / 1024)
        after[rows, :] = da
        ynorm2[rows, :] = da.astype(jnp.bfloat16)
        return carry

    lax.fori_loop(0, 8, to_after, 0)

    def to_mixed(n, carry):
        columns = pl.ds(pl.multiple_of(n * 512, 512), 512)
        mixed[:, columns] = rows_dot(ynorm2[...], wo[columns, :]).astype(jnp.bfloat16)
        return carry

    lax.fori_loop(0, 2, to_mixed, 0)

    def unmix(cb, n, carry):
        rows = pl.ds(pl.multiple_of(n * GROUP, GROUP), GROUP)
        allowed = seen((2 * GROUP, GROUP), 1)
        pairs = (2 * cb, 2 * cb + 1)
        held = [parts_of(rows, pair) for pair in pairs]
        outs = [mixed[rows, lanes_of(pair)] for pair in pairs]
        kept = [weights[pair, rows, :].astype(jnp.float32) for pair in pairs]
        turned = [rows_dot(k, q) for q, k, v in held]
        d_kept = [rows_dot(d, v) for d, (q, k, v) in zip(outs, held)]
        d_turned = [rows_dot(v, d) for d, (q, k, v) in zip(outs, held)]
        turned = [jnp.exp(jnp.where(allowed, s * scale, -1e30)) for s in turned]
        turned = [s / head_sums(s, 0) for s in turned]
        d_kept = [a * d for a, d in zip(kept, d_kept)]
        d_kept = [
            ((d - a * head_sums(d, 1)) * scale).astype(jnp.bfloat16)
            for a, d in zip(kept, d_kept)
        ]
        d_turned = [a * d for a, d in zip(turned, d_turned)]
        d_turned = [
            ((d - a * head_sums(d, 0)) * scale).astype(jnp.bfloat16)
            for a, d in zip(turned, d_turned)
        ]
        d_q = [product(d, k) for d, (q, k, v) in zip(d_kept, held)]
        d_k = [product(d, q) for d, (q, k, v) in zip(d_turned, held)]
        d_v = [product(a.astype(jnp.bfloat16), d) for a, d in zip(turned, outs)]
        for pair, dq, dk, dv in zip(pairs, d_q, d_k, d_v):
            packed[rows, lanes_of(pair)] = dq.astype(jnp.bfloat16)
            packed[rows, lanes_of(pair, 1)] = join_heads(dk, low).astype(jnp.bfloat16)
            packed[rows, lanes_of(pair, 2)] = join_heads(dv, low).astype(jnp.bfloat16)
        return carry

    swap_packed = {}

    def columns_of(cb):
        return [pl.ds(which * 1024 + cb * 256, 256) for which in range(3)]

    def unmix_block(cb):
        lax.fori_loop(0, 4, functools.partial(unmix, cb), 0)
        swap_packed[cb] = [
            send(packed.at[:, columns], packed_other.at[:, columns], other_core)
            for columns in columns_of(cb)
        ]

    far = {}
    near = {}

    def axis_of(cb):
        return (x, x_at) if cb < 2 else (y, y_at)

    def sign_of(cb):
        return 1 if cb % 2 == 0 else -1

    def chunk(cb, q):
        return core_sum.at[cb, q] if cb < 2 else core_sum.at[cb, :, q]

    def first_phase(cb):
        p, at = axis_of(cb)
        s = sign_of(cb)
        far[cb] = send(chunk(cb, step_of(p, 2)), first_in.at[cb, 0], at(s))
        near[cb] = send(chunk(cb, step_of(p, -s)), first_in.at[cb, 1], at(-s))

    def multiply(cb):
        for one in swap_packed[cb]:
            one.wait_recv()
        for side in range(2):
            own = ynorm_t[core, side * 4 : side * 4 + 4].reshape(256, 512)
            term = product(own, jnp.concatenate([packed[:, c] for c in columns_of(cb)], axis=1))
            term += product(
                turned_other[side * 4 : side * 4 + 4].reshape(256, 512),
                jnp.concatenate([packed_other[:, c] for c in columns_of(cb)], axis=1),
            )
            term = term.astype(jnp.bfloat16)
            for xi in range(2):
                for ylo in range(2):
                    for yhi in range(2):
                        at = xi * 128 + ylo * 64 + yhi * 32
                        core_sum[cb, side * 2 + xi, yhi * 2 + ylo] = term[at : at + 32]
        first_phase(cb)

    second = {}
    last = {}

    def second_phase(cb):
        p, at = axis_of(cb)
        s = sign_of(cb)
        far[cb].wait_recv()
        mid = chunk(cb, step_of(p, s))
        mid[...] = (mid[...].astype(jnp.float32) + first_in[cb, 0].astype(jnp.float32)).astype(
            jnp.bfloat16
        )
        last[cb] = send(mid, first_in.at[cb, 2], at(s))

    def other_axis(cb):
        p, at = axis_of(cb)
        near[cb].wait_recv()
        last[cb].wait_recv()
        first_out[cb] = (
            chunk(cb, p)[...].astype(jnp.float32)
            + first_in[cb, 1].astype(jnp.float32)
            + first_in[cb, 2].astype(jnp.float32)
        ).astype(jnp.bfloat16)
        q, at = (y, y_at) if cb < 2 else (x, x_at)
        second[cb] = [
            send(first_out.at[cb, step_of(q, by)], second_in.at[cb, by - 1], at(by))
            for by in (1, 2, 3)
        ]

    unmix_block(0)
    unmix_block(2)
    swap_turned.wait_recv()
    multiply(0)
    unmix_block(1)
    multiply(2)
    unmix_block(3)
    multiply(1)
    mixed[:, :512] = rows_dot(packed[...], wqkv[:512, :]).astype(jnp.bfloat16)
    multiply(3)
    mixed[:, 512:] = rows_dot(packed[...], wqkv[512:, :]).astype(jnp.bfloat16)
    second_phase(0)
    second_phase(2)

    def units_block(n, carry):
        rows = pl.ds(pl.multiple_of(n * 128, 128), 128)
        s = stream[rows, :]
        d = mixed[rows, :].astype(jnp.float32)
        r = lax.rsqrt(jnp.mean(s * s, axis=-1, keepdims=True) + eps)
        dot = jnp.sum(d * s, axis=-1, keepdims=True)
        ds = after[rows, :] + r * d - s * (r * r * r * dot / 1024)
        d_units[z, pl.ds(pl.multiple_of(n * 16, 16), 16), :] = jnp.sum(
            ds.reshape(16, 8, 1024), axis=1
        ).astype(jnp.bfloat16)
        return carry

    lax.fori_loop(0, 4, units_block, 0)
    units_right = send(d_units.at[z], d_units.at[z], z_at(1))
    units_left = send(d_units.at[z], d_units.at[z], z_at(-1))
    units_right.wait_recv()
    units_on_right = send(d_units.at[before, top_rows], d_units.at[before, top_rows], z_at(1))
    units_left.wait_recv()
    units_on_left = send(d_units.at[beyond, end_rows], d_units.at[beyond, end_rows], z_at(-1))
    second_phase(1)
    second_phase(3)
    units_on_right.wait_recv()
    units_on_left.wait_recv()
    load_win.wait()
    every = d_units[...].reshape(256, 1024)

    def normed_block(n, carry):
        columns = pl.ds(pl.multiple_of(n * 512, 512), 512)
        d_normed[:, columns] = rows_dot(every, win[columns, :]).astype(jnp.bfloat16)
        return carry

    lax.fori_loop(0, 4, normed_block, 0)
    for cb in (0, 2, 1, 3):
        other_axis(cb)
    lax.fori_loop(4, 8, normed_block, 0)

    wide_on_right.wait_recv()
    wide_on_left.wait_recv()
    wide_sends = (wide_right, wide_left, wide_on_right, wide_on_left)
    for copy in wide_sends:
        copy.wait_send()

    def hidden_block(n, carry):
        rows = pl.ds(pl.multiple_of((n % 2) * 32, 32), 32)
        h = wide[n // 2, rows, :].astype(jnp.float32)
        rscale = lax.rsqrt(jnp.mean(h * h, axis=-1, keepdims=True) + eps)
        grad_gain = (
            d_normed[pl.ds(pl.multiple_of(n * 32, 32), 32), :].astype(jnp.float32) * gain[...]
        )
        dot_rows = jnp.sum(grad_gain * h, axis=-1, keepdims=True)
        wide[n // 2, rows, :] = (
            rscale * grad_gain - h * (rscale * rscale * rscale * dot_rows / D)
        ).astype(jnp.bfloat16)
        return carry

    lax.fori_loop(0, 8, hidden_block, 0)
    for pair in range(2):
        totals = []
        for cb in (2 * pair, 2 * pair + 1):
            q = y if cb < 2 else x
            total = first_out[cb, q].astype(jnp.float32)
            for by in (1, 2, 3):
                second[cb][by - 1].wait_recv()
                total += second_in[cb, by - 1].astype(jnp.float32)
            totals.append(total)
        for zq in range(4):
            third_out[zq, pair] = jnp.concatenate(
                [one[zq * 8 : zq * 8 + 8] for one in totals], axis=0
            ).astype(jnp.bfloat16)
    third = [
        send(third_out.at[step_of(z, by)], third_in.at[by - 1], z_at(by)) for by in (1, 2, 3)
    ]
    for one in load_wout:
        one.wait()
    yhi = y // 2

    def attn_of(up):
        total = jnp.zeros((256, 256), jnp.float32)
        for part in range(2):
            rows = pl.ds(pl.multiple_of((up * 2 + part) * 256, 256), 256)
            total += rows_dot(
                wide[:, :, part * 2048 : (part + 1) * 2048].reshape(256, 2048), whead[rows, :]
            )
        return total.astype(jnp.bfloat16)

    d_other[0] = attn_of(1 - yhi)
    to_other = send(d_other.at[0], d_other.at[1], y_at(2))
    d_attn_ref[pl.ds(pl.multiple_of(yhi * 256, 256), 256), :] = attn_of(yhi)

    to_other.wait_recv()
    d_attn_ref[pl.ds(pl.multiple_of((1 - yhi) * 256, 256), 256), :] = d_other[1]
    for one in third:
        one.wait_recv()
    for pair in range(2):
        total = third_out[z, pair].astype(jnp.float32)
        for by in (1, 2, 3):
            total += third_in[by - 1, pair].astype(jnp.float32)
        for i in range(2):
            for which in range(3):
                at = which * 1024 + (pair * 2 + i) * 256
                d_wqkv_ref[:, at : at + 256] = total[
                    i * 8 : i * 8 + 8, which * 256 : which * 256 + 256
                ]

    for copy in sends:
        if not any(copy is one for one in wide_sends):
            copy.wait_send()


def back(units, earlier, codes, gain, hidden, w_qkv, w_o, w_head, w_in, w_out):
    bf16, f32 = jnp.bfloat16, jnp.float32
    vmem = pl.BlockSpec(memory_space=pltpu.VMEM)
    anywhere = pl.BlockSpec(memory_space=pl.ANY)
    return pl.pallas_call(
        back_kernel,
        out_shape=(
            jax.ShapeDtypeStruct((512, 256), bf16),
            jax.ShapeDtypeStruct((8, 3072), f32),
        ),
        in_specs=[vmem] * 4 + [anywhere] * 6,
        out_specs=(vmem,) * 2,
        scratch_shapes=[
            pltpu.VMEM((1024, 3072), bf16),
            pltpu.VMEM((1024, 1024), bf16),
            pltpu.VMEM((1024, 2048), bf16),
            pltpu.VMEM((D, 1024), bf16),
            pltpu.VMEM((4, 64, D), bf16),
            pltpu.VMEM((512, 1024), bf16),
            pltpu.VMEM((2, 8, 64, 512), bf16),
            pltpu.VMEM((512, 1024), f32),
            pltpu.VMEM((512, 3072), bf16),
            pltpu.VMEM((8, 512, 256), bf16),
            pltpu.VMEM((512, 1024), bf16),
            pltpu.VMEM((512, 1024), f32),
            pltpu.VMEM((512, 1024), bf16),
            pltpu.VMEM((512, 2048), bf16),
            pltpu.VMEM((4, 64, 1024), bf16),
            pltpu.VMEM((256, D), bf16),
            pltpu.VMEM((2, 256, 256), bf16),
            pltpu.VMEM((8, 64, 512), bf16),
            pltpu.VMEM((512, 3072), bf16),
            pltpu.VMEM((4, 4, 4, 32, CB), bf16),
            pltpu.VMEM((4, 3, 4, 32, CB), bf16),
            pltpu.VMEM((4, 4, 32, CB), bf16),
            pltpu.VMEM((4, 3, 32, CB), bf16),
            pltpu.VMEM((4, 2, 16, CB), bf16),
            pltpu.VMEM((3, 2, 16, CB), bf16),
            pltpu.VMEM((512, 128), f32),
            pltpu.VMEM((512, 1), jnp.int32),
            pltpu.SemaphoreType.DMA((24,)),
            pltpu.SemaphoreType.DMA((64,)),
            pltpu.SemaphoreType.DMA((64,)),
        ],
        compiler_params=pltpu.CompilerParams(
            collective_id=1, has_side_effects=True, vmem_limit_bytes=62 * 1024 * 1024
        ),
        cost_estimate=pl.CostEstimate(
            flops=22_000_000_000, bytes_accessed=40_000_000, transcendentals=2_000_000
        ),
    )(units, earlier, codes, gain, hidden, w_qkv, w_o, w_head, w_in, w_out)


def finish_kernel(attn_in, wqkv_in, attn_out, wqkv_out):
    attn_out[...] = attn_in[...]
    wqkv_out[...] = wqkv_in[...]


def finish(d_attn, d_wqkv):
    return pl.pallas_call(
        finish_kernel,
        out_shape=tuple(jax.ShapeDtypeStruct(one.shape, one.dtype) for one in (d_attn, d_wqkv)),
        in_specs=[pl.BlockSpec(memory_space=pltpu.VMEM)] * 2,
        out_specs=(pl.BlockSpec(memory_space=pltpu.VMEM),) * 2,
    )(d_attn, d_wqkv)


def body(
    q_heads,
    k_heads,
    v_heads,
    block_of,
    resid,
    w_out_t,
    norm_gain,
    w_in,
    embed,
    w_qkv,
    w_o,
    w_head,
    codes,
):
    gain = norm_gain.reshape(1, D)
    codes = codes.T
    units, earlier, hidden, win, wout = front(
        block_of, q_heads, k_heads, v_heads, resid, gain, w_in, w_out_t, embed, codes
    )
    return finish(*back(
        units,
        earlier,
        codes,
        gain,
        hidden,
        w_qkv,
        w_o,
        w_head,
        win.reshape(D, -1),
        wout,
    ))


def solution(mesh):
    in_specs = (
        P("ctx", "depth"),
        P("ctx", "depth"),
        P("ctx", "depth"),
        P(),
        P(("ctx", "depth"), None),
        P("depth", None),
        P(),
        P("depth", None),
        P(),
        P(),
        P(),
        P(),
        P(("ctx", "depth"), None),
    )
    out_specs = (P("ctx", "depth"), P(("ctx", "depth"), None))
    return jax.shard_map(body, mesh=mesh, in_specs=in_specs, out_specs=out_specs, check_vma=False)
```

```python
import math

import jax
import jax.numpy as jnp
from jax import lax
from jax.experimental import pallas as pl
from jax.experimental.pallas import tpu as pltpu
from jax.sharding import PartitionSpec as P

D = 4096
HS = 128
DHS = 64


eps = 1e-05
MESH = pl.DeviceIdType.MESH


def place():
    ctx = lax.axis_index("ctx")
    depth = lax.axis_index("depth")
    x = ctx // 4
    y = (depth // 4) * 2 + (ctx // 2) % 2
    return x, y, ctx % 2, depth % 4


def device_at(x, y, core, z):
    return (x * 4 + (y % 2) * 2 + core, (y // 2) * 4 + z)


def step_of(p, by):
    return (p + by + 4) % 4


def greet(devices):
    barrier = pltpu.get_barrier_semaphore()
    for device in devices:
        pl.semaphore_signal(barrier, inc=1, device_id=device, device_id_type=MESH)
    pl.semaphore_wait(barrier, len(devices))


def rows_dot(a, b):
    return lax.dot_general(a, b, (((1,), (1,)), ((), ())), preferred_element_type=jnp.float32)


def code_column(codes_ref, back_by):
    frame = lax.broadcasted_iota(jnp.int32, (512, 64), 0) // 8
    spread = (frame == lax.broadcasted_iota(jnp.int32, (512, 64), 1)).astype(jnp.bfloat16)
    codes = codes_ref[...]
    high = rows_dot(spread, (codes // 128).astype(jnp.float32).astype(jnp.bfloat16))
    low = rows_dot(spread, (codes % 128).astype(jnp.float32).astype(jnp.bfloat16))
    step = lax.broadcasted_iota(jnp.int32, (512, 8), 0) % 8 - back_by
    chosen = step == lax.broadcasted_iota(jnp.int32, (512, 8), 1)
    column = jnp.sum(jnp.where(chosen, high * 128 + low, 0.0), axis=1, keepdims=True)
    return jnp.where(step[:, :1] < 0, -1, column.astype(jnp.int32))


def front_kernel(
    block_of,
    q_in,
    k_in,
    v_in,
    resid_in,
    gain_ref,
    win_in,
    wout_in,
    embed_in,
    codes_ref,
    units_ref,
    earlier_ref,
    hidden_ref,
    win_out,
    wout_out,
    kv,
    other_head,
    queries,
    top,
    total,
    mixed,
    attn,
    heads_in,
    win,
    wout,
    embed,
    resid,
    partial,
    partial_in,
    entered,
    earlier_code,
    load_sem,
    send_sem,
    recv_sem,
):
    x, y, core, z = place()
    yhi = y // 2
    ylo = y % 2
    side = y + 1 - 2 * ylo
    cross = 3 - y
    own = yhi * 4 + z
    crossed = (1 - yhi) * 4 + z
    other_core = device_at(x, y, 1 - core, z)

    def x_at(by):
        return device_at(step_of(x, by), y, core, z)

    def z_at(by):
        return device_at(x, y, core, step_of(z, by))

    loads = []

    def load(source, target):
        i = len(loads)
        copy = pltpu.make_async_copy(source, target, load_sem.at[i])
        copy.start()
        loads.append(copy)
        return copy

    sends = []

    def send(source, target, device):
        i = len(sends)
        copy = pltpu.make_async_remote_copy(
            src_ref=source,
            dst_ref=target,
            send_sem=send_sem.at[i],
            recv_sem=recv_sem.at[i],
            device_id=device,
            device_id_type=MESH,
        )
        copy.start()
        sends.append(copy)
        return copy

    def half(which):
        return pl.ds(pl.multiple_of(which * 512, 512), 512)

    def lanes(which):
        return pl.ds(pl.multiple_of(which * 128, 128), 128)

    load_k = load(k_in.at[:, lanes(core)], kv.at[0, x, ylo, half(core)])
    load_v = load(v_in.at[:, lanes(core)], kv.at[1, x, ylo, half(core)])
    load_q = load(q_in.at[:, lanes(core)], queries.at[half(core)])
    load_other = [
        load(one.at[:, lanes(1 - core)], other_head.at[i]) for i, one in enumerate((k_in, v_in))
    ]
    greet(
        [
            other_core,
            x_at(1),
            x_at(-1),
            device_at(step_of(x, 1), y, 1 - core, z),
            device_at(step_of(x, -1), y, 1 - core, z),
            device_at(x, side, 1 - core, z),
            z_at(1),
            z_at(-1),
            device_at(x, side, core, z),
            device_at(x, cross, core, z),
            device_at(x, step_of(y, 2), core, z),
            device_at(x, step_of(y, 2), 1 - core, z),
        ]
    )
    for one in [load_k, load_v] + load_other:
        one.wait()
    here = kv.at[:, x, ylo, half(core)]
    swap_kv = send(other_head, here, other_core)

    def spread(xi, yi):
        return [
            send(here, here, device_at(xi, yi, core, z)),
            send(other_head, here, device_at(xi, yi, 1 - core, z)),
        ]

    kv_right = spread(step_of(x, 1), y)
    kv_left = spread(step_of(x, -1), y)
    kv_side = spread(x, side)
    swap_q = send(q_in.at[:, lanes(1 - core)], queries.at[half(core)], other_core)

    shard = win_in.at[pl.ds(pl.multiple_of(core * 256, 256), 256)]
    win_cross = send(shard, win.at[own, core], device_at(x, cross, core, z))
    win_right = send(shard, win.at[own, core], z_at(1))
    win_left = send(shard, win.at[own, core], z_at(-1))
    load_win = [
        load(win_in.at[pl.ds(i * 256, 256)], win.at[own, i]) for i in range(2)
    ]
    load_embed = load(embed_in, embed)
    load_wout = load(wout_in, wout.at[yhi])
    load_resid = load(resid_in, resid)

    top[...] = jnp.full_like(top, -1e29)
    total[...] = jnp.zeros_like(total)
    mixed[...] = jnp.zeros_like(mixed)
    factor = math.log2(math.e) / math.sqrt(HS)

    def attend(xi, yi):
        base = xi * 8 + yi * 4
        lane = lax.broadcasted_iota(jnp.int32, (1, 1024), 1)
        block = jnp.where(
            lane < 512,
            jnp.where(lane < 256, block_of[base], block_of[base + 1]),
            jnp.where(lane < 768, block_of[base + 2], block_of[base + 3]),
        )
        key_pos = lane % 256 + block * 256

        values = jnp.concatenate([kv[1, xi, yi], jnp.ones((1024, HS), jnp.bfloat16)], axis=1)

        def rows_of(n, carry):
            parts = [pl.ds(pl.multiple_of(n * 512 + i * 256, 256), 256) for i in range(2)]
            start = lax.broadcasted_iota(jnp.int32, (256, 1), 0)
            pos = [start + block_of[x * 8 + ylo * 4 + 2 * n + i] * 256 for i in range(2)]
            scores = [rows_dot(queries[rows, :], kv[0, xi, yi]) for rows in parts]
            scores = [jnp.where(p >= key_pos, s, -1e30) for p, s in zip(pos, scores)]
            before = [top[rows, :] for rows in parts]
            now = [
                jnp.maximum(b, jnp.max(s, axis=-1, keepdims=True)) for b, s in zip(before, scores)
            ]
            weights = [
                jnp.exp2((s - m[:, :1]) * factor).astype(jnp.bfloat16) for s, m in zip(scores, now)
            ]
            sums = [
                jnp.dot(w, values, preferred_element_type=jnp.float32) for w in weights
            ]
            for rows, b, m, s in zip(parts, before, now, sums):
                fade = jnp.exp2((b - m) * factor)
                top[rows, :] = m
                total[rows, :] = total[rows, :] * fade + s[:, HS:]
                mixed[rows, :] = mixed[rows, :] * fade + s[:, :HS]
            return carry

        lax.fori_loop(0, 2, rows_of, 0)

    load_q.wait()
    swap_q.wait_recv()
    swap_kv.wait_recv()
    attend(x, ylo)

    load_embed.wait()
    earlier_code[...] = code_column(codes_ref, 1)

    def look_up(n, carry):
        rows = pl.ds(pl.multiple_of(n * 128, 128), 128)
        entry = lax.broadcasted_iota(jnp.int32, (128, 2048), 1)
        hot = (entry == earlier_code[rows, :]).astype(jnp.bfloat16)
        earlier_ref[rows, :] = jnp.dot(
            hot, embed[...], preferred_element_type=jnp.float32
        ).astype(jnp.bfloat16)
        return carry

    lax.fori_loop(0, 4, look_up, 0)
    stores = []

    def pass_on(ref, left_arrived, right_arrived, at, before, after, first, second):
        for one in left_arrived:
            one.wait_recv()
        on_right = send(ref(before, first), ref(before, first), at(1))
        for one in right_arrived:
            one.wait_recv()
        on_left = send(ref(after, second), ref(after, second), at(-1))
        return on_right, on_left

    def keep(d, c):
        stores.append(load(win.at[d, c], win_out.at[d, c]))

    def kv_of(yi):
        return lambda xi, part: kv.at[:, xi, yi, part]

    def win_of(up):
        return lambda zi, part: win.at[up * 4 + zi, core, part]

    for one in load_win:
        one.wait()
    keep(own, 0)
    keep(own, 1)
    load_wout.wait()
    stores.append(load(wout.at[yhi], wout_out.at[yhi]))
    wout_half = pl.ds(pl.multiple_of(core * 128, 128), 128)
    wout_cross = send(
        wout_in.at[wout_half], wout.at[yhi, wout_half], device_at(x, cross, core, z)
    )
    before_x, after_x, far_x = step_of(x, -1), step_of(x, 1), step_of(x, 2)
    before_z, after_z, far_z = step_of(z, -1), step_of(z, 1), step_of(z, 2)
    first_half, second_half = pl.ds(0, 512), pl.ds(512, 512)
    win_first, win_second = pl.ds(0, 128), pl.ds(128, 128)
    side_lo = 1 - ylo
    to_core = []

    def share(d):
        to_core.append(send(win.at[d, core], win.at[d, core], other_core))
        keep(d, core)

    for one in kv_side:
        one.wait_recv()
    side_right = send(kv.at[:, x, side_lo, first_half], kv.at[:, x, side_lo, first_half], x_at(1))
    side_left = send(kv.at[:, x, side_lo, second_half], kv.at[:, x, side_lo, second_half], x_at(-1))
    for one in kv_right + kv_left:
        one.wait_recv()
    beside = device_at(x, side, core, z)
    kv_across = [
        send(kv.at[:, xi, ylo, part], kv.at[:, xi, ylo, part], beside)
        for xi, part in ((before_x, second_half), (after_x, first_half))
    ]
    win_on = pass_on(
        win_of(yhi), [win_right], [win_left], z_at, before_z, after_z, win_first, win_second
    )
    attend(x, side_lo)
    kv_on = pass_on(kv_of(ylo), [], [], x_at, before_x, after_x, first_half, second_half)
    share(yhi * 4 + before_z)
    share(yhi * 4 + after_z)
    attend(before_x, ylo)
    win_cross.wait_recv()
    cross_right = send(win.at[crossed, core], win.at[crossed, core], z_at(1))
    cross_left = send(win.at[crossed, core], win.at[crossed, core], z_at(-1))
    share(crossed)
    attend(after_x, ylo)
    side_on = pass_on(
        kv_of(side_lo), [side_right], [side_left], x_at, before_x, after_x, first_half, second_half
    )
    for one in kv_on:
        one.wait_recv()
    attend(far_x, ylo)
    for one in win_on:
        one.wait_recv()
    share(yhi * 4 + far_z)
    for one in kv_across:
        one.wait_recv()
    attend(before_x, side_lo)
    attend(after_x, side_lo)
    cross_on = pass_on(
        win_of(1 - yhi), [cross_right], [cross_left], z_at, before_z, after_z, win_first, win_second
    )
    share((1 - yhi) * 4 + before_z)
    share((1 - yhi) * 4 + after_z)
    for one in side_on:
        one.wait_recv()
    attend(far_x, side_lo)

    for n in range(4):
        rows = pl.ds(n * 256, 256)
        attn[n // 2, n % 2] = (mixed[rows, :] / total[rows, :]).astype(jnp.bfloat16)
    swaps = [
        send(attn.at[1 - core, yhi], heads_in.at[yhi, core], other_core),
        send(
            attn.at[core, 1 - yhi],
            heads_in.at[yhi, core],
            device_at(x, step_of(y, 2), core, z),
        ),
        send(
            attn.at[1 - core, 1 - yhi],
            heads_in.at[yhi, core],
            device_at(x, step_of(y, 2), 1 - core, z),
        ),
    ]
    heads_in[yhi, core] = attn[core, yhi]
    wout_cross.wait_recv()
    wout_core = send(wout.at[1 - yhi, wout_half], wout.at[1 - yhi, wout_half], other_core)
    stores.append(load(wout.at[1 - yhi, wout_half], wout_out.at[1 - yhi, wout_half]))
    wout_core.wait_recv()
    rest = pl.ds(pl.multiple_of((1 - core) * 128, 128), 128)
    stores.append(load(wout.at[1 - yhi, rest], wout_out.at[1 - yhi, rest]))
    for one in swaps:
        one.wait_recv()

    far = {}
    near = {}
    last = {}
    for cb in range(4):
        s = 1 if cb % 2 == 0 else -1
        columns = pl.ds(cb * 1024, 1024)
        sums = jnp.zeros((256, 1024), jnp.float32)
        for up in range(2):
            left = jnp.concatenate([heads_in[up, 0], heads_in[up, 1]], axis=1)
            sums += jnp.dot(left, wout[up, :, columns], preferred_element_type=jnp.float32)
        partial[cb] = sums.astype(jnp.bfloat16).reshape(4, 64, 1024)
        far[cb] = send(partial.at[cb, step_of(z, 2)], partial_in.at[cb, 0], z_at(s))
        near[cb] = send(partial.at[cb, step_of(z, -s)], partial_in.at[cb, 1], z_at(-s))
    for one in cross_on:
        one.wait_recv()
    share((1 - yhi) * 4 + far_z)
    arrived = [yhi * 4 + before_z, yhi * 4 + after_z, crossed, yhi * 4 + far_z]
    arrived += [(1 - yhi) * 4 + zi for zi in (before_z, after_z, far_z)]
    for one, d in zip(to_core, arrived):
        one.wait_recv()
        keep(d, 1 - core)
    for cb in range(4):
        s = 1 if cb % 2 == 0 else -1
        far[cb].wait_recv()
        mid = step_of(z, s)
        partial[cb, mid] = (
            partial[cb, mid].astype(jnp.float32) + partial_in[cb, 0].astype(jnp.float32)
        ).astype(jnp.bfloat16)
        last[cb] = send(partial.at[cb, mid], partial_in.at[cb, 2], z_at(s))
    load_resid.wait()
    squares = jnp.zeros((64, 1), jnp.float32)
    for cb in range(4):
        columns = pl.ds(cb * 1024, 1024)
        near[cb].wait_recv()
        last[cb].wait_recv()
        h = partial[cb, z].astype(jnp.float32) + resid[:, columns].astype(jnp.float32)
        h = h + partial_in[cb, 1].astype(jnp.float32) + partial_in[cb, 2].astype(jnp.float32)
        hidden_ref[:, columns] = h.astype(jnp.bfloat16)
        squares += jnp.sum(h * h, axis=-1, keepdims=True)
        gained = (h * gain_ref[:, columns]).astype(jnp.bfloat16)
        for n in range(2):
            some = pl.ds(n * 512, 512)
            term = jnp.dot(
                gained,
                win[2 * cb : 2 * cb + 2, :, :, some].reshape(1024, 512),
                preferred_element_type=jnp.float32,
            )
            entered[:, some] = term if cb == 0 else entered[:, some] + term
    rscale = lax.rsqrt(squares / D + eps)
    units_ref[...] = (entered[...] * rscale).astype(jnp.bfloat16)
    for one in stores:
        one.wait()
    for one in sends:
        one.wait_send()


def front(block_of, q, k, v, resid, gain, w_in, w_out, embed, codes):
    bf16, f32 = jnp.bfloat16, jnp.float32
    shapes = (
        ((64, 1024), bf16),
        ((512, 1024), bf16),
        ((64, D), bf16),
        ((8, 2, 256, 1024), bf16),
        ((2, 256, D), bf16),
    )
    vmem = pl.BlockSpec(memory_space=pltpu.VMEM)
    anywhere = pl.BlockSpec(memory_space=pl.ANY)
    return pl.pallas_call(
        front_kernel,
        out_shape=tuple(jax.ShapeDtypeStruct(*one) for one in shapes),
        in_specs=[pl.BlockSpec(memory_space=pltpu.SMEM)]
        + [anywhere] * 4
        + [vmem]
        + [anywhere] * 3
        + [vmem],
        out_specs=(vmem, vmem, vmem, anywhere, anywhere),
        scratch_shapes=[
            pltpu.VMEM((2, 4, 2, 1024, HS), bf16),
            pltpu.VMEM((2, 512, HS), bf16),
            pltpu.VMEM((1024, HS), bf16),
            pltpu.VMEM((1024, HS), f32),
            pltpu.VMEM((1024, HS), f32),
            pltpu.VMEM((1024, HS), f32),
            pltpu.VMEM((2, 2, 256, HS), bf16),
            pltpu.VMEM((2, 2, 256, HS), bf16),
            pltpu.VMEM((8, 2, 256, 1024), bf16),
            pltpu.VMEM((2, 256, D), bf16),
            pltpu.VMEM((2048, 1024), bf16),
            pltpu.VMEM((64, D), bf16),
            pltpu.VMEM((4, 4, 64, 1024), bf16),
            pltpu.VMEM((4, 3, 64, 1024), bf16),
            pltpu.VMEM((64, 1024), f32),
            pltpu.VMEM((512, 1), jnp.int32),
            pltpu.SemaphoreType.DMA((32,)),
            pltpu.SemaphoreType.DMA((56,)),
            pltpu.SemaphoreType.DMA((56,)),
        ],
        compiler_params=pltpu.CompilerParams(
            collective_id=2, has_side_effects=True, vmem_limit_bytes=60 * 1024 * 1024
        ),
        cost_estimate=pl.CostEstimate(
            flops=9_000_000_000, bytes_accessed=40_000_000, transcendentals=8_000_000
        ),
    )(block_of, q, k, v, resid, gain, w_in, w_out, embed, codes)


CB = 768
STEPS = 8
GROUP = 128


def lower_lanes():
    return lax.broadcasted_iota(jnp.int32, (1, 128), 1) < DHS


def split_heads(value, low):
    zero = jnp.zeros_like(value)
    return jnp.concatenate([jnp.where(low, value, zero), jnp.where(low, zero, value)], axis=0)


def join_heads(value, low):
    return jnp.where(low, value[:GROUP], value[GROUP:])


def head_sums(value, axis):
    halves = jnp.split(value, 2, axis=axis)
    return jnp.concatenate(
        [jnp.broadcast_to(jnp.sum(h, axis=axis, keepdims=True), h.shape) for h in halves], axis=axis
    )


def product(a, b):
    return jnp.dot(a, b, preferred_element_type=jnp.float32)


def back_kernel(
    units_ref,
    earlier_ref,
    codes_ref,
    gain,
    hidden_in,
    wqkv_in,
    wo_in,
    whead_in,
    win_in,
    wout_in,
    d_attn_ref,
    d_wqkv_ref,
    wqkv,
    wo,
    whead,
    win,
    wide,
    ynorm,
    ynorm_t,
    stream,
    packed,
    weights,
    mixed,
    after,
    ynorm2,
    grown,
    d_units,
    d_normed,
    d_other,
    g_parts,
    core_sum,
    first_in,
    first_out,
    second_in,
    third_out,
    third_in,
    sums,
    code_at,
    load_sem,
    send_sem,
    recv_sem,
):
    x, y, core, z = place()
    other_core = device_at(x, y, 1 - core, z)

    def x_at(by):
        return device_at(step_of(x, by), y, core, z)

    def y_at(by):
        return device_at(x, step_of(y, by), core, z)

    def z_at(by):
        return device_at(x, y, core, step_of(z, by))

    loads = []

    def load(source, target):
        copy = pltpu.make_async_copy(source, target, load_sem.at[len(loads)])
        copy.start()
        loads.append(copy)
        return copy

    sends = []

    def send(source, target, device):
        i = len(sends)
        copy = pltpu.make_async_remote_copy(
            src_ref=source,
            dst_ref=target,
            send_sem=send_sem.at[i],
            recv_sem=recv_sem.at[i],
            device_id=device,
            device_id_type=MESH,
        )
        copy.start()
        sends.append(copy)
        return copy

    load_hidden = load(hidden_in, wide.at[z])
    load_wqkv = [
        load(
            wqkv_in.at[pl.ds(n * 256, 256), pl.ds(part * 1024, 1024)],
            wqkv.at[pl.ds(n * 256, 256), pl.ds(part * 1024, 1024)],
        )
        for part in range(3)
        for n in range(4)
    ]

    frame_of = lax.broadcasted_iota(jnp.int32, (GROUP, 16), 0) // STEPS
    spread = (frame_of == lax.broadcasted_iota(jnp.int32, (GROUP, 16), 1)).astype(jnp.bfloat16)

    def enter(n, carry):
        rows = pl.ds(pl.multiple_of(n * GROUP, GROUP), GROUP)
        s = product(spread, units_ref[pl.ds(pl.multiple_of(n * 16, 16), 16), :])
        s = s + earlier_ref[rows, :].astype(jnp.float32)
        r = lax.rsqrt(jnp.mean(s * s, axis=-1, keepdims=True) + eps)
        stream[rows, :] = s
        ynorm[rows, :] = (s * r).astype(jnp.bfloat16)
        return carry

    lax.fori_loop(0, 4, enter, 0)
    greet([other_core] + [at(by) for at in (x_at, y_at, z_at) for by in (1, 2, 3)])
    load_hidden.wait()
    wide_right = send(wide.at[z], wide.at[z], z_at(1))
    wide_left = send(wide.at[z], wide.at[z], z_at(-1))
    code_at[...] = code_column(codes_ref, 0)
    for n in range(4):
        ynorm_t[n * 256 : (n + 1) * 256, :] = ynorm[:, n * 256 : (n + 1) * 256].T
    load_wo = load(wo_in, wo)
    load_whead = load(whead_in, whead)
    for n in range(3):
        columns = pl.ds(n * 1024, 1024)
        for one in load_wqkv[n * 4 : n * 4 + 4]:
            one.wait()
        packed[:, columns] = product(ynorm[...], wqkv[:, columns]).astype(jnp.bfloat16)
    load_win = load(win_in, win)

    low = lower_lanes()
    scale = 1.0 / math.sqrt(DHS)

    def seen(shape, queries):
        at_query = lax.broadcasted_iota(jnp.int32, shape, queries) % GROUP
        at_key = lax.broadcasted_iota(jnp.int32, shape, 1 - queries) % GROUP
        return jnp.logical_and(at_query // STEPS == at_key // STEPS, at_key <= at_query)

    def parts_of(rows, pair):
        at = pair * 128
        q = packed[rows, at : at + 128]
        k = split_heads(packed[rows, 1024 + at : 1024 + at + 128], low)
        v = split_heads(packed[rows, 2048 + at : 2048 + at + 128], low)
        return q, k, v

    def mix(n, carry):
        rows = pl.ds(pl.multiple_of(n * GROUP, GROUP), GROUP)
        allowed = seen((GROUP, 2 * GROUP), 0)
        for first in (0, 4):
            pairs = range(first, first + 4)
            held = [parts_of(rows, pair) for pair in pairs]
            scores = [rows_dot(q, k) for q, k, v in held]
            scores = [jnp.exp(jnp.where(allowed, s * scale, -1e30)) for s in scores]
            scores = [(s / head_sums(s, 1)).astype(jnp.bfloat16) for s in scores]
            outs = [product(a, v) for a, (q, k, v) in zip(scores, held)]
            for pair, a, out in zip(pairs, scores, outs):
                weights[pair, rows, :] = a
                mixed[rows, pair * 128 : pair * 128 + 128] = out.astype(jnp.bfloat16)
        return carry

    lax.fori_loop(0, 4, mix, 0)
    load_wo.wait()

    def add_mixed(n, carry):
        columns = pl.ds(pl.multiple_of(n * 512, 512), 512)
        after[:, columns] = stream[:, columns] + product(mixed[...], wo[:, columns])
        return carry

    lax.fori_loop(0, 2, add_mixed, 0)

    def norm2(n, carry):
        rows = pl.ds(pl.multiple_of(n * 64, 64), 64)
        s = after[rows, :]
        r = lax.rsqrt(jnp.mean(s * s, axis=-1, keepdims=True) + eps)
        ynorm2[rows, :] = (s * r).astype(jnp.bfloat16)
        return carry

    lax.fori_loop(0, 8, norm2, 0)
    load_whead.wait()

    def grow(n, carry):
        columns = pl.ds(pl.multiple_of(n * 512, 512), 512)
        e = jnp.exp(product(ynorm2[...], whead[:, columns]))
        grown[:, columns] = e.astype(jnp.bfloat16)
        sums[...] += e[:, :128] + e[:, 128:256] + e[:, 256:384] + e[:, 384:]
        return carry

    sums[...] = jnp.zeros_like(sums)
    lax.fori_loop(0, 4, grow, 0)

    def from_loss(n, carry):
        rows = pl.ds(pl.multiple_of(n * 64, 64), 64)
        inverse = 1.0 / jnp.sum(sums[rows, :], axis=-1, keepdims=True)
        code = code_at[rows, :]
        for part in range(4):
            columns = pl.ds(part * 512, 512)
            entry = lax.broadcasted_iota(jnp.int32, (64, 512), 1) + part * 512
            scaled = grown[rows, columns].astype(jnp.float32) * inverse
            grown[rows, columns] = jnp.where(entry == code, scaled - 1.0, scaled).astype(
                jnp.bfloat16
            )
        return carry

    lax.fori_loop(0, 8, from_loss, 0)
    wide_right.wait_recv()
    before, beyond = step_of(z, -1), step_of(z, 1)
    top_rows, end_rows = pl.ds(0, 32), pl.ds(32, 32)
    wide_on_right = send(wide.at[before, top_rows], wide.at[before, top_rows], z_at(1))
    wide_left.wait_recv()
    wide_on_left = send(wide.at[beyond, end_rows], wide.at[beyond, end_rows], z_at(-1))

    def to_ynorm2(n, carry):
        columns = pl.ds(pl.multiple_of(n * 512, 512), 512)
        ynorm2[:, columns] = rows_dot(grown[...], whead[columns, :]).astype(jnp.bfloat16)
        return carry

    lax.fori_loop(0, 2, to_ynorm2, 0)
    load_wout = [
        load(
            wout_in.at[up, :, pl.ds(part * 2048, 2048)],
            whead.at[pl.ds((up * 2 + part) * 256, 256)],
        )
        for up in range(2)
        for part in range(2)
    ]

    def to_after(n, carry):
        rows = pl.ds(pl.multiple_of(n * 64, 64), 64)
        s = after[rows, :]
        d = ynorm2[rows, :].astype(jnp.float32)
        r = lax.rsqrt(jnp.mean(s * s, axis=-1, keepdims=True) + eps)
        dot = jnp.sum(d * s, axis=-1, keepdims=True)
        da = r * d - s * (r * r * r * dot / 1024)
        after[rows, :] = da
        ynorm2[rows, :] = da.astype(jnp.bfloat16)
        return carry

    lax.fori_loop(0, 8, to_after, 0)

    def to_mixed(n, carry):
        columns = pl.ds(pl.multiple_of(n * 512, 512), 512)
        mixed[:, columns] = rows_dot(ynorm2[...], wo[columns, :]).astype(jnp.bfloat16)
        return carry

    lax.fori_loop(0, 2, to_mixed, 0)

    def unmix(n, carry):
        rows = pl.ds(pl.multiple_of(n * GROUP, GROUP), GROUP)
        allowed = seen((2 * GROUP, GROUP), 1)
        for first in (0, 4):
            pairs = range(first, first + 4)
            held = [parts_of(rows, pair) for pair in pairs]
            outs = [mixed[rows, pair * 128 : pair * 128 + 128] for pair in pairs]
            kept = [weights[pair, rows, :].astype(jnp.float32) for pair in pairs]
            turned = [rows_dot(k, q) for q, k, v in held]
            d_kept = [rows_dot(d, v) for d, (q, k, v) in zip(outs, held)]
            d_turned = [rows_dot(v, d) for d, (q, k, v) in zip(outs, held)]
            turned = [jnp.exp(jnp.where(allowed, s * scale, -1e30)) for s in turned]
            turned = [s / head_sums(s, 0) for s in turned]
            d_kept = [a * d for a, d in zip(kept, d_kept)]
            d_kept = [
                ((d - a * head_sums(d, 1)) * scale).astype(jnp.bfloat16)
                for a, d in zip(kept, d_kept)
            ]
            d_turned = [a * d for a, d in zip(turned, d_turned)]
            d_turned = [
                ((d - a * head_sums(d, 0)) * scale).astype(jnp.bfloat16)
                for a, d in zip(turned, d_turned)
            ]
            d_q = [product(d, k) for d, (q, k, v) in zip(d_kept, held)]
            d_k = [product(d, q) for d, (q, k, v) in zip(d_turned, held)]
            d_v = [product(a.astype(jnp.bfloat16), d) for a, d in zip(turned, outs)]
            for pair, dq, dk, dv in zip(pairs, d_q, d_k, d_v):
                at = pair * 128
                packed[rows, at : at + 128] = dq.astype(jnp.bfloat16)
                packed[rows, 1024 + at : 1024 + at + 128] = join_heads(dk, low).astype(jnp.bfloat16)
                packed[rows, 2048 + at : 2048 + at + 128] = join_heads(dv, low).astype(jnp.bfloat16)
        return carry

    lax.fori_loop(0, 4, unmix, 0)

    core_sends = {}
    far = {}
    near = {}

    def axis_of(cb):
        return (x, x_at) if cb < 2 else (y, y_at)

    def sign_of(cb):
        return 1 if cb % 2 == 0 else -1

    def chunk(cb, q):
        return core_sum.at[cb, q] if cb < 2 else core_sum.at[cb, :, q]

    def first_phase(cb):
        core_sends[cb].wait_recv()
        core_sum[cb] = (
            core_sum[cb].astype(jnp.float32) + g_parts[core, cb].astype(jnp.float32)
        ).astype(jnp.bfloat16)
        p, at = axis_of(cb)
        s = sign_of(cb)
        far[cb] = send(chunk(cb, step_of(p, 2)), first_in.at[cb, 0], at(s))
        near[cb] = send(chunk(cb, step_of(p, -s)), first_in.at[cb, 1], at(-s))

    def multiply(cb):
        def block(xi, carry):
            rows = pl.ds(pl.multiple_of(xi * 256, 256), 256)
            term = product(ynorm_t[rows, :], packed[:, cb * CB : (cb + 1) * CB])
            term = term.astype(jnp.bfloat16)
            for ylo in range(2):
                for c in range(2):
                    for yhi in range(2):
                        at = ylo * 128 + c * 64 + yhi * 32
                        g_parts[c, cb, xi, yhi * 2 + ylo] = term[at : at + 32]
            return carry

        lax.fori_loop(0, 4, block, 0)
        core_sends[cb] = send(g_parts.at[1 - core, cb], core_sum.at[cb], other_core)

    second = {}
    last = {}

    def second_phase(cb):
        p, at = axis_of(cb)
        s = sign_of(cb)
        far[cb].wait_recv()
        mid = chunk(cb, step_of(p, s))
        mid[...] = (mid[...].astype(jnp.float32) + first_in[cb, 0].astype(jnp.float32)).astype(
            jnp.bfloat16
        )
        last[cb] = send(mid, first_in.at[cb, 2], at(s))

    def other_axis(cb):
        p, at = axis_of(cb)
        near[cb].wait_recv()
        last[cb].wait_recv()
        first_out[cb] = (
            chunk(cb, p)[...].astype(jnp.float32)
            + first_in[cb, 1].astype(jnp.float32)
            + first_in[cb, 2].astype(jnp.float32)
        ).astype(jnp.bfloat16)
        q, at = (y, y_at) if cb < 2 else (x, x_at)
        second[cb] = [
            send(first_out.at[cb, step_of(q, by)], second_in.at[cb, by - 1], at(by))
            for by in (1, 2, 3)
        ]

    multiply(0)
    multiply(2)
    first_phase(0)
    multiply(1)
    first_phase(2)
    multiply(3)
    first_phase(1)
    mixed[:, :512] = rows_dot(packed[...], wqkv[:512, :]).astype(jnp.bfloat16)
    first_phase(3)
    mixed[:, 512:] = rows_dot(packed[...], wqkv[512:, :]).astype(jnp.bfloat16)
    second_phase(0)
    second_phase(2)

    def units_block(n, carry):
        rows = pl.ds(pl.multiple_of(n * 128, 128), 128)
        s = stream[rows, :]
        d = mixed[rows, :].astype(jnp.float32)
        r = lax.rsqrt(jnp.mean(s * s, axis=-1, keepdims=True) + eps)
        dot = jnp.sum(d * s, axis=-1, keepdims=True)
        ds = after[rows, :] + r * d - s * (r * r * r * dot / 1024)
        d_units[z, pl.ds(pl.multiple_of(n * 16, 16), 16), :] = jnp.sum(
            ds.reshape(16, 8, 1024), axis=1
        ).astype(jnp.bfloat16)
        return carry

    lax.fori_loop(0, 4, units_block, 0)
    units_right = send(d_units.at[z], d_units.at[z], z_at(1))
    units_left = send(d_units.at[z], d_units.at[z], z_at(-1))
    second_phase(1)
    second_phase(3)
    units_right.wait_recv()
    units_on_right = send(d_units.at[before, top_rows], d_units.at[before, top_rows], z_at(1))
    units_left.wait_recv()
    units_on_left = send(d_units.at[beyond, end_rows], d_units.at[beyond, end_rows], z_at(-1))
    other_axis(0)
    other_axis(2)
    other_axis(1)
    units_on_right.wait_recv()
    units_on_left.wait_recv()
    load_win.wait()
    every = d_units[...].reshape(256, 1024)

    def normed_block(n, carry):
        columns = pl.ds(pl.multiple_of(n * 512, 512), 512)
        d_normed[:, columns] = rows_dot(every, win[columns, :]).astype(jnp.bfloat16)
        return carry

    lax.fori_loop(0, 4, normed_block, 0)
    other_axis(3)
    lax.fori_loop(4, 8, normed_block, 0)

    wide_on_right.wait_recv()
    wide_on_left.wait_recv()
    wide_sends = (wide_right, wide_left, wide_on_right, wide_on_left)
    for copy in wide_sends:
        copy.wait_send()

    def hidden_block(n, carry):
        rows = pl.ds(pl.multiple_of((n % 2) * 32, 32), 32)
        h = wide[n // 2, rows, :].astype(jnp.float32)
        rscale = lax.rsqrt(jnp.mean(h * h, axis=-1, keepdims=True) + eps)
        grad_gain = (
            d_normed[pl.ds(pl.multiple_of(n * 32, 32), 32), :].astype(jnp.float32) * gain[...]
        )
        dot_rows = jnp.sum(grad_gain * h, axis=-1, keepdims=True)
        wide[n // 2, rows, :] = (
            rscale * grad_gain - h * (rscale * rscale * rscale * dot_rows / D)
        ).astype(jnp.bfloat16)
        return carry

    lax.fori_loop(0, 8, hidden_block, 0)
    for pair in range(2):
        totals = []
        for cb in (2 * pair, 2 * pair + 1):
            q = y if cb < 2 else x
            total = first_out[cb, q].astype(jnp.float32)
            for by in (1, 2, 3):
                second[cb][by - 1].wait_recv()
                total += second_in[cb, by - 1].astype(jnp.float32)
            totals.append(total)
        for zq in range(4):
            third_out[zq, pair] = jnp.concatenate(
                [one[zq * 8 : zq * 8 + 8] for one in totals], axis=0
            ).astype(jnp.bfloat16)
    third = [
        send(third_out.at[step_of(z, by)], third_in.at[by - 1], z_at(by)) for by in (1, 2, 3)
    ]
    for one in load_wout:
        one.wait()
    yhi = y // 2

    def attn_of(up):
        total = jnp.zeros((256, 256), jnp.float32)
        for part in range(2):
            rows = pl.ds(pl.multiple_of((up * 2 + part) * 256, 256), 256)
            total += rows_dot(
                wide[:, :, part * 2048 : (part + 1) * 2048].reshape(256, 2048), whead[rows, :]
            )
        return total.astype(jnp.bfloat16)

    d_other[0] = attn_of(1 - yhi)
    to_other = send(d_other.at[0], d_other.at[1], y_at(2))
    d_attn_ref[pl.ds(pl.multiple_of(yhi * 256, 256), 256), :] = attn_of(yhi)

    to_other.wait_recv()
    d_attn_ref[pl.ds(pl.multiple_of((1 - yhi) * 256, 256), 256), :] = d_other[1]
    for one in third:
        one.wait_recv()
    for pair in range(2):
        total = third_out[z, pair].astype(jnp.float32)
        for by in (1, 2, 3):
            total += third_in[by - 1, pair].astype(jnp.float32)
        d_wqkv_ref[:, pair * 2 * CB : (pair * 2 + 1) * CB] = total[:8]
        d_wqkv_ref[:, (pair * 2 + 1) * CB : (pair * 2 + 2) * CB] = total[8:]

    for copy in sends:
        if not any(copy is one for one in wide_sends):
            copy.wait_send()


def back(units, earlier, codes, gain, hidden, w_qkv, w_o, w_head, w_in, w_out):
    bf16, f32 = jnp.bfloat16, jnp.float32
    vmem = pl.BlockSpec(memory_space=pltpu.VMEM)
    anywhere = pl.BlockSpec(memory_space=pl.ANY)
    return pl.pallas_call(
        back_kernel,
        out_shape=(
            jax.ShapeDtypeStruct((512, 256), bf16),
            jax.ShapeDtypeStruct((8, 3072), f32),
        ),
        in_specs=[vmem] * 4 + [anywhere] * 6,
        out_specs=(vmem,) * 2,
        scratch_shapes=[
            pltpu.VMEM((1024, 3072), bf16),
            pltpu.VMEM((1024, 1024), bf16),
            pltpu.VMEM((1024, 2048), bf16),
            pltpu.VMEM((D, 1024), bf16),
            pltpu.VMEM((4, 64, D), bf16),
            pltpu.VMEM((512, 1024), bf16),
            pltpu.VMEM((1024, 512), bf16),
            pltpu.VMEM((512, 1024), f32),
            pltpu.VMEM((512, 3072), bf16),
            pltpu.VMEM((8, 512, 256), bf16),
            pltpu.VMEM((512, 1024), bf16),
            pltpu.VMEM((512, 1024), f32),
            pltpu.VMEM((512, 1024), bf16),
            pltpu.VMEM((512, 2048), bf16),
            pltpu.VMEM((4, 64, 1024), bf16),
            pltpu.VMEM((256, D), bf16),
            pltpu.VMEM((2, 256, 256), bf16),
            pltpu.VMEM((2, 4, 4, 4, 32, CB), bf16),
            pltpu.VMEM((4, 4, 4, 32, CB), bf16),
            pltpu.VMEM((4, 3, 4, 32, CB), bf16),
            pltpu.VMEM((4, 4, 32, CB), bf16),
            pltpu.VMEM((4, 3, 32, CB), bf16),
            pltpu.VMEM((4, 2, 16, CB), bf16),
            pltpu.VMEM((3, 2, 16, CB), bf16),
            pltpu.VMEM((512, 128), f32),
            pltpu.VMEM((512, 1), jnp.int32),
            pltpu.SemaphoreType.DMA((24,)),
            pltpu.SemaphoreType.DMA((48,)),
            pltpu.SemaphoreType.DMA((48,)),
        ],
        compiler_params=pltpu.CompilerParams(
            collective_id=1, has_side_effects=True, vmem_limit_bytes=62 * 1024 * 1024
        ),
        cost_estimate=pl.CostEstimate(
            flops=22_000_000_000, bytes_accessed=40_000_000, transcendentals=2_000_000
        ),
    )(units, earlier, codes, gain, hidden, w_qkv, w_o, w_head, w_in, w_out)


def finish_kernel(attn_in, wqkv_in, attn_out, wqkv_out):
    attn_out[...] = attn_in[...]
    wqkv_out[...] = wqkv_in[...]


def finish(d_attn, d_wqkv):
    return pl.pallas_call(
        finish_kernel,
        out_shape=tuple(jax.ShapeDtypeStruct(one.shape, one.dtype) for one in (d_attn, d_wqkv)),
        in_specs=[pl.BlockSpec(memory_space=pltpu.VMEM)] * 2,
        out_specs=(pl.BlockSpec(memory_space=pltpu.VMEM),) * 2,
    )(d_attn, d_wqkv)


def body(
    q_heads,
    k_heads,
    v_heads,
    block_of,
    resid,
    w_out_t,
    norm_gain,
    w_in,
    embed,
    w_qkv,
    w_o,
    w_head,
    codes,
):
    gain = norm_gain.reshape(1, D)
    codes = codes.T
    units, earlier, hidden, win, wout = front(
        block_of, q_heads, k_heads, v_heads, resid, gain, w_in, w_out_t, embed, codes
    )
    return finish(*back(
        units,
        earlier,
        codes,
        gain,
        hidden,
        w_qkv,
        w_o,
        w_head,
        win.reshape(D, -1),
        wout,
    ))


def solution(mesh):
    in_specs = (
        P("ctx", "depth"),
        P("ctx", "depth"),
        P("ctx", "depth"),
        P(),
        P(("ctx", "depth"), None),
        P("depth", None),
        P(),
        P("depth", None),
        P(),
        P(),
        P(),
        P(),
        P(("ctx", "depth"), None),
    )
    out_specs = (P("ctx", "depth"), P(("ctx", "depth"), None))
    return jax.shard_map(body, mesh=mesh, in_specs=in_specs, out_specs=out_specs, check_vma=False)
```
